32 devices in a mesh: grp: 4 (over x, core), seq: 8 (over z, y).
Axes of the slice: x: 2, y: 2, z: 4, core: 2. Of those that a mesh axis runs over, the one named last changes fastest.
Arguments:
- tokens: bfloat16 [16, 4, 5120], P(None, None, ('grp', 'seq')), may hold values from -90 to 90
- lengths: int32 [16], replicated, may hold values from 1 to 8192, as said below
- group_perm: int32 [16], replicated, may hold values from 0 to 15, as said below
- page_table: int32 [16, 64], replicated, may hold values from 0 to 31, as said below
- k_pool: bfloat16 [1024, 128, 1024], P(('grp', 'seq')), may hold values from -17 to 17
- v_pool: bfloat16 [1024, 128, 1024], P(('grp', 'seq')), may hold values from -7 to 7
- gain_in: float32 [5120], P(('grp', 'seq')), may hold values from 0.25 to 1.75
- qkv_weight: bfloat16 [5120, 7168], P('grp', 'seq'), may hold values from -0.15625 to 0.15625
- qkv_bias: float32 [7168], P('seq'), may hold values from -16 to 16
- o_weight: bfloat16 [5120, 5120], P('seq', 'grp'), may hold values from -0.078125 to 0.078125
- gain_mid: float32 [5120], P(('grp', 'seq')), may hold values from 0.25 to 1.75
- gate_weight: bfloat16 [5120, 13824], P('grp', 'seq'), may hold values from -0.078125 to 0.078125
- up_weight: bfloat16 [5120, 13824], P('grp', 'seq'), may hold values from -0.078125 to 0.078125
- down_weight: bfloat16 [13824, 5120], P('seq', 'grp'), may hold values from -0.0546875 to 0.0546875
Outputs:
- mixed: bfloat16 [16, 4, 5120], P(None, None, ('grp', 'seq'))
The draws below stay inside these ranges and needn't reach their ends.
Inputs may be any that keep to these rules, and one draw needn't show every extreme that they name: `lengths`: one request holds exactly 8192 cached tokens. A permutation of the requests; request group_perm[i] belongs to group i // 4. `page_table`: page p of request r lies on the device with grp index g and seq index p // 8, where g is the group of r; the slots named for one device are all different.
All inputs are finite; a program needn't handle non-finite values.
Results may differ from the reference program's by a relative error of at most 0.015.
Values may be sent and summed in bfloat16 or wider, within the bound.
A program may use at most 128 MiB of HBM per device.

```python
import math
import jax
import jax.numpy as jnp
from jax import lax

D = 5120
HEADS = 40
KV_HEADS = 8
HEAD_DIM = 128
FF = 13824
STEPS = 4
REQ_GRP = 4
SHARD_PAGES = 8
PAGE = 128
REQUESTS = 16
QKVW = 7168
POOL = 32
SLOTS = 1024
MAXPAGES = 64
MAXLEN = 8192
N_SEQ = 8
DEVICES = 32


def permute_slots(device_key):
    return jax.random.permutation(device_key, POOL)


def layout(key):
    order = jax.random.permutation(jax.random.fold_in(key, 101), REQUESTS).astype(jnp.int32)
    where_in = jnp.argsort(order).astype(jnp.int32)
    group_of = where_in // REQ_GRP
    member = where_in % REQ_GRP
    page_ids = jnp.arange(MAXPAGES, dtype=jnp.int32)
    shard_of = page_ids // SHARD_PAGES
    inside = page_ids % SHARD_PAGES
    device_of = group_of[:, None] * N_SEQ + shard_of[None, :]
    local_of = member[:, None] * SHARD_PAGES + inside[None, :]
    device_keys = jax.random.split(jax.random.fold_in(key, 102), DEVICES)
    shuffles = jax.vmap(permute_slots)(device_keys).astype(jnp.int32)
    return (order, shuffles[device_of, local_of].astype(jnp.int32))


def draw_group_perm(key, part):
    return layout(key)[0]


def draw_page_table(key, part):
    return layout(key)[1]


def draw_lengths(key, part):
    drawn = jax.random.randint(jax.random.fold_in(key, 103), (REQUESTS,), 1, MAXLEN + 1, dtype=jnp.int32)
    chosen = jax.random.randint(jax.random.fold_in(key, 104), (), 0, REQUESTS, dtype=jnp.int32)
    return drawn.at[chosen].set(MAXLEN)


def draw_tokens(key, part):
    shape = (REQUESTS, STEPS, D)
    columns = jnp.arange(D, dtype=jnp.float32) / D - 0.5
    row_scale = jnp.exp(jax.random.uniform(jax.random.fold_in(key, 301), (REQUESTS, STEPS, 1), jnp.float32, math.log(0.4), math.log(4.0)))
    jitter = jnp.exp(jax.random.uniform(jax.random.fold_in(key, 302), (D,), jnp.float32, math.log(0.6), math.log(1.7)))
    trend = 3.0 ** columns
    noise = jnp.clip(jax.random.normal(jax.random.fold_in(key, 305), shape, jnp.float32), -4.0, 4.0)
    return (noise * row_scale * trend * jitter).astype(jnp.bfloat16)


def draw_qkv_bias(key, part):
    values = jnp.clip(jax.random.normal(jax.random.fold_in(key, 202), (QKVW,), jnp.float32), -4.0, 4.0)
    return values


def draw_k_pool(key, part):
    shape = (SLOTS, PAGE, KV_HEADS * HEAD_DIM)
    values = 1.7 * jnp.clip(jax.random.normal(jax.random.fold_in(key, 207), shape, jnp.float32), -4.0, 4.0)
    return values.astype(jnp.bfloat16)


def levels(stream_key, extent, cuts, least, largest):
    factor_of = 1.0
    for axis_at, blocks in cuts:
        heights = jax.random.uniform(jax.random.fold_in(jax.random.fold_in(stream_key, 6), axis_at), (blocks,), jnp.float32, least / len(cuts), largest / len(cuts))
        factor_of = factor_of * jnp.repeat(jnp.exp(heights), extent[axis_at] // blocks).reshape((-1,) + (1,) * (len(extent) - 1 - axis_at))
    return factor_of


def bell_draw(own_key, shape, width, reach, pieces=(), kind=jnp.bfloat16):
    entries = width * jax.random.normal(own_key, shape, jnp.float32)
    if pieces:
        entries = entries * levels(own_key, shape, pieces, -0.22, 0.18)
    return jnp.clip(entries, -reach, reach).astype(kind)


def setup_inputs(seed: int = 0) -> dict:
    arg_keys = jax.random.split(jax.random.key(seed), 15)
    return {
        "tokens": draw_tokens(jax.random.fold_in(arg_keys[14], 71), 0),
        "lengths": draw_lengths(jax.random.fold_in(arg_keys[14], 71), 0),
        "group_perm": draw_group_perm(jax.random.fold_in(arg_keys[14], 71), 0),
        "page_table": draw_page_table(jax.random.fold_in(arg_keys[14], 71), 0),
        "k_pool": draw_k_pool(jax.random.fold_in(arg_keys[14], 71), 0),
        "v_pool": bell_draw(arg_keys[5], (SLOTS, PAGE, KV_HEADS * HEAD_DIM), 1.7, 7.0, ((0, 32),)),
        "gain_in": jnp.clip(1.0 + 0.15 * jax.random.normal(arg_keys[6], (D,), jnp.float32), 0.25, 1.75),
        "qkv_weight": bell_draw(arg_keys[7], (D, QKVW), (D // 3) ** -0.5, 0.15625, ((0, 4), (1, 8))),
        "qkv_bias": draw_qkv_bias(jax.random.fold_in(arg_keys[14], 71), 0),
        "o_weight": bell_draw(arg_keys[9], (HEADS * HEAD_DIM, D), (HEADS * HEAD_DIM) ** -0.5, 0.078125, ((0, 8), (1, 4))),
        "gain_mid": jnp.clip(1.0 + 0.15 * jax.random.normal(arg_keys[10], (D,), jnp.float32), 0.25, 1.75),
        "gate_weight": bell_draw(arg_keys[11], (D, FF), D ** -0.5, 0.078125, ((0, 4), (1, 8))),
        "up_weight": bell_draw(arg_keys[12], (D, FF), D ** -0.5, 0.078125, ((0, 4), (1, 8))),
        "down_weight": bell_draw(arg_keys[13], (FF, D), FF ** -0.5, 0.0546875, ((0, 8), (1, 4))),
    }


EPSILON = 1e-06
LOW_SCORE = -1e+30
ROPE_BASE = 1000000.0

def rotary(values, position):
    half_dim = values.shape[-1] // 2
    exponent = jnp.arange(half_dim, dtype=jnp.float32) * (2.0 / values.shape[-1])
    inverse = jnp.exp(-exponent * jnp.log(jnp.float32(ROPE_BASE)))
    angle = position[..., None, None] * inverse
    cosine = jnp.cos(angle)
    sine_part = jnp.sin(angle)
    first_half = values[..., :half_dim]
    second_half = values[..., half_dim:]
    return jnp.concatenate([first_half * cosine - second_half * sine_part, second_half * cosine + first_half * sine_part], axis=-1)

def rms_norm(values, gain):
    mean_square = lax.optimization_barrier(jnp.mean(values * values, axis=-1, keepdims=True))
    return (values * lax.rsqrt(mean_square + EPSILON) * gain).astype(jnp.bfloat16)

def reference(tokens, lengths, group_perm, page_table, k_pool, v_pool, gain_in, qkv_weight, qkv_bias, o_weight, gain_mid, gate_weight, up_weight, down_weight):
    q_width = HEADS * HEAD_DIM
    kv_width = KV_HEADS * HEAD_DIM
    group_q = HEADS // KV_HEADS
    query_rows = STEPS * group_q
    score_scale = HEAD_DIM ** (-0.5)
    inputs = tokens.astype(jnp.float32)
    normed_in = rms_norm(inputs, gain_in)
    projected = jnp.dot(normed_in.reshape(REQUESTS * STEPS, D), qkv_weight, preferred_element_type=jnp.float32)
    projected = projected.reshape(REQUESTS, STEPS, QKVW) + qkv_bias
    steps_range = jnp.arange(STEPS, dtype=jnp.int32)
    position = (lengths[:, None] + steps_range[None, :]).astype(jnp.float32)
    queries = rotary(projected[..., :q_width].reshape(REQUESTS, STEPS, HEADS, HEAD_DIM), position).astype(jnp.bfloat16)
    new_keys = rotary(projected[..., q_width:q_width + kv_width].reshape(REQUESTS, STEPS, KV_HEADS, HEAD_DIM), position).astype(jnp.bfloat16)
    new_values = projected[..., q_width + kv_width:].reshape(REQUESTS, STEPS, KV_HEADS, HEAD_DIM).astype(jnp.bfloat16)
    where_in = jnp.argsort(group_perm).astype(jnp.int32)
    group_of = where_in // REQ_GRP
    page_ids = jnp.arange(MAXPAGES, dtype=jnp.int32)
    slot_rows = (group_of[:, None] * N_SEQ + page_ids[None, :] // SHARD_PAGES) * POOL + page_table
    causal = (steps_range[None, :] <= (jnp.arange(query_rows, dtype=jnp.int32) // group_q)[:, None])[None]
    cache_positions = jnp.arange(MAXLEN, dtype=jnp.int32)

    def attend_one(item):
        slot_row, query_item, key_item, value_item, length = item
        cache_keys = k_pool[slot_row].reshape(MAXLEN, KV_HEADS, HEAD_DIM).astype(jnp.float32)
        cache_values = v_pool[slot_row].reshape(MAXLEN, KV_HEADS, HEAD_DIM).astype(jnp.float32)
        query_mat = query_item.reshape(STEPS, KV_HEADS, group_q, HEAD_DIM).transpose(1, 0, 2, 3).reshape(KV_HEADS, query_rows, HEAD_DIM).astype(jnp.float32)
        live_mask = (cache_positions < length)[None, None, :]
        cache_scores = jnp.einsum('hqd,khd->hqk', query_mat, cache_keys) * score_scale
        cache_scores = jnp.where(live_mask, cache_scores, LOW_SCORE)
        own_scores = jnp.einsum('hqd,khd->hqk', query_mat, key_item.astype(jnp.float32)) * score_scale
        own_scores = jnp.where(causal, own_scores, LOW_SCORE)
        top_score = jnp.maximum(lax.optimization_barrier(jnp.max(cache_scores, axis=-1)), lax.optimization_barrier(jnp.max(own_scores, axis=-1)))
        cache_weights = jnp.where(live_mask, jnp.exp(cache_scores - top_score[..., None]), 0.0)
        own_weights = jnp.where(causal, jnp.exp(own_scores - top_score[..., None]), 0.0)
        weight_sums = lax.optimization_barrier(jnp.sum(cache_weights, axis=-1)) + lax.optimization_barrier(jnp.sum(own_weights, axis=-1))
        cache_rounded = lax.optimization_barrier(cache_weights.astype(jnp.bfloat16)).astype(jnp.float32)
        own_rounded = lax.optimization_barrier(own_weights.astype(jnp.bfloat16)).astype(jnp.float32)
        weighted = jnp.einsum('hqk,khd->hqd', cache_rounded, cache_values) + jnp.einsum('hqk,khd->hqd', own_rounded, value_item.astype(jnp.float32))
        attended = weighted / weight_sums[..., None]
        return attended.reshape(KV_HEADS, STEPS, group_q, HEAD_DIM).transpose(1, 0, 2, 3).reshape(STEPS, q_width).astype(jnp.bfloat16)
    attended = lax.map(attend_one, (slot_rows, queries, new_keys, new_values, lengths))
    out_proj = jnp.dot(attended.reshape(REQUESTS * STEPS, q_width), o_weight, preferred_element_type=jnp.float32)
    residual = inputs + out_proj.reshape(REQUESTS, STEPS, D)
    normed_mid = rms_norm(residual, gain_mid).reshape(REQUESTS * STEPS, D)
    gate_sum = jnp.dot(normed_mid, gate_weight, preferred_element_type=jnp.float32)
    up_sum = jnp.dot(normed_mid, up_weight, preferred_element_type=jnp.float32)
    hidden = (jax.nn.silu(gate_sum) * up_sum).astype(jnp.bfloat16)
    down_sum = jnp.dot(hidden, down_weight, preferred_element_type=jnp.float32).reshape(REQUESTS, STEPS, D)
    return (residual + down_sum).astype(jnp.bfloat16)
```

```python
import functools

import jax
import jax.numpy as jnp
from jax import lax
from jax.experimental import pallas as pl
from jax.experimental.pallas import tpu as pltpu
from jax.sharding import PartitionSpec as P

D = 5120
HEADS = 40
KV_HEADS = 8
HEAD_DIM = 128
STEPS = 4
REQ_GRP = 4
SHARD_PAGES = 8
PAGE = 128
BLOCK_PAGES = 4


EPSILON = 1e-06
LOW_SCORE = -1e30
ROPE_BASE = 1000000.0


def rotary(values, position):
    half_dim = values.shape[-1] // 2
    exponent = jnp.arange(half_dim, dtype=jnp.float32) * (2.0 / values.shape[-1])
    inverse = jnp.exp(-exponent * jnp.log(jnp.float32(ROPE_BASE)))
    angle = position[..., None, None] * inverse
    cosine = jnp.cos(angle)
    sine_part = jnp.sin(angle)
    first_half = values[..., :half_dim]
    second_half = values[..., half_dim:]
    return jnp.concatenate(
        [
            first_half * cosine - second_half * sine_part,
            second_half * cosine + first_half * sine_part,
        ],
        axis=-1,
    )


def absorb(carried, query_mat, key_block, value_block, live_mask, score_scale):
    best_score, weight_sums, weighted = carried
    scores = (
        jnp.einsum("hqd,khd->hqk", query_mat, key_block, preferred_element_type=jnp.float32)
        * score_scale
    )
    scores = jnp.where(live_mask, scores, LOW_SCORE)
    fresh_top = jnp.maximum(best_score, jnp.max(scores, axis=-1))
    rescale = jnp.exp(best_score - fresh_top)
    weights = jnp.where(live_mask, jnp.exp(scores - fresh_top[..., None]), 0.0)
    weight_sums = weight_sums * rescale + jnp.sum(weights, axis=-1)
    weighted = weighted * rescale[..., None] + jnp.einsum(
        "hqk,khd->hqd",
        weights.astype(jnp.bfloat16),
        value_block,
        preferred_element_type=jnp.float32,
    )
    return (fresh_top, weight_sums, weighted)


def body(
    tokens,
    lengths,
    group_perm,
    page_table,
    k_pool,
    v_pool,
    gain_in,
    qkv_weight,
    qkv_bias,
    o_weight,
    gain_mid,
    gate_weight,
    up_weight,
    down_weight,
):
    n_seq = lax.axis_size("seq")
    grp_idx = lax.axis_index("grp")
    seq_idx = lax.axis_index("seq")
    group_q = HEADS // KV_HEADS
    query_rows = STEPS * group_q
    q_width = HEADS * HEAD_DIM
    kv_width = KV_HEADS * HEAD_DIM
    score_scale = HEAD_DIM ** (-0.5)
    sorted_rows = jnp.take(tokens, group_perm, axis=0).astype(jnp.float32)
    squares_in = lax.psum(jnp.sum(sorted_rows * sorted_rows, axis=-1), ("grp", "seq"))
    normed_in = (sorted_rows * lax.rsqrt(squares_in / D + EPSILON)[..., None] * gain_in).astype(
        jnp.bfloat16
    )
    proj_part = jnp.einsum(
        "rtc,ck->rtk",
        lax.all_gather(normed_in, "seq", axis=2, tiled=True),
        qkv_weight,
        preferred_element_type=jnp.float32,
    )
    proj_share = (
        lax.psum_scatter(
            proj_part.astype(jnp.bfloat16), "grp", scatter_dimension=0, tiled=True
        ).astype(jnp.float32)
        + qkv_bias
    )
    proj_full = lax.all_gather(proj_share, "seq", axis=2, tiled=True)
    members = lax.dynamic_slice_in_dim(group_perm, grp_idx * REQ_GRP, REQ_GRP)
    my_lengths = jnp.take(lengths, members)
    steps_range = jnp.arange(STEPS, dtype=jnp.int32)
    position = (my_lengths[:, None] + steps_range[None, :]).astype(jnp.float32)
    queries = rotary(
        proj_full[..., :q_width].reshape(REQ_GRP, STEPS, HEADS, HEAD_DIM), position
    ).astype(jnp.bfloat16)
    new_keys = rotary(
        proj_full[..., q_width : q_width + kv_width].reshape(REQ_GRP, STEPS, KV_HEADS, HEAD_DIM),
        position,
    ).astype(jnp.bfloat16)
    new_values = (
        proj_full[..., q_width + kv_width :]
        .reshape(REQ_GRP, STEPS, KV_HEADS, HEAD_DIM)
        .astype(jnp.bfloat16)
    )
    shard_rows = SHARD_PAGES * PAGE
    block_rows = BLOCK_PAGES * PAGE
    shard_base = seq_idx * shard_rows
    slot_table = lax.dynamic_slice_in_dim(
        jnp.take(page_table, members, axis=0), seq_idx * SHARD_PAGES, SHARD_PAGES, 1
    )
    is_last = seq_idx == n_seq - 1
    causal = (
        steps_range[None, :] <= (jnp.arange(query_rows, dtype=jnp.int32) // group_q)[:, None]
    ) & is_last
    causal = causal[None]
    query_all = (
        queries.reshape(REQ_GRP, STEPS, KV_HEADS, group_q, HEAD_DIM)
        .transpose(0, 2, 1, 3, 4)
        .reshape(REQ_GRP, KV_HEADS, query_rows, HEAD_DIM)
    )
    live_all = jnp.clip(my_lengths - shard_base, 0, shard_rows)
    block_offsets = jnp.arange(block_rows, dtype=jnp.int32)
    initial = (
        jnp.full((REQ_GRP, KV_HEADS, query_rows), LOW_SCORE, jnp.float32),
        jnp.zeros((REQ_GRP, KV_HEADS, query_rows), jnp.float32),
        jnp.zeros((REQ_GRP, KV_HEADS, query_rows, HEAD_DIM), jnp.float32),
    )
    absorb_all = jax.vmap(absorb, in_axes=(0, 0, 0, 0, None, None))
    carried = absorb_all(initial, query_all, new_keys, new_values, causal, score_scale)
    absorb_masked = jax.vmap(absorb, in_axes=(0, 0, 0, 0, 0, None))
    block_count = (jnp.max(live_all) + block_rows - 1) // block_rows

    def advance_all(block_index, running):
        slot_ids = lax.dynamic_slice_in_dim(slot_table, block_index * BLOCK_PAGES, BLOCK_PAGES, 1)
        key_block = jnp.take(k_pool, slot_ids.reshape(-1), axis=0).reshape(
            REQ_GRP, block_rows, KV_HEADS, HEAD_DIM
        )
        value_block = jnp.take(v_pool, slot_ids.reshape(-1), axis=0).reshape(
            REQ_GRP, block_rows, KV_HEADS, HEAD_DIM
        )
        positions = shard_base + block_index * block_rows + block_offsets
        live_mask = (positions[None, :] < my_lengths[:, None])[:, None, None, :]
        return absorb_masked(running, query_all, key_block, value_block, live_mask, score_scale)

    best_score, weight_sums, weighted = lax.fori_loop(0, block_count, advance_all, carried)
    top_score = lax.pmax(best_score, "seq")
    factor = jnp.exp(best_score - top_score)
    weight_sums, weighted = (
        lax.psum((weight_sums * factor).astype(jnp.bfloat16), "seq").astype(jnp.float32),
        lax.psum((weighted * factor[..., None]).astype(jnp.bfloat16), "seq").astype(jnp.float32),
    )
    attended = (weighted / weight_sums[..., None]).reshape(
        REQ_GRP, KV_HEADS, STEPS, group_q, HEAD_DIM
    )
    attended = (
        attended.transpose(0, 2, 1, 3, 4).reshape(REQ_GRP, STEPS, q_width).astype(jnp.bfloat16)
    )
    out_width = o_weight.shape[0]
    attended_cols = lax.dynamic_slice_in_dim(attended, seq_idx * out_width, out_width, 2)
    out_terms = jnp.einsum(
        "rtc,cd->rtd",
        lax.all_gather(attended_cols, "grp", axis=0, tiled=True),
        o_weight,
        preferred_element_type=jnp.float32,
    )
    attn_sum = lax.psum_scatter(
        out_terms.astype(jnp.bfloat16), "seq", scatter_dimension=2, tiled=True
    ).astype(jnp.float32)
    residual = sorted_rows + attn_sum
    squares_mid = lax.psum(jnp.sum(residual * residual, axis=-1), ("grp", "seq"))
    normed_mid = (residual * lax.rsqrt(squares_mid / D + EPSILON)[..., None] * gain_mid).astype(
        jnp.bfloat16
    )
    segment = lax.all_gather(normed_mid, "seq", axis=2, tiled=True)
    gate_part = jnp.einsum("rtc,cf->rtf", segment, gate_weight, preferred_element_type=jnp.float32)
    up_part = jnp.einsum("rtc,cf->rtf", segment, up_weight, preferred_element_type=jnp.float32)
    gate_sum, up_sum = (
        lax.psum(gate_part.astype(jnp.bfloat16), "grp").astype(jnp.float32),
        lax.psum(up_part.astype(jnp.bfloat16), "grp").astype(jnp.float32),
    )
    hidden = (jax.nn.silu(gate_sum) * up_sum).astype(jnp.bfloat16)
    down_terms = jnp.einsum("rtf,fd->rtd", hidden, down_weight, preferred_element_type=jnp.float32)
    down_sum = lax.psum_scatter(
        down_terms.astype(jnp.bfloat16), "seq", scatter_dimension=2, tiled=True
    ).astype(jnp.float32)
    restore = jnp.argsort(group_perm)
    return jnp.take(residual + down_sum, restore, axis=0).astype(jnp.bfloat16)


N_GRP = 4
N_SEQ = 8
ROWS = 64
GROWS = REQ_GRP * STEPS
FEAT = D // (N_GRP * N_SEQ)
FEAT_PAD = 256
DEPTH = D // N_GRP
GROUP_Q = HEADS // KV_HEADS
QROWS = 32
SHARD_ROWS = SHARD_PAGES * PAGE
MESH = pl.DeviceIdType.MESH


def stat_lanes(pieces, rows, at=0, width=128, base=None):
    lane = lax.broadcasted_iota(jnp.int32, (rows, width), 1)
    block = jnp.zeros((rows, width), jnp.float32) if base is None else base
    for offset, piece in enumerate(pieces):
        block = jnp.where(lane == at + offset, piece, block)
    return block


def split_bf16(value, count):
    pieces = []
    for _ in range(count):
        piece = value.astype(jnp.bfloat16).astype(jnp.float32)
        pieces.append(piece)
        value = value - piece
    return pieces


def fused_kernel(
    lengths,
    group_perm,
    page_table,
    tokens,
    gain_in,
    qkv_bias,
    gain_mid,
    k_hbm,
    v_hbm,
    qkv_hbm,
    o_hbm,
    gate_hbm,
    up_hbm,
    down_hbm,
    out,
    k_pool,
    v_pool,
    w_qkv,
    w_o,
    w_gate,
    w_up,
    w_down,
    x_all,
    x_wide,
    x_bf,
    qkv_send,
    qkv_recv,
    heads_all,
    q_pairs,
    new_k,
    new_v,
    att_send,
    att_recv,
    att_all,
    wide,
    o_send,
    o_recv,
    mid_all,
    ff_send,
    ff_recv,
    hid_all,
    down_send,
    down_recv,
    load_sem,
    send_sem,
    recv_sem,
):
    g = lax.axis_index("grp")
    s = lax.axis_index("seq")
    f32, bf16 = jnp.float32, jnp.bfloat16

    loads = [
        pltpu.make_async_copy(src, dst, load_sem.at[i])
        for i, (src, dst) in enumerate(
            [
                (qkv_hbm, w_qkv),
                (k_hbm, k_pool),
                (v_hbm, v_pool),
                (o_hbm, w_o),
                (gate_hbm, w_gate),
                (up_hbm, w_up),
                (down_hbm, w_down),
            ]
        )
    ]
    for load in loads:
        load.start()
    barrier = pltpu.get_barrier_semaphore()
    for d in range(1, N_SEQ):
        pl.semaphore_signal(
            barrier, inc=1, device_id={"seq": lax.rem(s + d, N_SEQ)}, device_id_type=MESH
        )
    for d in range(1, N_GRP):
        pl.semaphore_signal(
            barrier, inc=1, device_id={"grp": lax.rem(g + d, N_GRP)}, device_id_type=MESH
        )

    def exchange(stage, axis, source, target):
        me, count = (s, N_SEQ) if axis == "seq" else (g, N_GRP)
        copies = []
        for d in range(1, count):
            peer = lax.rem(me + d, count)
            copy = pltpu.make_async_remote_copy(
                src_ref=source(peer),
                dst_ref=target,
                send_sem=send_sem.at[stage, d],
                recv_sem=recv_sem.at[stage, d],
                device_id={axis: peer},
                device_id_type=MESH,
            )
            copy.start()
            copies.append(copy)
        return copies

    def arrive(copies):
        for copy in copies:
            copy.wait_recv()

    started = []

    row_i = lax.broadcasted_iota(jnp.int32, (ROWS, ROWS), 0)
    col_i = lax.broadcasted_iota(jnp.int32, (ROWS, ROWS), 1)
    origin = jnp.zeros((ROWS, ROWS), jnp.int32)
    for i in range(ROWS // STEPS):
        origin = jnp.where(row_i // STEPS == i, group_perm[i], origin)
    order = (
        ((col_i // STEPS) == origin) & ((col_i % STEPS) == (row_i % STEPS))
    ).astype(f32).astype(bf16)
    sorted_rows = jnp.dot(order, tokens[...], preferred_element_type=f32)

    def feature_block(values, gain):
        squares = jnp.sum(values * values, axis=1, keepdims=True)
        return stat_lanes(
            split_bf16(squares, 2), ROWS, FEAT, FEAT_PAD, values * gain
        ).astype(bf16)

    x_all[s] = feature_block(sorted_rows, gain_in[...])
    pl.semaphore_wait(barrier, N_SEQ + N_GRP - 2)

    def gather_features(stage, blocks):
        copies = exchange(stage, "seq", lambda peer: blocks.at[s], blocks.at[s])
        started.extend(copies)
        arrive(copies)
        lane = lax.broadcasted_iota(jnp.int32, (ROWS, FEAT_PAD), 1)
        x_wide[...] = jnp.zeros_like(x_wide)
        squares = jnp.zeros((ROWS, 1), f32)
        for i in range(N_SEQ):
            block = blocks[i].astype(f32)
            kept = jnp.where(lane < FEAT, block, 0.0)
            squares = squares + jnp.sum(block - kept, axis=1, keepdims=True)
            first = i * FEAT // 128 * 128
            kept = jnp.concatenate([kept, jnp.zeros((ROWS, 128), f32)], axis=1)
            if i * FEAT - first:
                kept = pltpu.roll(kept, i * FEAT - first, 1)
            x_wide[:, first : first + 384] += kept
        x_bf[...] = x_wide[:, :DEPTH].astype(bf16)
        return squares

    squares_in = gather_features(0, x_all)

    loads[0].wait()
    part = jnp.dot(x_bf[...], w_qkv[...], preferred_element_type=f32).astype(bf16)
    stats = stat_lanes(split_bf16(squares_in, 2), ROWS).astype(bf16)
    for i in range(N_GRP):
        rows = slice(i * GROWS, (i + 1) * GROWS)
        qkv_send[i, :, :896] = part[rows]
        qkv_send[i, :, 896:] = stats[rows]
    copies = exchange(1, "grp", lambda peer: qkv_send.at[peer], qkv_recv.at[g])
    started.extend(copies)
    qkv_recv[g] = qkv_send[g]

    row16 = lax.broadcasted_iota(jnp.int32, (GROWS, HEAD_DIM), 0)
    lane16 = lax.broadcasted_iota(jnp.int32, (GROWS, HEAD_DIM), 1)
    position = row16 % STEPS
    for r in range(REQ_GRP):
        length = lengths[group_perm[g * REQ_GRP + r]]
        position = position + jnp.where(row16 // STEPS == r, length, 0)
    half = HEAD_DIM // 2
    exponent = (lane16 % half).astype(f32) * (2.0 / HEAD_DIM)
    angle = position.astype(f32) * jnp.exp(-exponent * jnp.log(jnp.full((), ROPE_BASE, f32)))
    cosine = jnp.cos(angle)
    sine = jnp.where(lane16 < half, -jnp.sin(angle), jnp.sin(angle))

    arrive(copies)
    summed = sum(qkv_recv[i].astype(f32) for i in range(N_GRP))
    scale = lax.rsqrt(jnp.sum(summed[:, 896:], axis=1, keepdims=True) / D + EPSILON)
    share = summed[:, :896] * scale + qkv_bias[...]
    per_dev = 896 // HEAD_DIM
    for j in range(per_dev):
        unit = share[:, j * HEAD_DIM : (j + 1) * HEAD_DIM]
        turned = unit * cosine + pltpu.roll(unit, half, 1) * sine
        unit = jnp.where(s * per_dev + j < HEADS + KV_HEADS, turned, unit)
        heads_all[s, :, j * HEAD_DIM : (j + 1) * HEAD_DIM] = unit.astype(bf16)
    copies = exchange(2, "seq", lambda peer: heads_all.at[s], heads_all.at[s])
    started.extend(copies)
    q_pairs[...] = jnp.zeros_like(q_pairs)
    arrive(copies)

    def head(h):
        lane = (h % per_dev) * HEAD_DIM
        return heads_all[h // per_dev, :, lane : lane + HEAD_DIM]

    n_q = REQ_GRP * QROWS
    spread_row = lax.broadcasted_iota(jnp.int32, (n_q, GROUP_Q * GROWS), 0)
    spread_col = lax.broadcasted_iota(jnp.int32, (n_q, GROUP_Q * GROWS), 1)
    spread = (
        (spread_row // QROWS == spread_col % GROWS // STEPS)
        & (spread_row % QROWS // STEPS == spread_col // GROWS)
        & (spread_row % STEPS == spread_col % STEPS)
    ).astype(f32).astype(bf16)
    for k in range(KV_HEADS):
        stacked = jnp.concatenate([head(k * GROUP_Q + j) for j in range(GROUP_Q)], axis=0)
        placed = jnp.dot(spread, stacked, preferred_element_type=f32).astype(bf16)
        for r in range(REQ_GRP):
            q_pairs[
                r,
                k // 2,
                (k % 2) * QROWS : (k % 2 + 1) * QROWS,
                (k % 2) * HEAD_DIM : (k % 2 + 1) * HEAD_DIM,
            ] = placed[r * QROWS : (r + 1) * QROWS]
        new_k[:, k * HEAD_DIM : (k + 1) * HEAD_DIM] = head(HEADS + k)
        new_v[:, k * HEAD_DIM : (k + 1) * HEAD_DIM] = head(HEADS + KV_HEADS + k)

    loads[1].wait()
    loads[2].wait()
    score_scale = HEAD_DIM ** (-0.5)
    new_row = lax.broadcasted_iota(jnp.int32, (2 * QROWS, GROWS), 0)
    new_col = lax.broadcasted_iota(jnp.int32, (2 * QROWS, GROWS), 1)
    causal = (new_col % STEPS <= new_row % STEPS) & (s == N_SEQ - 1)
    columns = lax.broadcasted_iota(jnp.int32, (2 * QROWS, SHARD_ROWS), 1)
    contract_last = (((1,), (1,)), ((), ()))

    def attend(r, carry):
        request = group_perm[g * REQ_GRP + r]
        live = columns < lengths[request] - s * SHARD_ROWS
        own = causal & (new_col // STEPS == r)
        slots = [page_table[request, s * SHARD_PAGES + p] for p in range(SHARD_PAGES)]
        for pair in range(KV_HEADS // 2):
            lanes = slice(pair * 256, (pair + 1) * 256)
            query = q_pairs[r, pair]
            keys = jnp.concatenate([k_pool[slot, :, lanes] for slot in slots], axis=0)
            values = jnp.concatenate([v_pool[slot, :, lanes] for slot in slots], axis=0)
            scores = (
                lax.dot_general(query, keys, contract_last, preferred_element_type=f32)
                * score_scale
            )
            scores = jnp.where(live, scores, LOW_SCORE)
            fresh = (
                lax.dot_general(query, new_k[:, lanes], contract_last, preferred_element_type=f32)
                * score_scale
            )
            fresh = jnp.where(own, fresh, LOW_SCORE)
            top = jnp.maximum(
                jnp.max(scores, axis=1, keepdims=True), jnp.max(fresh, axis=1, keepdims=True)
            )
            weights = jnp.where(live, jnp.exp(scores - top), 0.0)
            new_weights = jnp.where(own, jnp.exp(fresh - top), 0.0)
            total = jnp.sum(weights, axis=1, keepdims=True) + jnp.sum(
                new_weights, axis=1, keepdims=True
            )
            weighted = jnp.dot(weights.astype(bf16), values, preferred_element_type=f32) + jnp.dot(
                new_weights.astype(bf16), new_v[:, lanes], preferred_element_type=f32
            )
            block = stat_lanes(split_bf16(top, 3) + split_bf16(total, 2), 2 * QROWS)
            rows = pl.ds(pl.multiple_of(r * QROWS, QROWS), QROWS)
            for k in range(2):
                mine = slice(k * QROWS, (k + 1) * QROWS)
                att_send[2 * pair + k, rows, :HEAD_DIM] = weighted[
                    mine, k * HEAD_DIM : (k + 1) * HEAD_DIM
                ].astype(bf16)
                att_send[2 * pair + k, rows, HEAD_DIM:] = block[mine].astype(bf16)
        return carry

    lax.fori_loop(0, REQ_GRP, attend, 0)
    copies = exchange(3, "seq", lambda peer: att_send.at[peer], att_recv.at[s])
    started.extend(copies)
    att_recv[s] = att_send[s]
    arrive(copies)

    tops, sums = [], []
    for i in range(N_SEQ):
        block = att_recv[i, :, HEAD_DIM:].astype(f32)
        tops.append(block[:, 0:1] + block[:, 1:2] + block[:, 2:3])
        sums.append(block[:, 3:4] + block[:, 4:5])
    best = functools.reduce(jnp.maximum, tops)
    total = jnp.zeros((n_q, 1), f32)
    weighted = jnp.zeros((n_q, HEAD_DIM), f32)
    for i in range(N_SEQ):
        factor = jnp.exp(tops[i] - best)
        total = total + factor * sums[i]
        weighted = weighted + factor * att_recv[i, :, :HEAD_DIM].astype(f32)
    attended = (weighted / total).astype(bf16)
    pick_row = lax.broadcasted_iota(jnp.int32, (GROUP_Q * GROWS, n_q), 0)
    pick_col = lax.broadcasted_iota(jnp.int32, (GROUP_Q * GROWS, n_q), 1)
    pick = (
        (pick_col // QROWS == pick_row % GROWS // STEPS)
        & (pick_col % QROWS // STEPS == pick_row // GROWS)
        & (pick_col % STEPS == pick_row % STEPS)
    ).astype(f32).astype(bf16)
    picked = jnp.dot(pick, attended, preferred_element_type=f32).astype(bf16)
    for j in range(GROUP_Q):
        att_all[g, :, j * HEAD_DIM : (j + 1) * HEAD_DIM] = picked[j * GROWS : (j + 1) * GROWS]
    copies = exchange(4, "grp", lambda peer: att_all.at[g], att_all.at[g])
    started.extend(copies)
    loads[3].wait()
    arrive(copies)

    def scatter_features(stage, send, recv):
        for i in range(N_SEQ):
            first = i * FEAT // 128 * 128
            window = wide[:, first : first + 384]
            if i * FEAT - first:
                window = pltpu.roll(window, 384 - (i * FEAT - first), 1)
            send[i] = window[:, :FEAT_PAD].astype(bf16)
        copies = exchange(stage, "seq", lambda peer: send.at[peer], recv.at[s])
        started.extend(copies)
        recv[s] = send[s]
        arrive(copies)
        return sum(recv[i].astype(f32) for i in range(N_SEQ))

    columns_in = jnp.concatenate([att_all[i] for i in range(N_GRP)], axis=0)
    wide[:, DEPTH:] = jnp.zeros((ROWS, 128), f32)
    wide[:, :DEPTH] = jnp.dot(columns_in, w_o[...], preferred_element_type=f32)
    attn_sum = scatter_features(5, o_send, o_recv)
    feature = lax.broadcasted_iota(jnp.int32, (ROWS, FEAT_PAD), 1) < FEAT
    residual = jnp.where(feature, sorted_rows + attn_sum, 0.0)
    mid_all[s] = feature_block(residual, gain_mid[...])
    squares_mid = gather_features(6, mid_all)

    stats = stat_lanes(split_bf16(squares_mid, 2), ROWS).astype(bf16)
    for i in range(N_GRP):
        ff_send[i, :, 3584:] = stats[i * GROWS : (i + 1) * GROWS]

    for at, (weight, load) in enumerate([(w_gate, loads[4]), (w_up, loads[5])]):
        load.wait()

        def ff_tile(c, carry, at=at, weight=weight):
            first = pl.multiple_of(c * 256, 256)
            tile = jnp.dot(
                x_bf[...], weight[:, pl.ds(first, 256)], preferred_element_type=f32
            ).astype(bf16)
            for i in range(N_GRP):
                ff_send[i, :, pl.ds(pl.multiple_of(at * 1792 + first, 256), 256)] = tile[
                    i * GROWS : (i + 1) * GROWS
                ]
            return carry

        lax.fori_loop(0, 6, ff_tile, 0)
        tile = jnp.dot(x_bf[...], weight[:, 1536:1728], preferred_element_type=f32)
        tile = jnp.concatenate([tile, jnp.zeros((ROWS, 64), f32)], axis=1).astype(bf16)
        for i in range(N_GRP):
            ff_send[i, :, at * 1792 + 1536 : (at + 1) * 1792] = tile[i * GROWS : (i + 1) * GROWS]
    copies = exchange(7, "grp", lambda peer: ff_send.at[peer], ff_recv.at[g])
    started.extend(copies)
    ff_recv[g] = ff_send[g]
    arrive(copies)
    stat = sum(ff_recv[i, :, 3584:].astype(f32) for i in range(N_GRP))
    scale = lax.rsqrt(jnp.sum(stat, axis=1, keepdims=True) / D + EPSILON)
    gate = sum(ff_recv[i, :, :1792].astype(f32) for i in range(N_GRP)) * scale
    up = sum(ff_recv[i, :, 1792:3584].astype(f32) for i in range(N_GRP)) * scale
    hid_all[g] = (gate / (1.0 + jnp.exp(-gate)) * up).astype(bf16)
    copies = exchange(8, "grp", lambda peer: hid_all.at[g], hid_all.at[g])
    started.extend(copies)
    loads[6].wait()
    arrive(copies)

    def down_tile(c, carry):
        first = pl.multiple_of(c * 256, 256)
        hidden = jnp.concatenate([hid_all[i, :, :1728] for i in range(N_GRP)], axis=0)
        wide[:, pl.ds(first, 256)] = jnp.dot(
            hidden, w_down[:, pl.ds(first, 256)], preferred_element_type=f32
        )
        return carry

    lax.fori_loop(0, DEPTH // 256, down_tile, 0)
    down_sum = scatter_features(9, down_send, down_recv)
    final = (residual + down_sum).astype(bf16)
    origin = jnp.zeros((ROWS, ROWS), jnp.int32)
    for i in range(ROWS // STEPS):
        origin = jnp.where(col_i // STEPS == i, group_perm[i], origin)
    back = (
        ((row_i // STEPS) == origin) & ((col_i % STEPS) == (row_i % STEPS))
    ).astype(f32).astype(bf16)
    out[...] = jnp.dot(back, final, preferred_element_type=f32).astype(bf16)
    for copy in started:
        copy.wait_send()


def fused_body(
    tokens,
    lengths,
    group_perm,
    page_table,
    k_pool,
    v_pool,
    gain_in,
    qkv_weight,
    qkv_bias,
    o_weight,
    gain_mid,
    gate_weight,
    up_weight,
    down_weight,
):
    pad = FEAT_PAD - FEAT
    rows = jnp.pad(tokens.reshape(ROWS, FEAT), ((0, 0), (0, pad)))
    gains = [jnp.pad(gain.reshape(1, FEAT), ((0, 0), (0, pad))) for gain in (gain_in, gain_mid)]
    smem = pl.BlockSpec(memory_space=pltpu.SMEM)
    vmem = pl.BlockSpec(memory_space=pltpu.VMEM)
    hbm = pl.BlockSpec(memory_space=pl.ANY)
    bf16, f32 = jnp.bfloat16, jnp.float32
    out = pl.pallas_call(
        fused_kernel,
        out_shape=jax.ShapeDtypeStruct((ROWS, FEAT_PAD), bf16),
        in_specs=[smem] * 3 + [vmem] * 4 + [hbm] * 7,
        out_specs=vmem,
        scratch_shapes=[
            pltpu.VMEM(k_pool.shape, bf16),
            pltpu.VMEM(v_pool.shape, bf16),
            pltpu.VMEM(qkv_weight.shape, bf16),
            pltpu.VMEM(o_weight.shape, bf16),
            pltpu.VMEM(gate_weight.shape, bf16),
            pltpu.VMEM(up_weight.shape, bf16),
            pltpu.VMEM(down_weight.shape, bf16),
            pltpu.VMEM((N_SEQ, ROWS, FEAT_PAD), bf16),
            pltpu.VMEM((ROWS, DEPTH + 128), f32),
            pltpu.VMEM((ROWS, DEPTH), bf16),
            pltpu.VMEM((N_GRP, GROWS, 1024), bf16),
            pltpu.VMEM((N_GRP, GROWS, 1024), bf16),
            pltpu.VMEM((N_SEQ, GROWS, 896), bf16),
            pltpu.VMEM((REQ_GRP, KV_HEADS // 2, 2 * QROWS, 256), bf16),
            pltpu.VMEM((GROWS, KV_HEADS * HEAD_DIM), bf16),
            pltpu.VMEM((GROWS, KV_HEADS * HEAD_DIM), bf16),
            pltpu.VMEM((N_SEQ, REQ_GRP * QROWS, 2 * HEAD_DIM), bf16),
            pltpu.VMEM((N_SEQ, REQ_GRP * QROWS, 2 * HEAD_DIM), bf16),
            pltpu.VMEM((N_GRP, GROWS, GROUP_Q * HEAD_DIM), bf16),
            pltpu.VMEM((ROWS, DEPTH + 128), f32),
            pltpu.VMEM((N_SEQ, ROWS, FEAT_PAD), bf16),
            pltpu.VMEM((N_SEQ, ROWS, FEAT_PAD), bf16),
            pltpu.VMEM((N_SEQ, ROWS, FEAT_PAD), bf16),
            pltpu.VMEM((N_GRP, GROWS, 3712), bf16),
            pltpu.VMEM((N_GRP, GROWS, 3712), bf16),
            pltpu.VMEM((N_GRP, GROWS, 1792), bf16),
            pltpu.VMEM((N_SEQ, ROWS, FEAT_PAD), bf16),
            pltpu.VMEM((N_SEQ, ROWS, FEAT_PAD), bf16),
            pltpu.SemaphoreType.DMA((7,)),
            pltpu.SemaphoreType.DMA((10, N_SEQ)),
            pltpu.SemaphoreType.DMA((10, N_SEQ)),
        ],
        compiler_params=pltpu.CompilerParams(
            collective_id=0, has_side_effects=True, vmem_limit_bytes=56 * 2**20
        ),
    )(
        lengths,
        group_perm,
        page_table,
        rows,
        gains[0],
        qkv_bias.reshape(1, -1),
        gains[1],
        k_pool,
        v_pool,
        qkv_weight,
        o_weight,
        gate_weight,
        up_weight,
        down_weight,
    )
    return out[:, :FEAT].reshape(tokens.shape)


def solution(mesh):
    fused = mesh.shape["seq"] == KV_HEADS and mesh.shape["grp"] == N_GRP
    return jax.shard_map(
        fused_body if fused else body,
        mesh=mesh,
        in_specs=(
            P(None, None, ("grp", "seq")),
            P(),
            P(),
            P(),
            P(("grp", "seq"), None, None),
            P(("grp", "seq"), None, None),
            P(("grp", "seq")),
            P("grp", "seq"),
            P("seq"),
            P("seq", "grp"),
            P(("grp", "seq")),
            P("grp", "seq"),
            P("grp", "seq"),
            P("seq", "grp"),
        ),
        out_specs=P(None, None, ("grp", "seq")),
        check_vma=False,
    )
```

```python
import functools

import jax
import jax.numpy as jnp
from jax import lax
from jax.experimental import pallas as pl
from jax.experimental.pallas import tpu as pltpu
from jax.sharding import PartitionSpec as P

D = 5120
HEADS = 40
KV_HEADS = 8
HEAD_DIM = 128
STEPS = 4
REQ_GRP = 4
SHARD_PAGES = 8
PAGE = 128
BLOCK_PAGES = 4


EPSILON = 1e-06
LOW_SCORE = -1e30
ROPE_BASE = 1000000.0


def rotary(values, position):
    half_dim = values.shape[-1] // 2
    exponent = jnp.arange(half_dim, dtype=jnp.float32) * (2.0 / values.shape[-1])
    inverse = jnp.exp(-exponent * jnp.log(jnp.float32(ROPE_BASE)))
    angle = position[..., None, None] * inverse
    cosine = jnp.cos(angle)
    sine_part = jnp.sin(angle)
    first_half = values[..., :half_dim]
    second_half = values[..., half_dim:]
    return jnp.concatenate(
        [
            first_half * cosine - second_half * sine_part,
            second_half * cosine + first_half * sine_part,
        ],
        axis=-1,
    )


def absorb(carried, query_mat, key_block, value_block, live_mask, score_scale):
    best_score, weight_sums, weighted = carried
    scores = (
        jnp.einsum("hqd,khd->hqk", query_mat, key_block, preferred_element_type=jnp.float32)
        * score_scale
    )
    scores = jnp.where(live_mask, scores, LOW_SCORE)
    fresh_top = jnp.maximum(best_score, jnp.max(scores, axis=-1))
    rescale = jnp.exp(best_score - fresh_top)
    weights = jnp.where(live_mask, jnp.exp(scores - fresh_top[..., None]), 0.0)
    weight_sums = weight_sums * rescale + jnp.sum(weights, axis=-1)
    weighted = weighted * rescale[..., None] + jnp.einsum(
        "hqk,khd->hqd",
        weights.astype(jnp.bfloat16),
        value_block,
        preferred_element_type=jnp.float32,
    )
    return (fresh_top, weight_sums, weighted)


def body(
    tokens,
    lengths,
    group_perm,
    page_table,
    k_pool,
    v_pool,
    gain_in,
    qkv_weight,
    qkv_bias,
    o_weight,
    gain_mid,
    gate_weight,
    up_weight,
    down_weight,
):
    n_seq = lax.axis_size("seq")
    grp_idx = lax.axis_index("grp")
    seq_idx = lax.axis_index("seq")
    group_q = HEADS // KV_HEADS
    query_rows = STEPS * group_q
    q_width = HEADS * HEAD_DIM
    kv_width = KV_HEADS * HEAD_DIM
    score_scale = HEAD_DIM ** (-0.5)
    sorted_rows = jnp.take(tokens, group_perm, axis=0).astype(jnp.float32)
    squares_in = lax.psum(jnp.sum(sorted_rows * sorted_rows, axis=-1), ("grp", "seq"))
    normed_in = (sorted_rows * lax.rsqrt(squares_in / D + EPSILON)[..., None] * gain_in).astype(
        jnp.bfloat16
    )
    proj_part = jnp.einsum(
        "rtc,ck->rtk",
        lax.all_gather(normed_in, "seq", axis=2, tiled=True),
        qkv_weight,
        preferred_element_type=jnp.float32,
    )
    proj_share = (
        lax.psum_scatter(
            proj_part.astype(jnp.bfloat16), "grp", scatter_dimension=0, tiled=True
        ).astype(jnp.float32)
        + qkv_bias
    )
    proj_full = lax.all_gather(proj_share, "seq", axis=2, tiled=True)
    members = lax.dynamic_slice_in_dim(group_perm, grp_idx * REQ_GRP, REQ_GRP)
    my_lengths = jnp.take(lengths, members)
    steps_range = jnp.arange(STEPS, dtype=jnp.int32)
    position = (my_lengths[:, None] + steps_range[None, :]).astype(jnp.float32)
    queries = rotary(
        proj_full[..., :q_width].reshape(REQ_GRP, STEPS, HEADS, HEAD_DIM), position
    ).astype(jnp.bfloat16)
    new_keys = rotary(
        proj_full[..., q_width : q_width + kv_width].reshape(REQ_GRP, STEPS, KV_HEADS, HEAD_DIM),
        position,
    ).astype(jnp.bfloat16)
    new_values = (
        proj_full[..., q_width + kv_width :]
        .reshape(REQ_GRP, STEPS, KV_HEADS, HEAD_DIM)
        .astype(jnp.bfloat16)
    )
    shard_rows = SHARD_PAGES * PAGE
    block_rows = BLOCK_PAGES * PAGE
    shard_base = seq_idx * shard_rows
    slot_table = lax.dynamic_slice_in_dim(
        jnp.take(page_table, members, axis=0), seq_idx * SHARD_PAGES, SHARD_PAGES, 1
    )
    is_last = seq_idx == n_seq - 1
    causal = (
        steps_range[None, :] <= (jnp.arange(query_rows, dtype=jnp.int32) // group_q)[:, None]
    ) & is_last
    causal = causal[None]
    query_all = (
        queries.reshape(REQ_GRP, STEPS, KV_HEADS, group_q, HEAD_DIM)
        .transpose(0, 2, 1, 3, 4)
        .reshape(REQ_GRP, KV_HEADS, query_rows, HEAD_DIM)
    )
    live_all = jnp.clip(my_lengths - shard_base, 0, shard_rows)
    block_offsets = jnp.arange(block_rows, dtype=jnp.int32)
    initial = (
        jnp.full((REQ_GRP, KV_HEADS, query_rows), LOW_SCORE, jnp.float32),
        jnp.zeros((REQ_GRP, KV_HEADS, query_rows), jnp.float32),
        jnp.zeros((REQ_GRP, KV_HEADS, query_rows, HEAD_DIM), jnp.float32),
    )
    absorb_all = jax.vmap(absorb, in_axes=(0, 0, 0, 0, None, None))
    carried = absorb_all(initial, query_all, new_keys, new_values, causal, score_scale)
    absorb_masked = jax.vmap(absorb, in_axes=(0, 0, 0, 0, 0, None))
    block_count = (jnp.max(live_all) + block_rows - 1) // block_rows

    def advance_all(block_index, running):
        slot_ids = lax.dynamic_slice_in_dim(slot_table, block_index * BLOCK_PAGES, BLOCK_PAGES, 1)
        key_block = jnp.take(k_pool, slot_ids.reshape(-1), axis=0).reshape(
            REQ_GRP, block_rows, KV_HEADS, HEAD_DIM
        )
        value_block = jnp.take(v_pool, slot_ids.reshape(-1), axis=0).reshape(
            REQ_GRP, block_rows, KV_HEADS, HEAD_DIM
        )
        positions = shard_base + block_index * block_rows + block_offsets
        live_mask = (positions[None, :] < my_lengths[:, None])[:, None, None, :]
        return absorb_masked(running, query_all, key_block, value_block, live_mask, score_scale)

    best_score, weight_sums, weighted = lax.fori_loop(0, block_count, advance_all, carried)
    top_score = lax.pmax(best_score, "seq")
    factor = jnp.exp(best_score - top_score)
    weight_sums, weighted = (
        lax.psum((weight_sums * factor).astype(jnp.bfloat16), "seq").astype(jnp.float32),
        lax.psum((weighted * factor[..., None]).astype(jnp.bfloat16), "seq").astype(jnp.float32),
    )
    attended = (weighted / weight_sums[..., None]).reshape(
        REQ_GRP, KV_HEADS, STEPS, group_q, HEAD_DIM
    )
    attended = (
        attended.transpose(0, 2, 1, 3, 4).reshape(REQ_GRP, STEPS, q_width).astype(jnp.bfloat16)
    )
    out_width = o_weight.shape[0]
    attended_cols = lax.dynamic_slice_in_dim(attended, seq_idx * out_width, out_width, 2)
    out_terms = jnp.einsum(
        "rtc,cd->rtd",
        lax.all_gather(attended_cols, "grp", axis=0, tiled=True),
        o_weight,
        preferred_element_type=jnp.float32,
    )
    attn_sum = lax.psum_scatter(
        out_terms.astype(jnp.bfloat16), "seq", scatter_dimension=2, tiled=True
    ).astype(jnp.float32)
    residual = sorted_rows + attn_sum
    squares_mid = lax.psum(jnp.sum(residual * residual, axis=-1), ("grp", "seq"))
    normed_mid = (residual * lax.rsqrt(squares_mid / D + EPSILON)[..., None] * gain_mid).astype(
        jnp.bfloat16
    )
    segment = lax.all_gather(normed_mid, "seq", axis=2, tiled=True)
    gate_part = jnp.einsum("rtc,cf->rtf", segment, gate_weight, preferred_element_type=jnp.float32)
    up_part = jnp.einsum("rtc,cf->rtf", segment, up_weight, preferred_element_type=jnp.float32)
    gate_sum, up_sum = (
        lax.psum(gate_part.astype(jnp.bfloat16), "grp").astype(jnp.float32),
        lax.psum(up_part.astype(jnp.bfloat16), "grp").astype(jnp.float32),
    )
    hidden = (jax.nn.silu(gate_sum) * up_sum).astype(jnp.bfloat16)
    down_terms = jnp.einsum("rtf,fd->rtd", hidden, down_weight, preferred_element_type=jnp.float32)
    down_sum = lax.psum_scatter(
        down_terms.astype(jnp.bfloat16), "seq", scatter_dimension=2, tiled=True
    ).astype(jnp.float32)
    restore = jnp.argsort(group_perm)
    return jnp.take(residual + down_sum, restore, axis=0).astype(jnp.bfloat16)


N_GRP = 4
N_SEQ = 8
ROWS = 64
GROWS = REQ_GRP * STEPS
FEAT = D // (N_GRP * N_SEQ)
FEAT_PAD = 256
DEPTH = D // N_GRP
GROUP_Q = HEADS // KV_HEADS
QROWS = 32
SHARD_ROWS = SHARD_PAGES * PAGE
MESH = pl.DeviceIdType.MESH


def stat_lanes(pieces, rows, at=0, width=128, base=None):
    lane = lax.broadcasted_iota(jnp.int32, (rows, width), 1)
    block = jnp.zeros((rows, width), jnp.float32) if base is None else base
    for offset, piece in enumerate(pieces):
        block = jnp.where(lane == at + offset, piece, block)
    return block


def split_bf16(value, count):
    pieces = []
    for _ in range(count):
        piece = value.astype(jnp.bfloat16).astype(jnp.float32)
        pieces.append(piece)
        value = value - piece
    return pieces


def pack(values, parts):
    rows, width = ROWS // parts, 128 // parts
    rest = values[:, 128:]
    below = rest[:rows]
    for a in range(1, parts):
        below = below + pltpu.roll(rest[a * rows : (a + 1) * rows], a * width, 1)
    return jnp.concatenate([values[:, :128], below], axis=0).astype(jnp.bfloat16)


def unpack(block, parts):
    rows, width = ROWS // parts, 128 // parts
    below = block[ROWS:]
    lane = lax.broadcasted_iota(jnp.int32, (rows, 128), 1)
    rest = [
        jnp.where(lane < width, pltpu.roll(below, 128 - a * width, 1) if a else below, 0.0)
        for a in range(parts)
    ]
    return jnp.concatenate([block[:ROWS], jnp.concatenate(rest, axis=0)], axis=1)


def fused_kernel(
    lengths,
    group_perm,
    page_table,
    tokens,
    gain_in,
    qkv_bias,
    gain_mid,
    k_hbm,
    v_hbm,
    qkv_hbm,
    o_hbm,
    gate_hbm,
    up_hbm,
    down_hbm,
    out,
    k_pool,
    v_pool,
    w_qkv,
    w_o,
    w_gate,
    w_up,
    w_down,
    x_all,
    x_wide,
    x_bf,
    qkv_send,
    qkv_recv,
    heads_all,
    q_pairs,
    new_k,
    new_v,
    att_held,
    att_send,
    att_recv,
    att_all,
    wide,
    o_send,
    o_recv,
    mid_all,
    gate_send,
    gate_recv,
    up_send,
    up_recv,
    hid_all,
    down_send,
    down_recv,
    padded,
    gains,
    load_sem,
    send_sem,
    recv_sem,
):
    g = lax.axis_index("grp")
    s = lax.axis_index("seq")
    f32, bf16 = jnp.float32, jnp.bfloat16

    loads = [
        pltpu.make_async_copy(src, dst, load_sem.at[i])
        for i, (src, dst) in enumerate(
            [
                (qkv_hbm, w_qkv),
                (k_hbm, k_pool),
                (v_hbm, v_pool),
                (o_hbm, w_o),
                (gate_hbm, w_gate),
                (up_hbm, w_up),
                (down_hbm, w_down),
            ]
        )
    ]
    for load in loads:
        load.start()
    barrier = pltpu.get_barrier_semaphore()
    for d in range(1, N_SEQ):
        pl.semaphore_signal(
            barrier, inc=1, device_id={"seq": lax.rem(s + d, N_SEQ)}, device_id_type=MESH
        )
    for d in range(1, N_GRP):
        pl.semaphore_signal(
            barrier, inc=1, device_id={"grp": lax.rem(g + d, N_GRP)}, device_id_type=MESH
        )

    def exchange(stage, axis, source, target):
        me, count = (s, N_SEQ) if axis == "seq" else (g, N_GRP)
        copies = []
        for d in range(1, count):
            peer = lax.rem(me + d, count)
            copy = pltpu.make_async_remote_copy(
                src_ref=source(peer),
                dst_ref=target,
                send_sem=send_sem.at[stage, d],
                recv_sem=recv_sem.at[stage, d],
                device_id={axis: peer},
                device_id_type=MESH,
            )
            copy.start()
            copies.append(copy)
        return copies

    def arrive(copies):
        for copy in copies:
            copy.wait_recv()

    started = []

    padded[...] = jnp.zeros_like(padded)
    for i in range(ROWS // STEPS):
        padded[i * STEPS : (i + 1) * STEPS, :FEAT] = tokens[group_perm[i]].astype(f32)
    gains[...] = jnp.zeros_like(gains)
    gains[0:1, :FEAT] = gain_in[...]
    gains[1:2, :FEAT] = gain_mid[...]
    sorted_rows = padded[...]

    def feature_block(values, gain):
        squares = jnp.sum(values * values, axis=1, keepdims=True)
        return pack(
            stat_lanes(split_bf16(squares, 2), ROWS, FEAT, FEAT_PAD, values * gain), 2
        )

    x_all[s] = feature_block(sorted_rows, gains[0:1, :])
    pl.semaphore_wait(barrier, N_SEQ + N_GRP - 2)

    def gather_features(stage, blocks):
        copies = exchange(stage, "seq", lambda peer: blocks.at[s], blocks.at[s])
        started.extend(copies)
        arrive(copies)
        lane = lax.broadcasted_iota(jnp.int32, (ROWS, FEAT_PAD), 1)
        x_wide[...] = jnp.zeros_like(x_wide)
        squares = jnp.zeros((ROWS, 1), f32)
        for i in range(N_SEQ):
            block = unpack(blocks[i].astype(f32), 2)
            kept = jnp.where(lane < FEAT, block, 0.0)
            squares = squares + jnp.sum(block - kept, axis=1, keepdims=True)
            first = i * FEAT // 128 * 128
            kept = jnp.concatenate([kept, jnp.zeros((ROWS, 128), f32)], axis=1)
            if i * FEAT - first:
                kept = pltpu.roll(kept, i * FEAT - first, 1)
            x_wide[:, first : first + 384] += kept
        x_bf[...] = x_wide[:, :DEPTH].astype(bf16)
        return squares

    squares_in = gather_features(0, x_all)

    loads[0].wait()
    part = jnp.dot(x_bf[...], w_qkv[...], preferred_element_type=f32).astype(bf16)
    stats = stat_lanes(split_bf16(squares_in, 2), ROWS).astype(bf16)
    for i in range(N_GRP):
        rows = slice(i * GROWS, (i + 1) * GROWS)
        qkv_send[i, :, :896] = part[rows]
        qkv_send[i, :, 896:] = stats[rows]
    copies = exchange(1, "grp", lambda peer: qkv_send.at[peer], qkv_recv.at[g])
    started.extend(copies)
    qkv_recv[g] = qkv_send[g]

    row16 = lax.broadcasted_iota(jnp.int32, (GROWS, HEAD_DIM), 0)
    lane16 = lax.broadcasted_iota(jnp.int32, (GROWS, HEAD_DIM), 1)
    position = row16 % STEPS
    for r in range(REQ_GRP):
        length = lengths[group_perm[g * REQ_GRP + r]]
        position = position + jnp.where(row16 // STEPS == r, length, 0)
    half = HEAD_DIM // 2
    exponent = (lane16 % half).astype(f32) * (2.0 / HEAD_DIM)
    angle = position.astype(f32) * jnp.exp(-exponent * jnp.log(jnp.full((), ROPE_BASE, f32)))
    cosine = jnp.cos(angle)
    sine = jnp.where(lane16 < half, -jnp.sin(angle), jnp.sin(angle))

    arrive(copies)
    summed = sum(qkv_recv[i].astype(f32) for i in range(N_GRP))
    scale = lax.rsqrt(jnp.sum(summed[:, 896:], axis=1, keepdims=True) / D + EPSILON)
    share = summed[:, :896] * scale + qkv_bias[...].reshape(1, 896)
    per_dev = 896 // HEAD_DIM
    for j in range(per_dev):
        unit = share[:, j * HEAD_DIM : (j + 1) * HEAD_DIM]
        turned = unit * cosine + pltpu.roll(unit, half, 1) * sine
        unit = jnp.where(s * per_dev + j < HEADS + KV_HEADS, turned, unit)
        heads_all[s, :, j * HEAD_DIM : (j + 1) * HEAD_DIM] = unit.astype(bf16)
    copies = exchange(2, "seq", lambda peer: heads_all.at[s], heads_all.at[s])
    started.extend(copies)
    q_pairs[...] = jnp.zeros_like(q_pairs)
    arrive(copies)

    def head(h):
        lane = (h % per_dev) * HEAD_DIM
        return heads_all[h // per_dev, :, lane : lane + HEAD_DIM]

    n_q = REQ_GRP * QROWS
    spread_row = lax.broadcasted_iota(jnp.int32, (n_q, GROUP_Q * GROWS), 0)
    spread_col = lax.broadcasted_iota(jnp.int32, (n_q, GROUP_Q * GROWS), 1)
    spread = (
        (spread_row // QROWS == spread_col % GROWS // STEPS)
        & (spread_row % QROWS // STEPS == spread_col // GROWS)
        & (spread_row % STEPS == spread_col % STEPS)
    ).astype(f32).astype(bf16)
    for k in range(KV_HEADS):
        stacked = jnp.concatenate([head(k * GROUP_Q + j) for j in range(GROUP_Q)], axis=0)
        placed = jnp.dot(spread, stacked, preferred_element_type=f32).astype(bf16)
        for r in range(REQ_GRP):
            q_pairs[
                r,
                k // 2,
                (k % 2) * QROWS : (k % 2 + 1) * QROWS,
                (k % 2) * HEAD_DIM : (k % 2 + 1) * HEAD_DIM,
            ] = placed[r * QROWS : (r + 1) * QROWS]
        new_k[:, k * HEAD_DIM : (k + 1) * HEAD_DIM] = head(HEADS + k)
        new_v[:, k * HEAD_DIM : (k + 1) * HEAD_DIM] = head(HEADS + KV_HEADS + k)

    loads[1].wait()
    loads[2].wait()
    score_scale = HEAD_DIM ** (-0.5)
    new_row = lax.broadcasted_iota(jnp.int32, (2 * QROWS, GROWS), 0)
    new_col = lax.broadcasted_iota(jnp.int32, (2 * QROWS, GROWS), 1)
    causal = (new_col % STEPS <= new_row % STEPS) & (s == N_SEQ - 1)
    columns = lax.broadcasted_iota(jnp.int32, (2 * QROWS, SHARD_ROWS), 1)
    contract_last = (((1,), (1,)), ((), ()))

    def attend(r, carry):
        request = group_perm[g * REQ_GRP + r]
        live = columns < lengths[request] - s * SHARD_ROWS
        own = causal & (new_col // STEPS == r)
        slots = [page_table[request, s * SHARD_PAGES + p] for p in range(SHARD_PAGES)]
        for pair in range(KV_HEADS // 2):
            lanes = slice(pair * 256, (pair + 1) * 256)
            query = q_pairs[r, pair]
            keys = jnp.concatenate([k_pool[slot, :, lanes] for slot in slots], axis=0)
            values = jnp.concatenate([v_pool[slot, :, lanes] for slot in slots], axis=0)
            scores = (
                lax.dot_general(query, keys, contract_last, preferred_element_type=f32)
                * score_scale
            )
            scores = jnp.where(live, scores, LOW_SCORE)
            fresh = (
                lax.dot_general(query, new_k[:, lanes], contract_last, preferred_element_type=f32)
                * score_scale
            )
            fresh = jnp.where(own, fresh, LOW_SCORE)
            top = jnp.maximum(
                jnp.max(scores, axis=1, keepdims=True), jnp.max(fresh, axis=1, keepdims=True)
            )
            weights = jnp.where(live, jnp.exp(scores - top), 0.0)
            new_weights = jnp.where(own, jnp.exp(fresh - top), 0.0)
            total = jnp.sum(weights, axis=1, keepdims=True) + jnp.sum(
                new_weights, axis=1, keepdims=True
            )
            weighted = jnp.dot(weights.astype(bf16), values, preferred_element_type=f32) + jnp.dot(
                new_weights.astype(bf16), new_v[:, lanes], preferred_element_type=f32
            )
            block = stat_lanes(split_bf16(top, 3) + split_bf16(total, 2), 2 * QROWS)
            rows = pl.ds(pl.multiple_of(r * QROWS, QROWS), QROWS)
            for k in range(2):
                mine = slice(k * QROWS, (k + 1) * QROWS)
                att_held[2 * pair + k, rows, :HEAD_DIM] = weighted[
                    mine, k * HEAD_DIM : (k + 1) * HEAD_DIM
                ].astype(bf16)
                att_held[2 * pair + k, rows, HEAD_DIM:] = block[mine].astype(bf16)
        return carry

    lax.fori_loop(0, REQ_GRP, attend, 0)
    pick_row = lax.broadcasted_iota(jnp.int32, (GROUP_Q * GROWS, n_q), 0)
    pick_col = lax.broadcasted_iota(jnp.int32, (GROUP_Q * GROWS, n_q), 1)
    pick = (
        (pick_col // QROWS == pick_row % GROWS // STEPS)
        & (pick_col % QROWS // STEPS == pick_row // GROWS)
        & (pick_col % STEPS == pick_row % STEPS)
    ).astype(f32).astype(bf16)
    n_out = GROUP_Q * GROWS
    for k in range(KV_HEADS):
        picked = jnp.dot(pick, att_held[k], preferred_element_type=f32)
        below = picked[:GROWS, HEAD_DIM:]
        for j in range(1, GROUP_Q):
            below = below + pltpu.roll(picked[j * GROWS : (j + 1) * GROWS, HEAD_DIM:], 8 * j, 1)
        att_send[k, :n_out] = picked[:, :HEAD_DIM].astype(bf16)
        att_send[k, n_out:] = below.astype(bf16)
    copies = exchange(3, "seq", lambda peer: att_send.at[peer], att_recv.at[s])
    started.extend(copies)
    att_recv[s] = att_send[s]
    arrive(copies)

    stat_lane = lax.broadcasted_iota(jnp.int32, (GROWS, HEAD_DIM), 1) % 8 == 0
    tops, sums = [], []
    for i in range(N_SEQ):
        block = att_recv[i, n_out:, :].astype(f32)
        shifted = [block] + [pltpu.roll(block, HEAD_DIM - n, 1) for n in range(1, 5)]
        tops.append(jnp.where(stat_lane, shifted[0] + shifted[1] + shifted[2], 0.0))
        sums.append(jnp.where(stat_lane, shifted[3] + shifted[4], 1.0))
    best = functools.reduce(jnp.maximum, tops)
    factors = [jnp.exp(top - best) for top in tops]
    total = sum(factor * part_sum for factor, part_sum in zip(factors, sums))
    for j in range(GROUP_Q):
        rows = slice(j * GROWS, (j + 1) * GROWS)
        weighted = sum(
            factors[i][:, 8 * j : 8 * j + 1] * att_recv[i, rows, :].astype(f32)
            for i in range(N_SEQ)
        )
        attended = weighted / total[:, 8 * j : 8 * j + 1]
        att_all[g, :, j * HEAD_DIM : (j + 1) * HEAD_DIM] = attended.astype(bf16)
    copies = exchange(4, "grp", lambda peer: att_all.at[g], att_all.at[g])
    started.extend(copies)
    loads[3].wait()
    arrive(copies)

    feature = lax.broadcasted_iota(jnp.int32, (ROWS, FEAT_PAD), 1) < FEAT

    def scatter_features(stage, send, recv):
        for i in range(N_SEQ):
            first = i * FEAT // 128 * 128
            window = wide[:, first : first + 384]
            if i * FEAT - first:
                window = pltpu.roll(window, 384 - (i * FEAT - first), 1)
            send[i] = pack(jnp.where(feature, window[:, :FEAT_PAD], 0.0), 4)
        copies = exchange(stage, "seq", lambda peer: send.at[peer], recv.at[s])
        started.extend(copies)
        recv[s] = send[s]
        arrive(copies)
        return unpack(sum(recv[i].astype(f32) for i in range(N_SEQ)), 4)

    columns_in = jnp.concatenate([att_all[i] for i in range(N_GRP)], axis=0)
    wide[:, DEPTH:] = jnp.zeros((ROWS, 128), f32)
    wide[:, :DEPTH] = jnp.dot(columns_in, w_o[...], preferred_element_type=f32)
    attn_sum = scatter_features(5, o_send, o_recv)
    residual = sorted_rows + attn_sum
    mid_all[s] = feature_block(residual, gains[1:2, :])
    squares_mid = gather_features(6, mid_all)

    stats = stat_lanes(split_bf16(squares_mid, 2), ROWS).astype(bf16)
    for i in range(N_GRP):
        gate_send[i, :, 1792:] = stats[i * GROWS : (i + 1) * GROWS]

    def project(weight, send):
        def ff_tile(c, carry):
            first = pl.multiple_of(c * 256, 256)
            tile = lax.dot_general(
                x_bf[...], weight[pl.ds(first, 256), :], contract_last, preferred_element_type=f32
            ).astype(bf16)
            for i in range(N_GRP):
                send[i, :, pl.ds(first, 256)] = tile[i * GROWS : (i + 1) * GROWS]
            return carry

        lax.fori_loop(0, 6, ff_tile, 0)
        tile = lax.dot_general(
            x_bf[...], weight[1536:1728, :], contract_last, preferred_element_type=f32
        )
        tile = jnp.concatenate([tile, jnp.zeros((ROWS, 64), f32)], axis=1).astype(bf16)
        for i in range(N_GRP):
            send[i, :, 1536:1792] = tile[i * GROWS : (i + 1) * GROWS]

    loads[4].wait()
    project(w_gate, gate_send)
    gate_copies = exchange(7, "grp", lambda peer: gate_send.at[peer], gate_recv.at[g])
    started.extend(gate_copies)
    loads[5].wait()
    project(w_up, up_send)
    up_copies = exchange(10, "grp", lambda peer: up_send.at[peer], up_recv.at[g])
    started.extend(up_copies)
    gate_recv[g] = gate_send[g]
    up_recv[g] = up_send[g]
    arrive(gate_copies)
    stat = sum(gate_recv[i, :, 1792:].astype(f32) for i in range(N_GRP))
    scale = lax.rsqrt(jnp.sum(stat, axis=1, keepdims=True) / D + EPSILON)
    gate = sum(gate_recv[i, :, :1792].astype(f32) for i in range(N_GRP)) * scale
    gate = gate / (1.0 + jnp.exp(-gate))
    arrive(up_copies)
    up = sum(up_recv[i].astype(f32) for i in range(N_GRP)) * scale
    hid_all[g] = (gate * up).astype(bf16)
    copies = exchange(8, "grp", lambda peer: hid_all.at[g], hid_all.at[g])
    started.extend(copies)
    loads[6].wait()
    arrive(copies)

    def down_tile(c, carry):
        first = pl.multiple_of(c * 256, 256)
        hidden = jnp.concatenate([hid_all[i, :, :1728] for i in range(N_GRP)], axis=0)
        wide[:, pl.ds(first, 256)] = jnp.dot(
            hidden, w_down[:, pl.ds(first, 256)], preferred_element_type=f32
        )
        return carry

    lax.fori_loop(0, DEPTH // 256, down_tile, 0)
    down_sum = scatter_features(9, down_send, down_recv)
    final = (residual + down_sum).astype(bf16)
    row_i = lax.broadcasted_iota(jnp.int32, (ROWS, ROWS), 0)
    col_i = lax.broadcasted_iota(jnp.int32, (ROWS, ROWS), 1)
    origin = jnp.zeros((ROWS, ROWS), jnp.int32)
    for i in range(ROWS // STEPS):
        origin = jnp.where(col_i // STEPS == i, group_perm[i], origin)
    back = (
        ((row_i // STEPS) == origin) & ((col_i % STEPS) == (row_i % STEPS))
    ).astype(f32).astype(bf16)
    ordered = jnp.dot(back, final, preferred_element_type=f32)
    for i in range(ROWS // STEPS):
        out[i] = ordered[i * STEPS : (i + 1) * STEPS, :FEAT].astype(bf16)
    for copy in started:
        copy.wait_send()


def fused_body(
    tokens,
    lengths,
    group_perm,
    page_table,
    k_pool,
    v_pool,
    gain_in,
    qkv_weight,
    qkv_bias,
    o_weight,
    gain_mid,
    gate_weight,
    up_weight,
    down_weight,
):
    gains = [gain.reshape(1, FEAT) for gain in (gain_in, gain_mid)]
    gate_rows, up_rows = gate_weight.T, up_weight.T
    smem = pl.BlockSpec(memory_space=pltpu.SMEM)
    vmem = pl.BlockSpec(memory_space=pltpu.VMEM)
    hbm = pl.BlockSpec(memory_space=pl.ANY)
    bf16, f32 = jnp.bfloat16, jnp.float32
    return pl.pallas_call(
        fused_kernel,
        out_shape=jax.ShapeDtypeStruct(tokens.shape, bf16),
        in_specs=[smem] * 3 + [vmem] * 4 + [hbm] * 7,
        out_specs=vmem,
        scratch_shapes=[
            pltpu.VMEM(k_pool.shape, bf16),
            pltpu.VMEM(v_pool.shape, bf16),
            pltpu.VMEM(qkv_weight.shape, bf16),
            pltpu.VMEM(o_weight.shape, bf16),
            pltpu.VMEM(gate_rows.shape, bf16),
            pltpu.VMEM(up_rows.shape, bf16),
            pltpu.VMEM(down_weight.shape, bf16),
            pltpu.VMEM((N_SEQ, 96, 128), bf16),
            pltpu.VMEM((ROWS, DEPTH + 128), f32),
            pltpu.VMEM((ROWS, DEPTH), bf16),
            pltpu.VMEM((N_GRP, GROWS, 1024), bf16),
            pltpu.VMEM((N_GRP, GROWS, 1024), bf16),
            pltpu.VMEM((N_SEQ, GROWS, 896), bf16),
            pltpu.VMEM((REQ_GRP, KV_HEADS // 2, 2 * QROWS, 256), bf16),
            pltpu.VMEM((GROWS, KV_HEADS * HEAD_DIM), bf16),
            pltpu.VMEM((GROWS, KV_HEADS * HEAD_DIM), bf16),
            pltpu.VMEM((N_SEQ, REQ_GRP * QROWS, 2 * HEAD_DIM), bf16),
            pltpu.VMEM((N_SEQ, 96, 128), bf16),
            pltpu.VMEM((N_SEQ, 96, 128), bf16),
            pltpu.VMEM((N_GRP, GROWS, GROUP_Q * HEAD_DIM), bf16),
            pltpu.VMEM((ROWS, DEPTH + 128), f32),
            pltpu.VMEM((N_SEQ, 80, 128), bf16),
            pltpu.VMEM((N_SEQ, 80, 128), bf16),
            pltpu.VMEM((N_SEQ, 96, 128), bf16),
            pltpu.VMEM((N_GRP, GROWS, 1920), bf16),
            pltpu.VMEM((N_GRP, GROWS, 1920), bf16),
            pltpu.VMEM((N_GRP, GROWS, 1792), bf16),
            pltpu.VMEM((N_GRP, GROWS, 1792), bf16),
            pltpu.VMEM((N_GRP, GROWS, 1792), bf16),
            pltpu.VMEM((N_SEQ, 80, 128), bf16),
            pltpu.VMEM((N_SEQ, 80, 128), bf16),
            pltpu.VMEM((ROWS, FEAT_PAD), f32),
            pltpu.VMEM((8, FEAT_PAD), f32),
            pltpu.SemaphoreType.DMA((7,)),
            pltpu.SemaphoreType.DMA((11, N_SEQ)),
            pltpu.SemaphoreType.DMA((11, N_SEQ)),
        ],
        compiler_params=pltpu.CompilerParams(
            collective_id=0, has_side_effects=True, vmem_limit_bytes=56 * 2**20
        ),
    )(
        lengths,
        group_perm,
        page_table,
        tokens,
        gains[0],
        qkv_bias,
        gains[1],
        k_pool,
        v_pool,
        qkv_weight,
        o_weight,
        gate_rows,
        up_rows,
        down_weight,
    )


def solution(mesh):
    fused = mesh.shape["seq"] == KV_HEADS and mesh.shape["grp"] == N_GRP
    return jax.shard_map(
        fused_body if fused else body,
        mesh=mesh,
        in_specs=(
            P(None, None, ("grp", "seq")),
            P(),
            P(),
            P(),
            P(("grp", "seq"), None, None),
            P(("grp", "seq"), None, None),
            P(("grp", "seq")),
            P("grp", "seq"),
            P("seq"),
            P("seq", "grp"),
            P(("grp", "seq")),
            P("grp", "seq"),
            P("grp", "seq"),
            P("seq", "grp"),
        ),
        out_specs=P(None, None, ("grp", "seq")),
        check_vma=False,
    )
```

```python
import functools

import jax
import jax.numpy as jnp
from jax import lax
from jax.experimental import pallas as pl
from jax.experimental.pallas import tpu as pltpu
from jax.sharding import PartitionSpec as P

D = 5120
HEADS = 40
KV_HEADS = 8
HEAD_DIM = 128
STEPS = 4
REQ_GRP = 4
SHARD_PAGES = 8
PAGE = 128
BLOCK_PAGES = 4


EPSILON = 1e-06
LOW_SCORE = -1e30
ROPE_BASE = 1000000.0


def rotary(values, position):
    half_dim = values.shape[-1] // 2
    exponent = jnp.arange(half_dim, dtype=jnp.float32) * (2.0 / values.shape[-1])
    inverse = jnp.exp(-exponent * jnp.log(jnp.float32(ROPE_BASE)))
    angle = position[..., None, None] * inverse
    cosine = jnp.cos(angle)
    sine_part = jnp.sin(angle)
    first_half = values[..., :half_dim]
    second_half = values[..., half_dim:]
    return jnp.concatenate(
        [
            first_half * cosine - second_half * sine_part,
            second_half * cosine + first_half * sine_part,
        ],
        axis=-1,
    )


def absorb(carried, query_mat, key_block, value_block, live_mask, score_scale):
    best_score, weight_sums, weighted = carried
    scores = (
        jnp.einsum("hqd,khd->hqk", query_mat, key_block, preferred_element_type=jnp.float32)
        * score_scale
    )
    scores = jnp.where(live_mask, scores, LOW_SCORE)
    fresh_top = jnp.maximum(best_score, jnp.max(scores, axis=-1))
    rescale = jnp.exp(best_score - fresh_top)
    weights = jnp.where(live_mask, jnp.exp(scores - fresh_top[..., None]), 0.0)
    weight_sums = weight_sums * rescale + jnp.sum(weights, axis=-1)
    weighted = weighted * rescale[..., None] + jnp.einsum(
        "hqk,khd->hqd",
        weights.astype(jnp.bfloat16),
        value_block,
        preferred_element_type=jnp.float32,
    )
    return (fresh_top, weight_sums, weighted)


def body(
    tokens,
    lengths,
    group_perm,
    page_table,
    k_pool,
    v_pool,
    gain_in,
    qkv_weight,
    qkv_bias,
    o_weight,
    gain_mid,
    gate_weight,
    up_weight,
    down_weight,
):
    n_seq = lax.axis_size("seq")
    grp_idx = lax.axis_index("grp")
    seq_idx = lax.axis_index("seq")
    group_q = HEADS // KV_HEADS
    query_rows = STEPS * group_q
    q_width = HEADS * HEAD_DIM
    kv_width = KV_HEADS * HEAD_DIM
    score_scale = HEAD_DIM ** (-0.5)
    sorted_rows = jnp.take(tokens, group_perm, axis=0).astype(jnp.float32)
    squares_in = lax.psum(jnp.sum(sorted_rows * sorted_rows, axis=-1), ("grp", "seq"))
    normed_in = (sorted_rows * lax.rsqrt(squares_in / D + EPSILON)[..., None] * gain_in).astype(
        jnp.bfloat16
    )
    proj_part = jnp.einsum(
        "rtc,ck->rtk",
        lax.all_gather(normed_in, "seq", axis=2, tiled=True),
        qkv_weight,
        preferred_element_type=jnp.float32,
    )
    proj_share = (
        lax.psum_scatter(
            proj_part.astype(jnp.bfloat16), "grp", scatter_dimension=0, tiled=True
        ).astype(jnp.float32)
        + qkv_bias
    )
    proj_full = lax.all_gather(proj_share, "seq", axis=2, tiled=True)
    members = lax.dynamic_slice_in_dim(group_perm, grp_idx * REQ_GRP, REQ_GRP)
    my_lengths = jnp.take(lengths, members)
    steps_range = jnp.arange(STEPS, dtype=jnp.int32)
    position = (my_lengths[:, None] + steps_range[None, :]).astype(jnp.float32)
    queries = rotary(
        proj_full[..., :q_width].reshape(REQ_GRP, STEPS, HEADS, HEAD_DIM), position
    ).astype(jnp.bfloat16)
    new_keys = rotary(
        proj_full[..., q_width : q_width + kv_width].reshape(REQ_GRP, STEPS, KV_HEADS, HEAD_DIM),
        position,
    ).astype(jnp.bfloat16)
    new_values = (
        proj_full[..., q_width + kv_width :]
        .reshape(REQ_GRP, STEPS, KV_HEADS, HEAD_DIM)
        .astype(jnp.bfloat16)
    )
    shard_rows = SHARD_PAGES * PAGE
    block_rows = BLOCK_PAGES * PAGE
    shard_base = seq_idx * shard_rows
    slot_table = lax.dynamic_slice_in_dim(
        jnp.take(page_table, members, axis=0), seq_idx * SHARD_PAGES, SHARD_PAGES, 1
    )
    is_last = seq_idx == n_seq - 1
    causal = (
        steps_range[None, :] <= (jnp.arange(query_rows, dtype=jnp.int32) // group_q)[:, None]
    ) & is_last
    causal = causal[None]
    query_all = (
        queries.reshape(REQ_GRP, STEPS, KV_HEADS, group_q, HEAD_DIM)
        .transpose(0, 2, 1, 3, 4)
        .reshape(REQ_GRP, KV_HEADS, query_rows, HEAD_DIM)
    )
    live_all = jnp.clip(my_lengths - shard_base, 0, shard_rows)
    block_offsets = jnp.arange(block_rows, dtype=jnp.int32)
    initial = (
        jnp.full((REQ_GRP, KV_HEADS, query_rows), LOW_SCORE, jnp.float32),
        jnp.zeros((REQ_GRP, KV_HEADS, query_rows), jnp.float32),
        jnp.zeros((REQ_GRP, KV_HEADS, query_rows, HEAD_DIM), jnp.float32),
    )
    absorb_all = jax.vmap(absorb, in_axes=(0, 0, 0, 0, None, None))
    carried = absorb_all(initial, query_all, new_keys, new_values, causal, score_scale)
    absorb_masked = jax.vmap(absorb, in_axes=(0, 0, 0, 0, 0, None))
    block_count = (jnp.max(live_all) + block_rows - 1) // block_rows

    def advance_all(block_index, running):
        slot_ids = lax.dynamic_slice_in_dim(slot_table, block_index * BLOCK_PAGES, BLOCK_PAGES, 1)
        key_block = jnp.take(k_pool, slot_ids.reshape(-1), axis=0).reshape(
            REQ_GRP, block_rows, KV_HEADS, HEAD_DIM
        )
        value_block = jnp.take(v_pool, slot_ids.reshape(-1), axis=0).reshape(
            REQ_GRP, block_rows, KV_HEADS, HEAD_DIM
        )
        positions = shard_base + block_index * block_rows + block_offsets
        live_mask = (positions[None, :] < my_lengths[:, None])[:, None, None, :]
        return absorb_masked(running, query_all, key_block, value_block, live_mask, score_scale)

    best_score, weight_sums, weighted = lax.fori_loop(0, block_count, advance_all, carried)
    top_score = lax.pmax(best_score, "seq")
    factor = jnp.exp(best_score - top_score)
    weight_sums, weighted = (
        lax.psum((weight_sums * factor).astype(jnp.bfloat16), "seq").astype(jnp.float32),
        lax.psum((weighted * factor[..., None]).astype(jnp.bfloat16), "seq").astype(jnp.float32),
    )
    attended = (weighted / weight_sums[..., None]).reshape(
        REQ_GRP, KV_HEADS, STEPS, group_q, HEAD_DIM
    )
    attended = (
        attended.transpose(0, 2, 1, 3, 4).reshape(REQ_GRP, STEPS, q_width).astype(jnp.bfloat16)
    )
    out_width = o_weight.shape[0]
    attended_cols = lax.dynamic_slice_in_dim(attended, seq_idx * out_width, out_width, 2)
    out_terms = jnp.einsum(
        "rtc,cd->rtd",
        lax.all_gather(attended_cols, "grp", axis=0, tiled=True),
        o_weight,
        preferred_element_type=jnp.float32,
    )
    attn_sum = lax.psum_scatter(
        out_terms.astype(jnp.bfloat16), "seq", scatter_dimension=2, tiled=True
    ).astype(jnp.float32)
    residual = sorted_rows + attn_sum
    squares_mid = lax.psum(jnp.sum(residual * residual, axis=-1), ("grp", "seq"))
    normed_mid = (residual * lax.rsqrt(squares_mid / D + EPSILON)[..., None] * gain_mid).astype(
        jnp.bfloat16
    )
    segment = lax.all_gather(normed_mid, "seq", axis=2, tiled=True)
    gate_part = jnp.einsum("rtc,cf->rtf", segment, gate_weight, preferred_element_type=jnp.float32)
    up_part = jnp.einsum("rtc,cf->rtf", segment, up_weight, preferred_element_type=jnp.float32)
    gate_sum, up_sum = (
        lax.psum(gate_part.astype(jnp.bfloat16), "grp").astype(jnp.float32),
        lax.psum(up_part.astype(jnp.bfloat16), "grp").astype(jnp.float32),
    )
    hidden = (jax.nn.silu(gate_sum) * up_sum).astype(jnp.bfloat16)
    down_terms = jnp.einsum("rtf,fd->rtd", hidden, down_weight, preferred_element_type=jnp.float32)
    down_sum = lax.psum_scatter(
        down_terms.astype(jnp.bfloat16), "seq", scatter_dimension=2, tiled=True
    ).astype(jnp.float32)
    restore = jnp.argsort(group_perm)
    return jnp.take(residual + down_sum, restore, axis=0).astype(jnp.bfloat16)


N_GRP = 4
N_SEQ = 8
ROWS = 64
GROWS = REQ_GRP * STEPS
FEAT = D // (N_GRP * N_SEQ)
FEAT_PAD = 256
DEPTH = D // N_GRP
GROUP_Q = HEADS // KV_HEADS
QROWS = 32
SHARD_ROWS = SHARD_PAGES * PAGE
MESH = pl.DeviceIdType.MESH


def stat_lanes(pieces, rows, at=0, width=128, base=None):
    lane = lax.broadcasted_iota(jnp.int32, (rows, width), 1)
    block = jnp.zeros((rows, width), jnp.float32) if base is None else base
    for offset, piece in enumerate(pieces):
        block = jnp.where(lane == at + offset, piece, block)
    return block


def split_bf16(value, count):
    pieces = []
    for _ in range(count):
        piece = value.astype(jnp.bfloat16).astype(jnp.float32)
        pieces.append(piece)
        value = value - piece
    return pieces


def pack(values, parts):
    rows, width = ROWS // parts, 128 // parts
    rest = values[:, 128:]
    below = rest[:rows]
    for a in range(1, parts):
        below = below + pltpu.roll(rest[a * rows : (a + 1) * rows], a * width, 1)
    return jnp.concatenate([values[:, :128], below], axis=0).astype(jnp.bfloat16)


def unpack(block, parts):
    rows, width = ROWS // parts, 128 // parts
    below = block[ROWS:]
    lane = lax.broadcasted_iota(jnp.int32, (rows, 128), 1)
    rest = [
        jnp.where(lane < width, pltpu.roll(below, 128 - a * width, 1) if a else below, 0.0)
        for a in range(parts)
    ]
    return jnp.concatenate([block[:ROWS], jnp.concatenate(rest, axis=0)], axis=1)


def fused_kernel(
    lengths,
    group_perm,
    page_table,
    tokens,
    gain_in,
    qkv_bias,
    gain_mid,
    k_hbm,
    v_hbm,
    qkv_hbm,
    o_hbm,
    gate_hbm,
    up_hbm,
    down_hbm,
    out,
    k_pool,
    v_pool,
    w_qkv,
    w_o,
    w_gate,
    w_up,
    w_down,
    x_all,
    x_wide,
    x_bf,
    qkv_send,
    qkv_recv,
    heads_all,
    q_pairs,
    new_k,
    new_v,
    att_held,
    att_send,
    att_recv,
    att_all,
    wide,
    o_send,
    o_recv,
    mid_all,
    gate_send,
    gate_recv,
    up_send,
    up_recv,
    hid_all,
    down_send,
    down_recv,
    padded,
    gains,
    load_sem,
    send_sem,
    recv_sem,
):
    g = lax.axis_index("grp")
    s = lax.axis_index("seq")
    f32, bf16 = jnp.float32, jnp.bfloat16

    loads = [
        pltpu.make_async_copy(src, dst, load_sem.at[i])
        for i, (src, dst) in enumerate(
            [
                (qkv_hbm, w_qkv),
                (k_hbm, k_pool),
                (v_hbm, v_pool),
                (o_hbm, w_o),
                (gate_hbm, w_gate),
                (up_hbm, w_up),
                (down_hbm, w_down),
            ]
        )
    ]
    for load in loads:
        load.start()
    barrier = pltpu.get_barrier_semaphore()
    for d in range(1, N_SEQ):
        pl.semaphore_signal(
            barrier, inc=1, device_id={"seq": lax.rem(s + d, N_SEQ)}, device_id_type=MESH
        )
    for d in range(1, N_GRP):
        pl.semaphore_signal(
            barrier, inc=1, device_id={"grp": lax.rem(g + d, N_GRP)}, device_id_type=MESH
        )

    def exchange(stage, axis, source, target):
        me, count = (s, N_SEQ) if axis == "seq" else (g, N_GRP)
        copies = []
        for d in sorted(range(1, count), key=lambda d: abs(2 * d - count)):
            peer = lax.rem(me + d, count)
            copy = pltpu.make_async_remote_copy(
                src_ref=source(peer),
                dst_ref=target,
                send_sem=send_sem.at[stage, d],
                recv_sem=recv_sem.at[stage, d],
                device_id={axis: peer},
                device_id_type=MESH,
            )
            copy.start()
            copies.append(copy)
        return copies

    def gather_seq(stage, blocks):
        partner = s + 1 - 2 * lax.rem(s, 2)

        def push(block, peer, at):
            copy = pltpu.make_async_remote_copy(
                src_ref=blocks.at[block],
                dst_ref=blocks.at[block],
                send_sem=send_sem.at[stage, at],
                recv_sem=recv_sem.at[stage, at],
                device_id={"seq": peer},
                device_id_type=MESH,
            )
            copy.start()
            started.append(copy)
            return copy

        along = {d: push(s, lax.rem(s + d, N_SEQ), d) for d in (4, 2, 6)}
        across = [push(s, partner, 1)]
        for d in (2, 6, 4):
            along[d].wait_recv()
            across.append(push(lax.rem(s - d + N_SEQ, N_SEQ), partner, d + 1))
        arrive(across)

    def arrive(copies):
        for copy in copies:
            copy.wait_recv()

    started = []

    padded[...] = jnp.zeros_like(padded)
    wide[...] = jnp.zeros_like(wide)
    for i in range(ROWS // STEPS):
        padded[i * STEPS : (i + 1) * STEPS, :FEAT] = tokens[group_perm[i]].astype(f32)
    gains[...] = jnp.zeros_like(gains)
    gains[0:1, :FEAT] = gain_in[...]
    gains[1:2, :FEAT] = gain_mid[...]
    sorted_rows = padded[...]

    def feature_block(values, gain):
        squares = jnp.sum(values * values, axis=1, keepdims=True)
        return pack(
            stat_lanes(split_bf16(squares, 2), ROWS, FEAT, FEAT_PAD, values * gain), 2
        )

    x_all[s] = feature_block(sorted_rows, gains[0:1, :])
    pl.semaphore_wait(barrier, N_SEQ + N_GRP - 2)

    def gather_features(stage, blocks):
        gather_seq(stage, blocks)
        lane = lax.broadcasted_iota(jnp.int32, (ROWS, FEAT_PAD), 1)
        x_wide[...] = jnp.zeros_like(x_wide)
        squares = jnp.zeros((ROWS, 1), f32)
        for i in range(N_SEQ):
            block = unpack(blocks[i].astype(f32), 2)
            kept = jnp.where(lane < FEAT, block, 0.0)
            squares = squares + jnp.sum(block - kept, axis=1, keepdims=True)
            first = i * FEAT // 128 * 128
            kept = jnp.concatenate([kept, jnp.zeros((ROWS, 128), f32)], axis=1)
            if i * FEAT - first:
                kept = pltpu.roll(kept, i * FEAT - first, 1)
            x_wide[:, first : first + 384] += kept
        x_bf[...] = x_wide[:, :DEPTH].astype(bf16)
        return squares

    squares_in = gather_features(0, x_all)

    loads[0].wait()
    part = jnp.dot(x_bf[...], w_qkv[...], preferred_element_type=f32).astype(bf16)
    stats = stat_lanes(split_bf16(squares_in, 2), ROWS).astype(bf16)
    for i in range(N_GRP):
        rows = slice(i * GROWS, (i + 1) * GROWS)
        qkv_send[i, :, :896] = part[rows]
        qkv_send[i, :, 896:] = stats[rows]
    copies = exchange(1, "grp", lambda peer: qkv_send.at[peer], qkv_recv.at[g])
    started.extend(copies)
    qkv_recv[g] = qkv_send[g]

    row16 = lax.broadcasted_iota(jnp.int32, (GROWS, HEAD_DIM), 0)
    lane16 = lax.broadcasted_iota(jnp.int32, (GROWS, HEAD_DIM), 1)
    position = row16 % STEPS
    for r in range(REQ_GRP):
        length = lengths[group_perm[g * REQ_GRP + r]]
        position = position + jnp.where(row16 // STEPS == r, length, 0)
    half = HEAD_DIM // 2
    exponent = (lane16 % half).astype(f32) * (2.0 / HEAD_DIM)
    angle = position.astype(f32) * jnp.exp(-exponent * jnp.log(jnp.full((), ROPE_BASE, f32)))
    cosine = jnp.cos(angle)
    sine = jnp.where(lane16 < half, -jnp.sin(angle), jnp.sin(angle))

    arrive(copies)
    summed = sum(qkv_recv[i].astype(f32) for i in range(N_GRP))
    scale = lax.rsqrt(jnp.sum(summed[:, 896:], axis=1, keepdims=True) / D + EPSILON)
    share = summed[:, :896] * scale + qkv_bias[...].reshape(1, 896)
    per_dev = 896 // HEAD_DIM
    for j in range(per_dev):
        unit = share[:, j * HEAD_DIM : (j + 1) * HEAD_DIM]
        turned = unit * cosine + pltpu.roll(unit, half, 1) * sine
        unit = jnp.where(s * per_dev + j < HEADS + KV_HEADS, turned, unit)
        heads_all[s, :, j * HEAD_DIM : (j + 1) * HEAD_DIM] = unit.astype(bf16)
    q_pairs[...] = jnp.zeros_like(q_pairs)
    gather_seq(2, heads_all)

    def head(h):
        lane = (h % per_dev) * HEAD_DIM
        return heads_all[h // per_dev, :, lane : lane + HEAD_DIM]

    n_q = REQ_GRP * QROWS
    spread_row = lax.broadcasted_iota(jnp.int32, (n_q, GROUP_Q * GROWS), 0)
    spread_col = lax.broadcasted_iota(jnp.int32, (n_q, GROUP_Q * GROWS), 1)
    spread = (
        (spread_row // QROWS == spread_col % GROWS // STEPS)
        & (spread_row % QROWS // STEPS == spread_col // GROWS)
        & (spread_row % STEPS == spread_col % STEPS)
    ).astype(f32).astype(bf16)
    for k in range(KV_HEADS):
        stacked = jnp.concatenate([head(k * GROUP_Q + j) for j in range(GROUP_Q)], axis=0)
        placed = jnp.dot(spread, stacked, preferred_element_type=f32).astype(bf16)
        for r in range(REQ_GRP):
            q_pairs[
                r,
                k // 2,
                (k % 2) * QROWS : (k % 2 + 1) * QROWS,
                (k % 2) * HEAD_DIM : (k % 2 + 1) * HEAD_DIM,
            ] = placed[r * QROWS : (r + 1) * QROWS]
        new_k[:, k * HEAD_DIM : (k + 1) * HEAD_DIM] = head(HEADS + k)
        new_v[:, k * HEAD_DIM : (k + 1) * HEAD_DIM] = head(HEADS + KV_HEADS + k)

    loads[1].wait()
    loads[2].wait()
    score_scale = HEAD_DIM ** (-0.5)
    new_row = lax.broadcasted_iota(jnp.int32, (2 * QROWS, GROWS), 0)
    new_col = lax.broadcasted_iota(jnp.int32, (2 * QROWS, GROWS), 1)
    causal = (new_col % STEPS <= new_row % STEPS) & (s == N_SEQ - 1)
    columns = lax.broadcasted_iota(jnp.int32, (2 * QROWS, SHARD_ROWS), 1)
    contract_last = (((1,), (1,)), ((), ()))

    def attend(r, carry):
        request = group_perm[g * REQ_GRP + r]
        live = columns < lengths[request] - s * SHARD_ROWS
        own = causal & (new_col // STEPS == r)
        slots = [page_table[request, s * SHARD_PAGES + p] for p in range(SHARD_PAGES)]
        for pair in range(KV_HEADS // 2):
            lanes = slice(pair * 256, (pair + 1) * 256)
            query = q_pairs[r, pair]
            keys = jnp.concatenate([k_pool[slot, :, lanes] for slot in slots], axis=0)
            values = jnp.concatenate([v_pool[slot, :, lanes] for slot in slots], axis=0)
            scores = (
                lax.dot_general(query, keys, contract_last, preferred_element_type=f32)
                * score_scale
            )
            scores = jnp.where(live, scores, LOW_SCORE)
            fresh = (
                lax.dot_general(query, new_k[:, lanes], contract_last, preferred_element_type=f32)
                * score_scale
            )
            fresh = jnp.where(own, fresh, LOW_SCORE)
            top = jnp.maximum(
                jnp.max(scores, axis=1, keepdims=True), jnp.max(fresh, axis=1, keepdims=True)
            )
            weights = jnp.where(live, jnp.exp(scores - top), 0.0)
            new_weights = jnp.where(own, jnp.exp(fresh - top), 0.0)
            total = jnp.sum(weights, axis=1, keepdims=True) + jnp.sum(
                new_weights, axis=1, keepdims=True
            )
            weighted = jnp.dot(weights.astype(bf16), values, preferred_element_type=f32) + jnp.dot(
                new_weights.astype(bf16), new_v[:, lanes], preferred_element_type=f32
            )
            block = stat_lanes(split_bf16(top, 3) + split_bf16(total, 2), 2 * QROWS)
            rows = pl.ds(pl.multiple_of(r * QROWS, QROWS), QROWS)
            for k in range(2):
                mine = slice(k * QROWS, (k + 1) * QROWS)
                att_held[2 * pair + k, rows, :HEAD_DIM] = weighted[
                    mine, k * HEAD_DIM : (k + 1) * HEAD_DIM
                ].astype(bf16)
                att_held[2 * pair + k, rows, HEAD_DIM:] = block[mine].astype(bf16)
        return carry

    half_rows = GROWS // 2
    n_out = GROUP_Q * half_rows
    pick_row = lax.broadcasted_iota(jnp.int32, (n_out, n_q // 2), 0)
    pick_col = lax.broadcasted_iota(jnp.int32, (n_out, n_q // 2), 1)
    pick = (
        (pick_col // QROWS == pick_row % half_rows // STEPS)
        & (pick_col % QROWS // STEPS == pick_row // half_rows)
        & (pick_col % STEPS == pick_row % STEPS)
    ).astype(f32).astype(bf16)
    att_copies = []
    for part in range(2):
        lax.fori_loop(2 * part, 2 * part + 2, attend, 0)
        for k in range(KV_HEADS):
            held = att_held[k, part * n_q // 2 : (part + 1) * n_q // 2, :]
            picked = jnp.dot(pick, held, preferred_element_type=f32)
            below = picked[:half_rows, HEAD_DIM:]
            for j in range(1, GROUP_Q):
                stat = picked[j * half_rows : (j + 1) * half_rows, HEAD_DIM:]
                below = below + pltpu.roll(stat, 8 * j, 1)
            att_send[part, k] = jnp.concatenate([picked[:, :HEAD_DIM], below], axis=0).astype(bf16)
        copies = exchange(
            (3, 11)[part], "seq", lambda peer: att_send.at[part, peer], att_recv.at[part, s]
        )
        started.extend(copies)
        att_copies.append(copies)
        att_recv[part, s] = att_send[part, s]

    stat_lane = lax.broadcasted_iota(jnp.int32, (half_rows, HEAD_DIM), 1) % 8 == 0
    halves = []
    for part in range(2):
        arrive(att_copies[part])
        blocks = [att_recv[part, i].astype(f32) for i in range(N_SEQ)]
        tops, sums = [], []
        for block in blocks:
            below = block[n_out:]
            shifted = [below] + [pltpu.roll(below, HEAD_DIM - n, 1) for n in range(1, 5)]
            tops.append(jnp.where(stat_lane, shifted[0] + shifted[1] + shifted[2], 0.0))
            sums.append(jnp.where(stat_lane, shifted[3] + shifted[4], 1.0))
        best = functools.reduce(jnp.maximum, tops)
        factors = [jnp.exp(top - best) for top in tops]
        total = sum(factor * part_sum for factor, part_sum in zip(factors, sums))
        joined = []
        for j in range(GROUP_Q):
            rows = slice(j * half_rows, (j + 1) * half_rows)
            weighted = sum(
                factor[:, 8 * j : 8 * j + 1] * block[rows]
                for factor, block in zip(factors, blocks)
            )
            joined.append(weighted / total[:, 8 * j : 8 * j + 1])
        halves.append(joined)
    for j in range(GROUP_Q):
        attended = jnp.concatenate([halves[0][j], halves[1][j]], axis=0)
        att_all[g, :, j * HEAD_DIM : (j + 1) * HEAD_DIM] = attended.astype(bf16)
    copies = exchange(4, "grp", lambda peer: att_all.at[g], att_all.at[g])
    started.extend(copies)
    loads[3].wait()
    arrive(copies)

    feature = lax.broadcasted_iota(jnp.int32, (ROWS, FEAT_PAD), 1) < FEAT

    def scatter_features(stage, rows, weight, send, recv):
        def copy_of(i, source):
            return pltpu.make_async_remote_copy(
                src_ref=send.at[i],
                dst_ref=recv.at[source],
                send_sem=send_sem.at[stage, i],
                recv_sem=recv_sem.at[stage, source],
                device_id={"seq": i},
                device_id_type=MESH,
            )

        parts = [
            (((0, 384), (896, DEPTH)), (0, 7, 1, 6)),
            (((384, 896),), (2, 5, 3, 4)),
        ]
        for pieces, peers in parts:
            for begin, end in pieces:
                wide[:, begin:end] = jnp.dot(
                    rows, weight[:, begin:end], preferred_element_type=f32
                )
            for i in peers:
                first = i * FEAT // 128 * 128
                window = wide[:, first : first + 384]
                if i * FEAT - first:
                    window = pltpu.roll(window, 384 - (i * FEAT - first), 1)
                send[i] = pack(jnp.where(feature, window[:, :FEAT_PAD], 0.0), 4)

                @pl.when(s != i)
                def _(i=i):
                    copy_of(i, s).start()

        recv[s] = send[s]
        for i in range(N_SEQ):

            @pl.when(s != i)
            def _(i=i):
                copy_of(i, i).wait_recv()
                copy_of(i, i).wait_send()

        return unpack(sum(recv[i].astype(f32) for i in range(N_SEQ)), 4)

    columns_in = jnp.concatenate([att_all[i] for i in range(N_GRP)], axis=0)
    attn_sum = scatter_features(5, columns_in, w_o, o_send, o_recv)
    residual = sorted_rows + attn_sum
    mid_all[s] = feature_block(residual, gains[1:2, :])
    squares_mid = gather_features(6, mid_all)

    stats = stat_lanes(split_bf16(squares_mid, 2), ROWS).astype(bf16)
    for i in range(N_GRP):
        gate_send[i, :, 1792:] = stats[i * GROWS : (i + 1) * GROWS]

    def project(weight, send):
        def ff_tile(c, carry):
            first = pl.multiple_of(c * 256, 256)
            tile = lax.dot_general(
                x_bf[...], weight[pl.ds(first, 256), :], contract_last, preferred_element_type=f32
            ).astype(bf16)
            for i in range(N_GRP):
                send[i, :, pl.ds(first, 256)] = tile[i * GROWS : (i + 1) * GROWS]
            return carry

        lax.fori_loop(0, 6, ff_tile, 0)
        tile = lax.dot_general(
            x_bf[...], weight[1536:1728, :], contract_last, preferred_element_type=f32
        )
        tile = jnp.concatenate([tile, jnp.zeros((ROWS, 64), f32)], axis=1).astype(bf16)
        for i in range(N_GRP):
            send[i, :, 1536:1792] = tile[i * GROWS : (i + 1) * GROWS]

    loads[4].wait()
    project(w_gate, gate_send)
    gate_copies = exchange(7, "grp", lambda peer: gate_send.at[peer], gate_recv.at[g])
    started.extend(gate_copies)
    loads[5].wait()
    project(w_up, up_send)
    up_copies = exchange(10, "grp", lambda peer: up_send.at[peer], up_recv.at[g])
    started.extend(up_copies)
    gate_recv[g] = gate_send[g]
    up_recv[g] = up_send[g]
    arrive(gate_copies)
    stat = sum(gate_recv[i, :, 1792:].astype(f32) for i in range(N_GRP))
    scale = lax.rsqrt(jnp.sum(stat, axis=1, keepdims=True) / D + EPSILON)
    gate = sum(gate_recv[i, :, :1792].astype(f32) for i in range(N_GRP)) * scale
    gate = gate / (1.0 + jnp.exp(-gate))
    arrive(up_copies)
    up = sum(up_recv[i].astype(f32) for i in range(N_GRP)) * scale
    hid_all[g] = (gate * up).astype(bf16)
    copies = exchange(8, "grp", lambda peer: hid_all.at[g], hid_all.at[g])
    started.extend(copies)
    loads[6].wait()
    arrive(copies)

    hidden = jnp.concatenate([hid_all[i, :, :1728] for i in range(N_GRP)], axis=0)
    down_sum = scatter_features(9, hidden, w_down, down_send, down_recv)
    final = (residual + down_sum).astype(bf16)
    row_i = lax.broadcasted_iota(jnp.int32, (ROWS, ROWS), 0)
    col_i = lax.broadcasted_iota(jnp.int32, (ROWS, ROWS), 1)
    origin = jnp.zeros((ROWS, ROWS), jnp.int32)
    for i in range(ROWS // STEPS):
        origin = jnp.where(col_i // STEPS == i, group_perm[i], origin)
    back = (
        ((row_i // STEPS) == origin) & ((col_i % STEPS) == (row_i % STEPS))
    ).astype(f32).astype(bf16)
    ordered = jnp.dot(back, final, preferred_element_type=f32)
    for i in range(ROWS // STEPS):
        out[i] = ordered[i * STEPS : (i + 1) * STEPS, :FEAT].astype(bf16)
    for copy in started:
        copy.wait_send()


def fused_body(
    tokens,
    lengths,
    group_perm,
    page_table,
    k_pool,
    v_pool,
    gain_in,
    qkv_weight,
    qkv_bias,
    o_weight,
    gain_mid,
    gate_weight,
    up_weight,
    down_weight,
):
    gains = [gain.reshape(1, FEAT) for gain in (gain_in, gain_mid)]
    gate_rows, up_rows = gate_weight.T, up_weight.T
    smem = pl.BlockSpec(memory_space=pltpu.SMEM)
    vmem = pl.BlockSpec(memory_space=pltpu.VMEM)
    hbm = pl.BlockSpec(memory_space=pl.ANY)
    bf16, f32 = jnp.bfloat16, jnp.float32
    return pl.pallas_call(
        fused_kernel,
        out_shape=jax.ShapeDtypeStruct(tokens.shape, bf16),
        in_specs=[smem] * 3 + [vmem] * 4 + [hbm] * 7,
        out_specs=vmem,
        scratch_shapes=[
            pltpu.VMEM(k_pool.shape, bf16),
            pltpu.VMEM(v_pool.shape, bf16),
            pltpu.VMEM(qkv_weight.shape, bf16),
            pltpu.VMEM(o_weight.shape, bf16),
            pltpu.VMEM(gate_rows.shape, bf16),
            pltpu.VMEM(up_rows.shape, bf16),
            pltpu.VMEM(down_weight.shape, bf16),
            pltpu.VMEM((N_SEQ, 96, 128), bf16),
            pltpu.VMEM((ROWS, DEPTH + 128), f32),
            pltpu.VMEM((ROWS, DEPTH), bf16),
            pltpu.VMEM((N_GRP, GROWS, 1024), bf16),
            pltpu.VMEM((N_GRP, GROWS, 1024), bf16),
            pltpu.VMEM((N_SEQ, GROWS, 896), bf16),
            pltpu.VMEM((REQ_GRP, KV_HEADS // 2, 2 * QROWS, 256), bf16),
            pltpu.VMEM((GROWS, KV_HEADS * HEAD_DIM), bf16),
            pltpu.VMEM((GROWS, KV_HEADS * HEAD_DIM), bf16),
            pltpu.VMEM((N_SEQ, REQ_GRP * QROWS, 2 * HEAD_DIM), bf16),
            pltpu.VMEM((2, N_SEQ, 48, 128), bf16),
            pltpu.VMEM((2, N_SEQ, 48, 128), bf16),
            pltpu.VMEM((N_GRP, GROWS, GROUP_Q * HEAD_DIM), bf16),
            pltpu.VMEM((ROWS, DEPTH + 128), f32),
            pltpu.VMEM((N_SEQ, 80, 128), bf16),
            pltpu.VMEM((N_SEQ, 80, 128), bf16),
            pltpu.VMEM((N_SEQ, 96, 128), bf16),
            pltpu.VMEM((N_GRP, GROWS, 1920), bf16),
            pltpu.VMEM((N_GRP, GROWS, 1920), bf16),
            pltpu.VMEM((N_GRP, GROWS, 1792), bf16),
            pltpu.VMEM((N_GRP, GROWS, 1792), bf16),
            pltpu.VMEM((N_GRP, GROWS, 1792), bf16),
            pltpu.VMEM((N_SEQ, 80, 128), bf16),
            pltpu.VMEM((N_SEQ, 80, 128), bf16),
            pltpu.VMEM((ROWS, FEAT_PAD), f32),
            pltpu.VMEM((8, FEAT_PAD), f32),
            pltpu.SemaphoreType.DMA((7,)),
            pltpu.SemaphoreType.DMA((12, N_SEQ)),
            pltpu.SemaphoreType.DMA((12, N_SEQ)),
        ],
        compiler_params=pltpu.CompilerParams(
            collective_id=0, has_side_effects=True, vmem_limit_bytes=56 * 2**20
        ),
    )(
        lengths,
        group_perm,
        page_table,
        tokens,
        gains[0],
        qkv_bias,
        gains[1],
        k_pool,
        v_pool,
        qkv_weight,
        o_weight,
        gate_rows,
        up_rows,
        down_weight,
    )


def solution(mesh):
    fused = mesh.shape["seq"] == KV_HEADS and mesh.shape["grp"] == N_GRP
    return jax.shard_map(
        fused_body if fused else body,
        mesh=mesh,
        in_specs=(
            P(None, None, ("grp", "seq")),
            P(),
            P(),
            P(),
            P(("grp", "seq"), None, None),
            P(("grp", "seq"), None, None),
            P(("grp", "seq")),
            P("grp", "seq"),
            P("seq"),
            P("seq", "grp"),
            P(("grp", "seq")),
            P("grp", "seq"),
            P("grp", "seq"),
            P("seq", "grp"),
        ),
        out_specs=P(None, None, ("grp", "seq")),
        check_vma=False,
    )
```

```python
import functools

import jax
import jax.numpy as jnp
from jax import lax
from jax.experimental import pallas as pl
from jax.experimental.pallas import tpu as pltpu
from jax.sharding import PartitionSpec as P

D = 5120
HEADS = 40
KV_HEADS = 8
HEAD_DIM = 128
STEPS = 4
REQ_GRP = 4
SHARD_PAGES = 8
PAGE = 128
BLOCK_PAGES = 4


EPSILON = 1e-06
LOW_SCORE = -1e30
ROPE_BASE = 1000000.0


def rotary(values, position):
    half_dim = values.shape[-1] // 2
    exponent = jnp.arange(half_dim, dtype=jnp.float32) * (2.0 / values.shape[-1])
    inverse = jnp.exp(-exponent * jnp.log(jnp.float32(ROPE_BASE)))
    angle = position[..., None, None] * inverse
    cosine = jnp.cos(angle)
    sine_part = jnp.sin(angle)
    first_half = values[..., :half_dim]
    second_half = values[..., half_dim:]
    return jnp.concatenate(
        [
            first_half * cosine - second_half * sine_part,
            second_half * cosine + first_half * sine_part,
        ],
        axis=-1,
    )


def absorb(carried, query_mat, key_block, value_block, live_mask, score_scale):
    best_score, weight_sums, weighted = carried
    scores = (
        jnp.einsum("hqd,khd->hqk", query_mat, key_block, preferred_element_type=jnp.float32)
        * score_scale
    )
    scores = jnp.where(live_mask, scores, LOW_SCORE)
    fresh_top = jnp.maximum(best_score, jnp.max(scores, axis=-1))
    rescale = jnp.exp(best_score - fresh_top)
    weights = jnp.where(live_mask, jnp.exp(scores - fresh_top[..., None]), 0.0)
    weight_sums = weight_sums * rescale + jnp.sum(weights, axis=-1)
    weighted = weighted * rescale[..., None] + jnp.einsum(
        "hqk,khd->hqd",
        weights.astype(jnp.bfloat16),
        value_block,
        preferred_element_type=jnp.float32,
    )
    return (fresh_top, weight_sums, weighted)


def body(
    tokens,
    lengths,
    group_perm,
    page_table,
    k_pool,
    v_pool,
    gain_in,
    qkv_weight,
    qkv_bias,
    o_weight,
    gain_mid,
    gate_weight,
    up_weight,
    down_weight,
):
    n_seq = lax.axis_size("seq")
    grp_idx = lax.axis_index("grp")
    seq_idx = lax.axis_index("seq")
    group_q = HEADS // KV_HEADS
    query_rows = STEPS * group_q
    q_width = HEADS * HEAD_DIM
    kv_width = KV_HEADS * HEAD_DIM
    score_scale = HEAD_DIM ** (-0.5)
    sorted_rows = jnp.take(tokens, group_perm, axis=0).astype(jnp.float32)
    squares_in = lax.psum(jnp.sum(sorted_rows * sorted_rows, axis=-1), ("grp", "seq"))
    normed_in = (sorted_rows * lax.rsqrt(squares_in / D + EPSILON)[..., None] * gain_in).astype(
        jnp.bfloat16
    )
    proj_part = jnp.einsum(
        "rtc,ck->rtk",
        lax.all_gather(normed_in, "seq", axis=2, tiled=True),
        qkv_weight,
        preferred_element_type=jnp.float32,
    )
    proj_share = (
        lax.psum_scatter(
            proj_part.astype(jnp.bfloat16), "grp", scatter_dimension=0, tiled=True
        ).astype(jnp.float32)
        + qkv_bias
    )
    proj_full = lax.all_gather(proj_share, "seq", axis=2, tiled=True)
    members = lax.dynamic_slice_in_dim(group_perm, grp_idx * REQ_GRP, REQ_GRP)
    my_lengths = jnp.take(lengths, members)
    steps_range = jnp.arange(STEPS, dtype=jnp.int32)
    position = (my_lengths[:, None] + steps_range[None, :]).astype(jnp.float32)
    queries = rotary(
        proj_full[..., :q_width].reshape(REQ_GRP, STEPS, HEADS, HEAD_DIM), position
    ).astype(jnp.bfloat16)
    new_keys = rotary(
        proj_full[..., q_width : q_width + kv_width].reshape(REQ_GRP, STEPS, KV_HEADS, HEAD_DIM),
        position,
    ).astype(jnp.bfloat16)
    new_values = (
        proj_full[..., q_width + kv_width :]
        .reshape(REQ_GRP, STEPS, KV_HEADS, HEAD_DIM)
        .astype(jnp.bfloat16)
    )
    shard_rows = SHARD_PAGES * PAGE
    block_rows = BLOCK_PAGES * PAGE
    shard_base = seq_idx * shard_rows
    slot_table = lax.dynamic_slice_in_dim(
        jnp.take(page_table, members, axis=0), seq_idx * SHARD_PAGES, SHARD_PAGES, 1
    )
    is_last = seq_idx == n_seq - 1
    causal = (
        steps_range[None, :] <= (jnp.arange(query_rows, dtype=jnp.int32) // group_q)[:, None]
    ) & is_last
    causal = causal[None]
    query_all = (
        queries.reshape(REQ_GRP, STEPS, KV_HEADS, group_q, HEAD_DIM)
        .transpose(0, 2, 1, 3, 4)
        .reshape(REQ_GRP, KV_HEADS, query_rows, HEAD_DIM)
    )
    live_all = jnp.clip(my_lengths - shard_base, 0, shard_rows)
    block_offsets = jnp.arange(block_rows, dtype=jnp.int32)
    initial = (
        jnp.full((REQ_GRP, KV_HEADS, query_rows), LOW_SCORE, jnp.float32),
        jnp.zeros((REQ_GRP, KV_HEADS, query_rows), jnp.float32),
        jnp.zeros((REQ_GRP, KV_HEADS, query_rows, HEAD_DIM), jnp.float32),
    )
    absorb_all = jax.vmap(absorb, in_axes=(0, 0, 0, 0, None, None))
    carried = absorb_all(initial, query_all, new_keys, new_values, causal, score_scale)
    absorb_masked = jax.vmap(absorb, in_axes=(0, 0, 0, 0, 0, None))
    block_count = (jnp.max(live_all) + block_rows - 1) // block_rows

    def advance_all(block_index, running):
        slot_ids = lax.dynamic_slice_in_dim(slot_table, block_index * BLOCK_PAGES, BLOCK_PAGES, 1)
        key_block = jnp.take(k_pool, slot_ids.reshape(-1), axis=0).reshape(
            REQ_GRP, block_rows, KV_HEADS, HEAD_DIM
        )
        value_block = jnp.take(v_pool, slot_ids.reshape(-1), axis=0).reshape(
            REQ_GRP, block_rows, KV_HEADS, HEAD_DIM
        )
        positions = shard_base + block_index * block_rows + block_offsets
        live_mask = (positions[None, :] < my_lengths[:, None])[:, None, None, :]
        return absorb_masked(running, query_all, key_block, value_block, live_mask, score_scale)

    best_score, weight_sums, weighted = lax.fori_loop(0, block_count, advance_all, carried)
    top_score = lax.pmax(best_score, "seq")
    factor = jnp.exp(best_score - top_score)
    weight_sums, weighted = (
        lax.psum((weight_sums * factor).astype(jnp.bfloat16), "seq").astype(jnp.float32),
        lax.psum((weighted * factor[..., None]).astype(jnp.bfloat16), "seq").astype(jnp.float32),
    )
    attended = (weighted / weight_sums[..., None]).reshape(
        REQ_GRP, KV_HEADS, STEPS, group_q, HEAD_DIM
    )
    attended = (
        attended.transpose(0, 2, 1, 3, 4).reshape(REQ_GRP, STEPS, q_width).astype(jnp.bfloat16)
    )
    out_width = o_weight.shape[0]
    attended_cols = lax.dynamic_slice_in_dim(attended, seq_idx * out_width, out_width, 2)
    out_terms = jnp.einsum(
        "rtc,cd->rtd",
        lax.all_gather(attended_cols, "grp", axis=0, tiled=True),
        o_weight,
        preferred_element_type=jnp.float32,
    )
    attn_sum = lax.psum_scatter(
        out_terms.astype(jnp.bfloat16), "seq", scatter_dimension=2, tiled=True
    ).astype(jnp.float32)
    residual = sorted_rows + attn_sum
    squares_mid = lax.psum(jnp.sum(residual * residual, axis=-1), ("grp", "seq"))
    normed_mid = (residual * lax.rsqrt(squares_mid / D + EPSILON)[..., None] * gain_mid).astype(
        jnp.bfloat16
    )
    segment = lax.all_gather(normed_mid, "seq", axis=2, tiled=True)
    gate_part = jnp.einsum("rtc,cf->rtf", segment, gate_weight, preferred_element_type=jnp.float32)
    up_part = jnp.einsum("rtc,cf->rtf", segment, up_weight, preferred_element_type=jnp.float32)
    gate_sum, up_sum = (
        lax.psum(gate_part.astype(jnp.bfloat16), "grp").astype(jnp.float32),
        lax.psum(up_part.astype(jnp.bfloat16), "grp").astype(jnp.float32),
    )
    hidden = (jax.nn.silu(gate_sum) * up_sum).astype(jnp.bfloat16)
    down_terms = jnp.einsum("rtf,fd->rtd", hidden, down_weight, preferred_element_type=jnp.float32)
    down_sum = lax.psum_scatter(
        down_terms.astype(jnp.bfloat16), "seq", scatter_dimension=2, tiled=True
    ).astype(jnp.float32)
    restore = jnp.argsort(group_perm)
    return jnp.take(residual + down_sum, restore, axis=0).astype(jnp.bfloat16)


N_GRP = 4
N_SEQ = 8
ROWS = 64
GROWS = REQ_GRP * STEPS
FEAT = D // (N_GRP * N_SEQ)
FEAT_PAD = 256
DEPTH = D // N_GRP
GROUP_Q = HEADS // KV_HEADS
QROWS = 32
SHARD_ROWS = SHARD_PAGES * PAGE
MESH = pl.DeviceIdType.MESH


def stat_lanes(pieces, rows, at=0, width=128, base=None):
    lane = lax.broadcasted_iota(jnp.int32, (rows, width), 1)
    block = jnp.zeros((rows, width), jnp.float32) if base is None else base
    for offset, piece in enumerate(pieces):
        block = jnp.where(lane == at + offset, piece, block)
    return block


def split_bf16(value, count):
    pieces = []
    for _ in range(count):
        piece = value.astype(jnp.bfloat16).astype(jnp.float32)
        pieces.append(piece)
        value = value - piece
    return pieces


def pack(values, parts):
    rows, width = ROWS // parts, 128 // parts
    rest = values[:, 128:]
    below = rest[:rows]
    for a in range(1, parts):
        below = below + pltpu.roll(rest[a * rows : (a + 1) * rows], a * width, 1)
    return jnp.concatenate([values[:, :128], below], axis=0).astype(jnp.bfloat16)


def unpack(block, parts):
    rows, width = ROWS // parts, 128 // parts
    below = block[ROWS:]
    lane = lax.broadcasted_iota(jnp.int32, (rows, 128), 1)
    rest = [
        jnp.where(lane < width, pltpu.roll(below, 128 - a * width, 1) if a else below, 0.0)
        for a in range(parts)
    ]
    return jnp.concatenate([block[:ROWS], jnp.concatenate(rest, axis=0)], axis=1)


def fused_kernel(
    lengths,
    group_perm,
    page_table,
    tokens,
    gain_in,
    qkv_bias,
    gain_mid,
    k_hbm,
    v_hbm,
    qkv_hbm,
    o_hbm,
    gate_hbm,
    up_hbm,
    down_hbm,
    out,
    k_pool,
    v_pool,
    w_qkv,
    w_o,
    w_gate,
    w_up,
    w_down,
    x_all,
    x_wide,
    x_bf,
    qkv_send,
    qkv_recv,
    heads_all,
    q_pairs,
    new_k,
    new_v,
    att_held,
    att_send,
    att_recv,
    att_all,
    wide,
    o_send,
    o_recv,
    mid_all,
    ff_send,
    ff_recv,
    hid_all,
    down_send,
    down_recv,
    padded,
    gains,
    load_sem,
    send_sem,
    recv_sem,
):
    g = lax.axis_index("grp")
    s = lax.axis_index("seq")
    f32, bf16 = jnp.float32, jnp.bfloat16

    loads = [
        pltpu.make_async_copy(src, dst, load_sem.at[i])
        for i, (src, dst) in enumerate(
            [
                (qkv_hbm, w_qkv),
                (k_hbm, k_pool),
                (v_hbm, v_pool),
                (o_hbm, w_o),
                (gate_hbm, w_gate),
                (up_hbm, w_up),
                (down_hbm, w_down),
            ]
        )
    ]
    for load in loads:
        load.start()
    barrier = pltpu.get_barrier_semaphore()
    for d in range(1, N_SEQ):
        pl.semaphore_signal(
            barrier, inc=1, device_id={"seq": lax.rem(s + d, N_SEQ)}, device_id_type=MESH
        )
    for d in range(1, N_GRP):
        pl.semaphore_signal(
            barrier, inc=1, device_id={"grp": lax.rem(g + d, N_GRP)}, device_id_type=MESH
        )

    def exchange(stage, axis, source, target):
        me, count = (s, N_SEQ) if axis == "seq" else (g, N_GRP)
        copies = []
        for d in range(1, count):
            peer = lax.rem(me + d, count)
            copy = pltpu.make_async_remote_copy(
                src_ref=source(peer),
                dst_ref=target,
                send_sem=send_sem.at[stage, d],
                recv_sem=recv_sem.at[stage, d],
                device_id={axis: peer},
                device_id_type=MESH,
            )
            copy.start()
            copies.append(copy)
        return copies

    def arrive(copies):
        for copy in copies:
            copy.wait_recv()

    started = []

    padded[...] = jnp.zeros_like(padded)
    wide[...] = jnp.zeros_like(wide)
    for i in range(ROWS // STEPS):
        padded[i * STEPS : (i + 1) * STEPS, :FEAT] = tokens[group_perm[i]].astype(f32)
    gains[...] = jnp.zeros_like(gains)
    gains[0:1, :FEAT] = gain_in[...]
    gains[1:2, :FEAT] = gain_mid[...]
    sorted_rows = padded[...]

    def feature_block(values, gain):
        squares = jnp.sum(values * values, axis=1, keepdims=True)
        return pack(
            stat_lanes(split_bf16(squares, 2), ROWS, FEAT, FEAT_PAD, values * gain), 2
        )

    x_all[s] = feature_block(sorted_rows, gains[0:1, :])
    pl.semaphore_wait(barrier, N_SEQ + N_GRP - 2)

    def gather_features(stage, blocks):
        copies = exchange(stage, "seq", lambda peer: blocks.at[s], blocks.at[s])
        started.extend(copies)
        arrive(copies)
        lane = lax.broadcasted_iota(jnp.int32, (ROWS, FEAT_PAD), 1)
        x_wide[...] = jnp.zeros_like(x_wide)
        squares = jnp.zeros((ROWS, 1), f32)
        for i in range(N_SEQ):
            block = unpack(blocks[i].astype(f32), 2)
            kept = jnp.where(lane < FEAT, block, 0.0)
            squares = squares + jnp.sum(block - kept, axis=1, keepdims=True)
            first = i * FEAT // 128 * 128
            kept = jnp.concatenate([kept, jnp.zeros((ROWS, 128), f32)], axis=1)
            if i * FEAT - first:
                kept = pltpu.roll(kept, i * FEAT - first, 1)
            x_wide[:, first : first + 384] += kept
        x_bf[...] = x_wide[:, :DEPTH].astype(bf16)
        return squares

    squares_in = gather_features(0, x_all)

    loads[0].wait()
    part = jnp.dot(x_bf[...], w_qkv[...], preferred_element_type=f32).astype(bf16)
    stats = stat_lanes(split_bf16(squares_in, 2), ROWS).astype(bf16)
    for i in range(N_GRP):
        rows = slice(i * GROWS, (i + 1) * GROWS)
        qkv_send[i, :, :896] = part[rows]
        qkv_send[i, :, 896:] = stats[rows]
    copies = exchange(1, "grp", lambda peer: qkv_send.at[peer], qkv_recv.at[g])
    started.extend(copies)
    qkv_recv[g] = qkv_send[g]

    row16 = lax.broadcasted_iota(jnp.int32, (GROWS, HEAD_DIM), 0)
    lane16 = lax.broadcasted_iota(jnp.int32, (GROWS, HEAD_DIM), 1)
    position = row16 % STEPS
    for r in range(REQ_GRP):
        length = lengths[group_perm[g * REQ_GRP + r]]
        position = position + jnp.where(row16 // STEPS == r, length, 0)
    half = HEAD_DIM // 2
    exponent = (lane16 % half).astype(f32) * (2.0 / HEAD_DIM)
    angle = position.astype(f32) * jnp.exp(-exponent * jnp.log(jnp.full((), ROPE_BASE, f32)))
    cosine = jnp.cos(angle)
    sine = jnp.where(lane16 < half, -jnp.sin(angle), jnp.sin(angle))

    arrive(copies)
    summed = sum(qkv_recv[i].astype(f32) for i in range(N_GRP))
    scale = lax.rsqrt(jnp.sum(summed[:, 896:], axis=1, keepdims=True) / D + EPSILON)
    share = summed[:, :896] * scale + qkv_bias[...].reshape(1, 896)
    per_dev = 896 // HEAD_DIM
    for j in range(per_dev):
        unit = share[:, j * HEAD_DIM : (j + 1) * HEAD_DIM]
        turned = unit * cosine + pltpu.roll(unit, half, 1) * sine
        unit = jnp.where(s * per_dev + j < HEADS + KV_HEADS, turned, unit)
        heads_all[s, :, j * HEAD_DIM : (j + 1) * HEAD_DIM] = unit.astype(bf16)
    copies = exchange(2, "seq", lambda peer: heads_all.at[s], heads_all.at[s])
    started.extend(copies)
    q_pairs[...] = jnp.zeros_like(q_pairs)
    arrive(copies)

    def head(h):
        lane = (h % per_dev) * HEAD_DIM
        return heads_all[h // per_dev, :, lane : lane + HEAD_DIM]

    n_q = REQ_GRP * QROWS
    spread_row = lax.broadcasted_iota(jnp.int32, (n_q, GROUP_Q * GROWS), 0)
    spread_col = lax.broadcasted_iota(jnp.int32, (n_q, GROUP_Q * GROWS), 1)
    spread = (
        (spread_row // QROWS == spread_col % GROWS // STEPS)
        & (spread_row % QROWS // STEPS == spread_col // GROWS)
        & (spread_row % STEPS == spread_col % STEPS)
    ).astype(f32).astype(bf16)
    for k in range(KV_HEADS):
        stacked = jnp.concatenate([head(k * GROUP_Q + j) for j in range(GROUP_Q)], axis=0)
        placed = jnp.dot(spread, stacked, preferred_element_type=f32).astype(bf16)
        for r in range(REQ_GRP):
            q_pairs[
                r,
                k // 2,
                (k % 2) * QROWS : (k % 2 + 1) * QROWS,
                (k % 2) * HEAD_DIM : (k % 2 + 1) * HEAD_DIM,
            ] = placed[r * QROWS : (r + 1) * QROWS]
        new_k[:, k * HEAD_DIM : (k + 1) * HEAD_DIM] = head(HEADS + k)
        new_v[:, k * HEAD_DIM : (k + 1) * HEAD_DIM] = head(HEADS + KV_HEADS + k)

    loads[1].wait()
    loads[2].wait()
    score_scale = HEAD_DIM ** (-0.5)
    new_row = lax.broadcasted_iota(jnp.int32, (2 * QROWS, GROWS), 0)
    new_col = lax.broadcasted_iota(jnp.int32, (2 * QROWS, GROWS), 1)
    causal = (new_col % STEPS <= new_row % STEPS) & (s == N_SEQ - 1)
    columns = lax.broadcasted_iota(jnp.int32, (2 * QROWS, SHARD_ROWS), 1)
    contract_last = (((1,), (1,)), ((), ()))

    def attend(r, carry):
        request = group_perm[g * REQ_GRP + r]
        live = columns < lengths[request] - s * SHARD_ROWS
        own = causal & (new_col // STEPS == r)
        slots = [page_table[request, s * SHARD_PAGES + p] for p in range(SHARD_PAGES)]
        for pair in range(KV_HEADS // 2):
            lanes = slice(pair * 256, (pair + 1) * 256)
            query = q_pairs[r, pair]
            keys = jnp.concatenate([k_pool[slot, :, lanes] for slot in slots], axis=0)
            values = jnp.concatenate([v_pool[slot, :, lanes] for slot in slots], axis=0)
            scores = (
                lax.dot_general(query, keys, contract_last, preferred_element_type=f32)
                * score_scale
            )
            scores = jnp.where(live, scores, LOW_SCORE)
            fresh = (
                lax.dot_general(query, new_k[:, lanes], contract_last, preferred_element_type=f32)
                * score_scale
            )
            fresh = jnp.where(own, fresh, LOW_SCORE)
            top = jnp.maximum(
                jnp.max(scores, axis=1, keepdims=True), jnp.max(fresh, axis=1, keepdims=True)
            )
            weights = jnp.where(live, jnp.exp(scores - top), 0.0)
            new_weights = jnp.where(own, jnp.exp(fresh - top), 0.0)
            total = jnp.sum(weights, axis=1, keepdims=True) + jnp.sum(
                new_weights, axis=1, keepdims=True
            )
            weighted = jnp.dot(weights.astype(bf16), values, preferred_element_type=f32) + jnp.dot(
                new_weights.astype(bf16), new_v[:, lanes], preferred_element_type=f32
            )
            block = stat_lanes(split_bf16(top, 3) + split_bf16(total, 2), 2 * QROWS)
            rows = pl.ds(pl.multiple_of(r * QROWS, QROWS), QROWS)
            for k in range(2):
                mine = slice(k * QROWS, (k + 1) * QROWS)
                att_held[2 * pair + k, rows, :HEAD_DIM] = weighted[
                    mine, k * HEAD_DIM : (k + 1) * HEAD_DIM
                ].astype(bf16)
                att_held[2 * pair + k, rows, HEAD_DIM:] = block[mine].astype(bf16)
        return carry

    lax.fori_loop(0, REQ_GRP, attend, 0)
    pick_row = lax.broadcasted_iota(jnp.int32, (GROUP_Q * GROWS, n_q), 0)
    pick_col = lax.broadcasted_iota(jnp.int32, (GROUP_Q * GROWS, n_q), 1)
    pick = (
        (pick_col // QROWS == pick_row % GROWS // STEPS)
        & (pick_col % QROWS // STEPS == pick_row // GROWS)
        & (pick_col % STEPS == pick_row % STEPS)
    ).astype(f32).astype(bf16)
    n_out = GROUP_Q * GROWS
    for k in range(KV_HEADS):
        picked = jnp.dot(pick, att_held[k], preferred_element_type=f32)
        below = picked[:GROWS, HEAD_DIM:]
        for j in range(1, GROUP_Q):
            below = below + pltpu.roll(picked[j * GROWS : (j + 1) * GROWS, HEAD_DIM:], 8 * j, 1)
        att_send[k, :n_out] = picked[:, :HEAD_DIM].astype(bf16)
        att_send[k, n_out:] = below.astype(bf16)
    copies = exchange(3, "seq", lambda peer: att_send.at[peer], att_recv.at[s])
    started.extend(copies)
    att_recv[s] = att_send[s]
    arrive(copies)

    stat_lane = lax.broadcasted_iota(jnp.int32, (GROWS, HEAD_DIM), 1) % 8 == 0
    tops, sums = [], []
    for i in range(N_SEQ):
        block = att_recv[i, n_out:, :].astype(f32)
        shifted = [block] + [pltpu.roll(block, HEAD_DIM - n, 1) for n in range(1, 5)]
        tops.append(jnp.where(stat_lane, shifted[0] + shifted[1] + shifted[2], 0.0))
        sums.append(jnp.where(stat_lane, shifted[3] + shifted[4], 1.0))
    best = functools.reduce(jnp.maximum, tops)
    factors = [jnp.exp(top - best) for top in tops]
    total = sum(factor * part_sum for factor, part_sum in zip(factors, sums))
    for j in range(GROUP_Q):
        rows = slice(j * GROWS, (j + 1) * GROWS)
        weighted = sum(
            factors[i][:, 8 * j : 8 * j + 1] * att_recv[i, rows, :].astype(f32)
            for i in range(N_SEQ)
        )
        attended = weighted / total[:, 8 * j : 8 * j + 1]
        att_all[g, :, j * HEAD_DIM : (j + 1) * HEAD_DIM] = attended.astype(bf16)
    copies = exchange(4, "grp", lambda peer: att_all.at[g], att_all.at[g])
    started.extend(copies)
    loads[3].wait()
    arrive(copies)

    feature = lax.broadcasted_iota(jnp.int32, (ROWS, FEAT_PAD), 1) < FEAT

    def scatter_features(stage, rows, weight, send, recv):
        def copy_of(i, source):
            return pltpu.make_async_remote_copy(
                src_ref=send.at[i],
                dst_ref=recv.at[source],
                send_sem=send_sem.at[stage, i],
                recv_sem=recv_sem.at[stage, source],
                device_id={"seq": i},
                device_id_type=MESH,
            )

        depth = weight.shape[0] // len(rows)
        parts = [
            (((0, 384), (896, DEPTH)), (0, 7, 1, 6)),
            (((384, 896),), (2, 5, 3, 4)),
        ]
        for pieces, peers in parts:
            for begin, end in pieces:
                wide[:, begin:end] = sum(
                    jnp.dot(rows[n], weight[n * depth : (n + 1) * depth, begin:end],
                            preferred_element_type=f32)
                    for n in range(len(rows))
                )
            for i in peers:
                first = i * FEAT // 128 * 128
                window = wide[:, first : first + 384]
                if i * FEAT - first:
                    window = pltpu.roll(window, 384 - (i * FEAT - first), 1)
                send[i] = pack(jnp.where(feature, window[:, :FEAT_PAD], 0.0), 4)

                @pl.when(s != i)
                def _(i=i):
                    copy_of(i, s).start()

        recv[s] = send[s]
        for i in range(N_SEQ):

            @pl.when(s != i)
            def _(i=i):
                copy_of(i, i).wait_recv()
                copy_of(i, i).wait_send()

        return unpack(sum(recv[i].astype(f32) for i in range(N_SEQ)), 4)

    columns_in = jnp.concatenate([att_all[i] for i in range(N_GRP)], axis=0)
    attn_sum = scatter_features(5, [columns_in], w_o, o_send, o_recv)
    residual = sorted_rows + attn_sum
    mid_all[s] = feature_block(residual, gains[1:2, :])
    squares_mid = gather_features(6, mid_all)

    stats = stat_lanes(split_bf16(squares_mid, 2), ROWS)
    stats = jnp.concatenate([stats, stats], axis=0).T[:16].astype(bf16)
    wide_x = x_wide[:, :DEPTH]
    gate_x = jnp.concatenate([wide_x, jnp.zeros_like(wide_x)], axis=0).T
    up_x = pltpu.roll(gate_x, ROWS, 1).astype(bf16)
    gate_x = gate_x.astype(bf16)
    units = w_gate.shape[0] // N_GRP
    loads[4].wait()
    loads[5].wait()
    copies = []
    for d in (2, 3, 1, 0):
        peer = lax.rem(g + d, N_GRP)
        rows = pl.ds(pl.multiple_of(peer * units, 16), units)
        part = jnp.dot(w_gate[rows, :], gate_x, preferred_element_type=f32) + jnp.dot(
            w_up[rows, :], up_x, preferred_element_type=f32
        )
        ff_send[peer, :units] = part.astype(bf16)
        ff_send[peer, units:] = stats
        if d:
            copy = pltpu.make_async_remote_copy(
                src_ref=ff_send.at[peer],
                dst_ref=ff_recv.at[g],
                send_sem=send_sem.at[7, d],
                recv_sem=recv_sem.at[7, d],
                device_id={"grp": peer},
                device_id_type=MESH,
            )
            copy.start()
            copies.append(copy)
    started.extend(copies)
    ff_recv[g] = ff_send[g]
    arrive(copies)
    summed = sum(ff_recv[i].astype(f32) for i in range(N_GRP))
    scale = lax.rsqrt((summed[units : units + 1] + summed[units + 1 : units + 2]) / D + EPSILON)
    summed = summed[:units] * scale
    hidden = summed / (1.0 + jnp.exp(-summed)) * pltpu.roll(summed, ROWS, 1)
    hidden = jnp.concatenate([hidden, jnp.zeros((512 - units, 128), f32)], axis=0)
    hid_all[g] = hidden.T[:ROWS].astype(bf16)
    copies = exchange(8, "grp", lambda peer: hid_all.at[g], hid_all.at[g])
    started.extend(copies)
    loads[6].wait()
    arrive(copies)
    hidden = [hid_all[i, :, :units] for i in range(N_GRP)]
    down_sum = scatter_features(9, hidden, w_down, down_send, down_recv)
    final = (residual + down_sum).astype(bf16)
    row_i = lax.broadcasted_iota(jnp.int32, (ROWS, ROWS), 0)
    col_i = lax.broadcasted_iota(jnp.int32, (ROWS, ROWS), 1)
    origin = jnp.zeros((ROWS, ROWS), jnp.int32)
    for i in range(ROWS // STEPS):
        origin = jnp.where(col_i // STEPS == i, group_perm[i], origin)
    back = (
        ((row_i // STEPS) == origin) & ((col_i % STEPS) == (row_i % STEPS))
    ).astype(f32).astype(bf16)
    ordered = jnp.dot(back, final, preferred_element_type=f32)
    for i in range(ROWS // STEPS):
        out[i] = ordered[i * STEPS : (i + 1) * STEPS, :FEAT].astype(bf16)
    for copy in started:
        copy.wait_send()


def fused_body(
    tokens,
    lengths,
    group_perm,
    page_table,
    k_pool,
    v_pool,
    gain_in,
    qkv_weight,
    qkv_bias,
    o_weight,
    gain_mid,
    gate_weight,
    up_weight,
    down_weight,
):
    gains = [gain.reshape(1, FEAT) for gain in (gain_in, gain_mid)]
    gate_rows, up_rows = gate_weight.T, up_weight.T
    smem = pl.BlockSpec(memory_space=pltpu.SMEM)
    vmem = pl.BlockSpec(memory_space=pltpu.VMEM)
    hbm = pl.BlockSpec(memory_space=pl.ANY)
    bf16, f32 = jnp.bfloat16, jnp.float32
    return pl.pallas_call(
        fused_kernel,
        out_shape=jax.ShapeDtypeStruct(tokens.shape, bf16),
        in_specs=[smem] * 3 + [vmem] * 4 + [hbm] * 7,
        out_specs=vmem,
        scratch_shapes=[
            pltpu.VMEM(k_pool.shape, bf16),
            pltpu.VMEM(v_pool.shape, bf16),
            pltpu.VMEM(qkv_weight.shape, bf16),
            pltpu.VMEM(o_weight.shape, bf16),
            pltpu.VMEM(gate_rows.shape, bf16),
            pltpu.VMEM(up_rows.shape, bf16),
            pltpu.VMEM(down_weight.shape, bf16),
            pltpu.VMEM((N_SEQ, 96, 128), bf16),
            pltpu.VMEM((ROWS, DEPTH + 128), f32),
            pltpu.VMEM((ROWS, DEPTH), bf16),
            pltpu.VMEM((N_GRP, GROWS, 1024), bf16),
            pltpu.VMEM((N_GRP, GROWS, 1024), bf16),
            pltpu.VMEM((N_SEQ, GROWS, 896), bf16),
            pltpu.VMEM((REQ_GRP, KV_HEADS // 2, 2 * QROWS, 256), bf16),
            pltpu.VMEM((GROWS, KV_HEADS * HEAD_DIM), bf16),
            pltpu.VMEM((GROWS, KV_HEADS * HEAD_DIM), bf16),
            pltpu.VMEM((N_SEQ, REQ_GRP * QROWS, 2 * HEAD_DIM), bf16),
            pltpu.VMEM((N_SEQ, 96, 128), bf16),
            pltpu.VMEM((N_SEQ, 96, 128), bf16),
            pltpu.VMEM((N_GRP, GROWS, GROUP_Q * HEAD_DIM), bf16),
            pltpu.VMEM((ROWS, DEPTH + 128), f32),
            pltpu.VMEM((N_SEQ, 80, 128), bf16),
            pltpu.VMEM((N_SEQ, 80, 128), bf16),
            pltpu.VMEM((N_SEQ, 96, 128), bf16),
            pltpu.VMEM((N_GRP, gate_rows.shape[0] // N_GRP + 16, 128), bf16),
            pltpu.VMEM((N_GRP, gate_rows.shape[0] // N_GRP + 16, 128), bf16),
            pltpu.VMEM((N_GRP, ROWS, 512), bf16),
            pltpu.VMEM((N_SEQ, 80, 128), bf16),
            pltpu.VMEM((N_SEQ, 80, 128), bf16),
            pltpu.VMEM((ROWS, FEAT_PAD), f32),
            pltpu.VMEM((8, FEAT_PAD), f32),
            pltpu.SemaphoreType.DMA((7,)),
            pltpu.SemaphoreType.DMA((11, N_SEQ)),
            pltpu.SemaphoreType.DMA((11, N_SEQ)),
        ],
        compiler_params=pltpu.CompilerParams(
            collective_id=0, has_side_effects=True, vmem_limit_bytes=56 * 2**20
        ),
    )(
        lengths,
        group_perm,
        page_table,
        tokens,
        gains[0],
        qkv_bias,
        gains[1],
        k_pool,
        v_pool,
        qkv_weight,
        o_weight,
        gate_rows,
        up_rows,
        down_weight,
    )


def solution(mesh):
    fused = mesh.shape["seq"] == KV_HEADS and mesh.shape["grp"] == N_GRP
    return jax.shard_map(
        fused_body if fused else body,
        mesh=mesh,
        in_specs=(
            P(None, None, ("grp", "seq")),
            P(),
            P(),
            P(),
            P(("grp", "seq"), None, None),
            P(("grp", "seq"), None, None),
            P(("grp", "seq")),
            P("grp", "seq"),
            P("seq"),
            P("seq", "grp"),
            P(("grp", "seq")),
            P("grp", "seq"),
            P("grp", "seq"),
            P("seq", "grp"),
        ),
        out_specs=P(None, None, ("grp", "seq")),
        check_vma=False,
    )
```

```python
import functools

import jax
import jax.numpy as jnp
from jax import lax
from jax.experimental import pallas as pl
from jax.experimental.pallas import tpu as pltpu
from jax.sharding import PartitionSpec as P

D = 5120
HEADS = 40
KV_HEADS = 8
HEAD_DIM = 128
STEPS = 4
REQ_GRP = 4
SHARD_PAGES = 8
PAGE = 128
BLOCK_PAGES = 4


EPSILON = 1e-06
LOW_SCORE = -1e30
ROPE_BASE = 1000000.0


def rotary(values, position):
    half_dim = values.shape[-1] // 2
    exponent = jnp.arange(half_dim, dtype=jnp.float32) * (2.0 / values.shape[-1])
    inverse = jnp.exp(-exponent * jnp.log(jnp.float32(ROPE_BASE)))
    angle = position[..., None, None] * inverse
    cosine = jnp.cos(angle)
    sine_part = jnp.sin(angle)
    first_half = values[..., :half_dim]
    second_half = values[..., half_dim:]
    return jnp.concatenate(
        [
            first_half * cosine - second_half * sine_part,
            second_half * cosine + first_half * sine_part,
        ],
        axis=-1,
    )


def absorb(carried, query_mat, key_block, value_block, live_mask, score_scale):
    best_score, weight_sums, weighted = carried
    scores = (
        jnp.einsum("hqd,khd->hqk", query_mat, key_block, preferred_element_type=jnp.float32)
        * score_scale
    )
    scores = jnp.where(live_mask, scores, LOW_SCORE)
    fresh_top = jnp.maximum(best_score, jnp.max(scores, axis=-1))
    rescale = jnp.exp(best_score - fresh_top)
    weights = jnp.where(live_mask, jnp.exp(scores - fresh_top[..., None]), 0.0)
    weight_sums = weight_sums * rescale + jnp.sum(weights, axis=-1)
    weighted = weighted * rescale[..., None] + jnp.einsum(
        "hqk,khd->hqd",
        weights.astype(jnp.bfloat16),
        value_block,
        preferred_element_type=jnp.float32,
    )
    return (fresh_top, weight_sums, weighted)


def body(
    tokens,
    lengths,
    group_perm,
    page_table,
    k_pool,
    v_pool,
    gain_in,
    qkv_weight,
    qkv_bias,
    o_weight,
    gain_mid,
    gate_weight,
    up_weight,
    down_weight,
):
    n_seq = lax.axis_size("seq")
    grp_idx = lax.axis_index("grp")
    seq_idx = lax.axis_index("seq")
    group_q = HEADS // KV_HEADS
    query_rows = STEPS * group_q
    q_width = HEADS * HEAD_DIM
    kv_width = KV_HEADS * HEAD_DIM
    score_scale = HEAD_DIM ** (-0.5)
    sorted_rows = jnp.take(tokens, group_perm, axis=0).astype(jnp.float32)
    squares_in = lax.psum(jnp.sum(sorted_rows * sorted_rows, axis=-1), ("grp", "seq"))
    normed_in = (sorted_rows * lax.rsqrt(squares_in / D + EPSILON)[..., None] * gain_in).astype(
        jnp.bfloat16
    )
    proj_part = jnp.einsum(
        "rtc,ck->rtk",
        lax.all_gather(normed_in, "seq", axis=2, tiled=True),
        qkv_weight,
        preferred_element_type=jnp.float32,
    )
    proj_share = (
        lax.psum_scatter(
            proj_part.astype(jnp.bfloat16), "grp", scatter_dimension=0, tiled=True
        ).astype(jnp.float32)
        + qkv_bias
    )
    proj_full = lax.all_gather(proj_share, "seq", axis=2, tiled=True)
    members = lax.dynamic_slice_in_dim(group_perm, grp_idx * REQ_GRP, REQ_GRP)
    my_lengths = jnp.take(lengths, members)
    steps_range = jnp.arange(STEPS, dtype=jnp.int32)
    position = (my_lengths[:, None] + steps_range[None, :]).astype(jnp.float32)
    queries = rotary(
        proj_full[..., :q_width].reshape(REQ_GRP, STEPS, HEADS, HEAD_DIM), position
    ).astype(jnp.bfloat16)
    new_keys = rotary(
        proj_full[..., q_width : q_width + kv_width].reshape(REQ_GRP, STEPS, KV_HEADS, HEAD_DIM),
        position,
    ).astype(jnp.bfloat16)
    new_values = (
        proj_full[..., q_width + kv_width :]
        .reshape(REQ_GRP, STEPS, KV_HEADS, HEAD_DIM)
        .astype(jnp.bfloat16)
    )
    shard_rows = SHARD_PAGES * PAGE
    block_rows = BLOCK_PAGES * PAGE
    shard_base = seq_idx * shard_rows
    slot_table = lax.dynamic_slice_in_dim(
        jnp.take(page_table, members, axis=0), seq_idx * SHARD_PAGES, SHARD_PAGES, 1
    )
    is_last = seq_idx == n_seq - 1
    causal = (
        steps_range[None, :] <= (jnp.arange(query_rows, dtype=jnp.int32) // group_q)[:, None]
    ) & is_last
    causal = causal[None]
    query_all = (
        queries.reshape(REQ_GRP, STEPS, KV_HEADS, group_q, HEAD_DIM)
        .transpose(0, 2, 1, 3, 4)
        .reshape(REQ_GRP, KV_HEADS, query_rows, HEAD_DIM)
    )
    live_all = jnp.clip(my_lengths - shard_base, 0, shard_rows)
    block_offsets = jnp.arange(block_rows, dtype=jnp.int32)
    initial = (
        jnp.full((REQ_GRP, KV_HEADS, query_rows), LOW_SCORE, jnp.float32),
        jnp.zeros((REQ_GRP, KV_HEADS, query_rows), jnp.float32),
        jnp.zeros((REQ_GRP, KV_HEADS, query_rows, HEAD_DIM), jnp.float32),
    )
    absorb_all = jax.vmap(absorb, in_axes=(0, 0, 0, 0, None, None))
    carried = absorb_all(initial, query_all, new_keys, new_values, causal, score_scale)
    absorb_masked = jax.vmap(absorb, in_axes=(0, 0, 0, 0, 0, None))
    block_count = (jnp.max(live_all) + block_rows - 1) // block_rows

    def advance_all(block_index, running):
        slot_ids = lax.dynamic_slice_in_dim(slot_table, block_index * BLOCK_PAGES, BLOCK_PAGES, 1)
        key_block = jnp.take(k_pool, slot_ids.reshape(-1), axis=0).reshape(
            REQ_GRP, block_rows, KV_HEADS, HEAD_DIM
        )
        value_block = jnp.take(v_pool, slot_ids.reshape(-1), axis=0).reshape(
            REQ_GRP, block_rows, KV_HEADS, HEAD_DIM
        )
        positions = shard_base + block_index * block_rows + block_offsets
        live_mask = (positions[None, :] < my_lengths[:, None])[:, None, None, :]
        return absorb_masked(running, query_all, key_block, value_block, live_mask, score_scale)

    best_score, weight_sums, weighted = lax.fori_loop(0, block_count, advance_all, carried)
    top_score = lax.pmax(best_score, "seq")
    factor = jnp.exp(best_score - top_score)
    weight_sums, weighted = (
        lax.psum((weight_sums * factor).astype(jnp.bfloat16), "seq").astype(jnp.float32),
        lax.psum((weighted * factor[..., None]).astype(jnp.bfloat16), "seq").astype(jnp.float32),
    )
    attended = (weighted / weight_sums[..., None]).reshape(
        REQ_GRP, KV_HEADS, STEPS, group_q, HEAD_DIM
    )
    attended = (
        attended.transpose(0, 2, 1, 3, 4).reshape(REQ_GRP, STEPS, q_width).astype(jnp.bfloat16)
    )
    out_width = o_weight.shape[0]
    attended_cols = lax.dynamic_slice_in_dim(attended, seq_idx * out_width, out_width, 2)
    out_terms = jnp.einsum(
        "rtc,cd->rtd",
        lax.all_gather(attended_cols, "grp", axis=0, tiled=True),
        o_weight,
        preferred_element_type=jnp.float32,
    )
    attn_sum = lax.psum_scatter(
        out_terms.astype(jnp.bfloat16), "seq", scatter_dimension=2, tiled=True
    ).astype(jnp.float32)
    residual = sorted_rows + attn_sum
    squares_mid = lax.psum(jnp.sum(residual * residual, axis=-1), ("grp", "seq"))
    normed_mid = (residual * lax.rsqrt(squares_mid / D + EPSILON)[..., None] * gain_mid).astype(
        jnp.bfloat16
    )
    segment = lax.all_gather(normed_mid, "seq", axis=2, tiled=True)
    gate_part = jnp.einsum("rtc,cf->rtf", segment, gate_weight, preferred_element_type=jnp.float32)
    up_part = jnp.einsum("rtc,cf->rtf", segment, up_weight, preferred_element_type=jnp.float32)
    gate_sum, up_sum = (
        lax.psum(gate_part.astype(jnp.bfloat16), "grp").astype(jnp.float32),
        lax.psum(up_part.astype(jnp.bfloat16), "grp").astype(jnp.float32),
    )
    hidden = (jax.nn.silu(gate_sum) * up_sum).astype(jnp.bfloat16)
    down_terms = jnp.einsum("rtf,fd->rtd", hidden, down_weight, preferred_element_type=jnp.float32)
    down_sum = lax.psum_scatter(
        down_terms.astype(jnp.bfloat16), "seq", scatter_dimension=2, tiled=True
    ).astype(jnp.float32)
    restore = jnp.argsort(group_perm)
    return jnp.take(residual + down_sum, restore, axis=0).astype(jnp.bfloat16)


N_GRP = 4
N_SEQ = 8
ROWS = 64
GROWS = REQ_GRP * STEPS
FEAT = D // (N_GRP * N_SEQ)
FEAT_PAD = 256
DEPTH = D // N_GRP
GROUP_Q = HEADS // KV_HEADS
QROWS = 32
SHARD_ROWS = SHARD_PAGES * PAGE
MESH = pl.DeviceIdType.MESH


def stat_lanes(pieces, rows, at=0, width=128, base=None):
    lane = lax.broadcasted_iota(jnp.int32, (rows, width), 1)
    block = jnp.zeros((rows, width), jnp.float32) if base is None else base
    for offset, piece in enumerate(pieces):
        block = jnp.where(lane == at + offset, piece, block)
    return block


def split_bf16(value, count):
    pieces = []
    for _ in range(count):
        piece = value.astype(jnp.bfloat16).astype(jnp.float32)
        pieces.append(piece)
        value = value - piece
    return pieces


def pack(values, parts):
    rows, width = ROWS // parts, 128 // parts
    rest = values[:, 128:]
    below = rest[:rows]
    for a in range(1, parts):
        below = below + pltpu.roll(rest[a * rows : (a + 1) * rows], a * width, 1)
    return jnp.concatenate([values[:, :128], below], axis=0).astype(jnp.bfloat16)


def unpack(block, parts):
    rows, width = ROWS // parts, 128 // parts
    below = block[ROWS:]
    lane = lax.broadcasted_iota(jnp.int32, (rows, 128), 1)
    rest = [
        jnp.where(lane < width, pltpu.roll(below, 128 - a * width, 1) if a else below, 0.0)
        for a in range(parts)
    ]
    return jnp.concatenate([block[:ROWS], jnp.concatenate(rest, axis=0)], axis=1)


def fused_kernel(
    lengths,
    group_perm,
    page_table,
    tokens,
    gain_in,
    qkv_bias,
    gain_mid,
    k_hbm,
    v_hbm,
    qkv_hbm,
    o_hbm,
    gate_hbm,
    up_hbm,
    down_hbm,
    out,
    k_pool,
    v_pool,
    w_qkv,
    w_o,
    w_gate,
    w_up,
    w_down,
    x_all,
    x_wide,
    x_bf,
    qkv_send,
    qkv_recv,
    heads_all,
    q_pairs,
    new_k,
    new_v,
    att_held,
    att_send,
    att_recv,
    att_all,
    wide,
    o_send,
    o_recv,
    mid_all,
    ff_send,
    ff_recv,
    hid_all,
    down_send,
    down_recv,
    padded,
    gains,
    load_sem,
    send_sem,
    recv_sem,
):
    g = lax.axis_index("grp")
    s = lax.axis_index("seq")
    f32, bf16 = jnp.float32, jnp.bfloat16

    loads = [
        pltpu.make_async_copy(src, dst, load_sem.at[i])
        for i, (src, dst) in enumerate(
            [
                (qkv_hbm, w_qkv),
                (k_hbm, k_pool),
                (v_hbm, v_pool),
                (o_hbm, w_o),
                (gate_hbm, w_gate),
                (up_hbm, w_up),
                (down_hbm, w_down),
            ]
        )
    ]
    loads[0].start()
    barrier = pltpu.get_barrier_semaphore()
    for d in range(1, N_SEQ):
        pl.semaphore_signal(
            barrier, inc=1, device_id={"seq": lax.rem(s + d, N_SEQ)}, device_id_type=MESH
        )
    for d in range(1, N_GRP):
        pl.semaphore_signal(
            barrier, inc=1, device_id={"grp": lax.rem(g + d, N_GRP)}, device_id_type=MESH
        )

    def exchange(stage, axis, source, target):
        me, count = (s, N_SEQ) if axis == "seq" else (g, N_GRP)
        copies = []
        for d in range(1, count):
            peer = lax.rem(me + d, count)
            copy = pltpu.make_async_remote_copy(
                src_ref=source(peer),
                dst_ref=target,
                send_sem=send_sem.at[stage, d],
                recv_sem=recv_sem.at[stage, d],
                device_id={axis: peer},
                device_id_type=MESH,
            )
            copy.start()
            copies.append(copy)
        return copies

    def arrive(copies):
        for copy in copies:
            copy.wait_recv()

    started = []

    padded[...] = jnp.zeros_like(padded)
    wide[...] = jnp.zeros_like(wide)
    for i in range(ROWS // STEPS):
        padded[i * STEPS : (i + 1) * STEPS, :FEAT] = tokens[group_perm[i]].astype(f32)
    gains[...] = jnp.zeros_like(gains)
    gains[0:1, :FEAT] = gain_in[...]
    gains[1:2, :FEAT] = gain_mid[...]
    sorted_rows = padded[...]

    def feature_block(values, gain):
        squares = jnp.sum(values * values, axis=1, keepdims=True)
        return pack(
            stat_lanes(split_bf16(squares, 2), ROWS, FEAT, FEAT_PAD, values * gain), 2
        )

    x_all[s] = feature_block(sorted_rows, gains[0:1, :])
    pl.semaphore_wait(barrier, N_SEQ + N_GRP - 2)

    def gather_features(stage, blocks):
        copies = exchange(stage, "seq", lambda peer: blocks.at[s], blocks.at[s])
        started.extend(copies)
        if stage == 0:
            loads[1].start()
        arrive(copies)
        lane = lax.broadcasted_iota(jnp.int32, (ROWS, FEAT_PAD), 1)
        x_wide[...] = jnp.zeros_like(x_wide)
        squares = jnp.zeros((ROWS, 1), f32)
        for i in range(N_SEQ):
            block = unpack(blocks[i].astype(f32), 2)
            kept = jnp.where(lane < FEAT, block, 0.0)
            squares = squares + jnp.sum(block - kept, axis=1, keepdims=True)
            first = i * FEAT // 128 * 128
            kept = jnp.concatenate([kept, jnp.zeros((ROWS, 128), f32)], axis=1)
            if i * FEAT - first:
                kept = pltpu.roll(kept, i * FEAT - first, 1)
            x_wide[:, first : first + 384] += kept
        x_bf[...] = x_wide[:, :DEPTH].astype(bf16)
        return squares

    squares_in = gather_features(0, x_all)

    loads[0].wait()
    part = jnp.dot(x_bf[...], w_qkv[...], preferred_element_type=f32).astype(bf16)
    stats = stat_lanes(split_bf16(squares_in, 2), ROWS).astype(bf16)
    for i in range(N_GRP):
        rows = slice(i * GROWS, (i + 1) * GROWS)
        qkv_send[i, :, :896] = part[rows]
        qkv_send[i, :, 896:] = stats[rows]
    copies = exchange(1, "grp", lambda peer: qkv_send.at[peer], qkv_recv.at[g])
    started.extend(copies)
    for load in loads[2:]:
        load.start()
    qkv_recv[g] = qkv_send[g]

    row16 = lax.broadcasted_iota(jnp.int32, (GROWS, HEAD_DIM), 0)
    lane16 = lax.broadcasted_iota(jnp.int32, (GROWS, HEAD_DIM), 1)
    position = row16 % STEPS
    for r in range(REQ_GRP):
        length = lengths[group_perm[g * REQ_GRP + r]]
        position = position + jnp.where(row16 // STEPS == r, length, 0)
    half = HEAD_DIM // 2
    exponent = (lane16 % half).astype(f32) * (2.0 / HEAD_DIM)
    angle = position.astype(f32) * jnp.exp(-exponent * jnp.log(jnp.full((), ROPE_BASE, f32)))
    cosine = jnp.cos(angle)
    sine = jnp.where(lane16 < half, -jnp.sin(angle), jnp.sin(angle))

    arrive(copies)
    summed = sum(qkv_recv[i].astype(f32) for i in range(N_GRP))
    scale = lax.rsqrt(jnp.sum(summed[:, 896:], axis=1, keepdims=True) / D + EPSILON)
    share = summed[:, :896] * scale + qkv_bias[...].reshape(1, 896)
    per_dev = 896 // HEAD_DIM
    for j in range(per_dev):
        unit = share[:, j * HEAD_DIM : (j + 1) * HEAD_DIM]
        turned = unit * cosine + pltpu.roll(unit, half, 1) * sine
        unit = jnp.where(s * per_dev + j < HEADS + KV_HEADS, turned, unit)
        heads_all[s, :, j * HEAD_DIM : (j + 1) * HEAD_DIM] = unit.astype(bf16)
    copies = exchange(2, "seq", lambda peer: heads_all.at[s], heads_all.at[s])
    started.extend(copies)
    q_pairs[...] = jnp.zeros_like(q_pairs)
    arrive(copies)

    def head(h):
        lane = (h % per_dev) * HEAD_DIM
        return heads_all[h // per_dev, :, lane : lane + HEAD_DIM]

    n_q = REQ_GRP * QROWS
    spread_row = lax.broadcasted_iota(jnp.int32, (n_q, GROUP_Q * GROWS), 0)
    spread_col = lax.broadcasted_iota(jnp.int32, (n_q, GROUP_Q * GROWS), 1)
    spread = (
        (spread_row // QROWS == spread_col % GROWS // STEPS)
        & (spread_row % QROWS // STEPS == spread_col // GROWS)
        & (spread_row % STEPS == spread_col % STEPS)
    ).astype(f32).astype(bf16)
    for k in range(KV_HEADS):
        stacked = jnp.concatenate([head(k * GROUP_Q + j) for j in range(GROUP_Q)], axis=0)
        placed = jnp.dot(spread, stacked, preferred_element_type=f32).astype(bf16)
        for r in range(REQ_GRP):
            q_pairs[
                r,
                k // 2,
                (k % 2) * QROWS : (k % 2 + 1) * QROWS,
                (k % 2) * HEAD_DIM : (k % 2 + 1) * HEAD_DIM,
            ] = placed[r * QROWS : (r + 1) * QROWS]
        new_k[:, k * HEAD_DIM : (k + 1) * HEAD_DIM] = head(HEADS + k)
        new_v[:, k * HEAD_DIM : (k + 1) * HEAD_DIM] = head(HEADS + KV_HEADS + k)

    loads[1].wait()
    loads[2].wait()
    score_scale = HEAD_DIM ** (-0.5)
    new_row = lax.broadcasted_iota(jnp.int32, (2 * QROWS, GROWS), 0)
    new_col = lax.broadcasted_iota(jnp.int32, (2 * QROWS, GROWS), 1)
    causal = (new_col % STEPS <= new_row % STEPS) & (s == N_SEQ - 1)
    columns = lax.broadcasted_iota(jnp.int32, (2 * QROWS, SHARD_ROWS), 1)
    contract_last = (((1,), (1,)), ((), ()))

    def attend(r, carry):
        request = group_perm[g * REQ_GRP + r]
        live = columns < lengths[request] - s * SHARD_ROWS
        own = causal & (new_col // STEPS == r)
        slots = [page_table[request, s * SHARD_PAGES + p] for p in range(SHARD_PAGES)]
        for pair in range(KV_HEADS // 2):
            lanes = slice(pair * 256, (pair + 1) * 256)
            query = q_pairs[r, pair]
            keys = jnp.concatenate([k_pool[slot, :, lanes] for slot in slots], axis=0)
            values = jnp.concatenate([v_pool[slot, :, lanes] for slot in slots], axis=0)
            scores = (
                lax.dot_general(query, keys, contract_last, preferred_element_type=f32)
                * score_scale
            )
            scores = jnp.where(live, scores, LOW_SCORE)
            fresh = (
                lax.dot_general(query, new_k[:, lanes], contract_last, preferred_element_type=f32)
                * score_scale
            )
            fresh = jnp.where(own, fresh, LOW_SCORE)
            top = jnp.maximum(
                jnp.max(scores, axis=1, keepdims=True), jnp.max(fresh, axis=1, keepdims=True)
            )
            weights = jnp.where(live, jnp.exp(scores - top), 0.0)
            new_weights = jnp.where(own, jnp.exp(fresh - top), 0.0)
            total = jnp.sum(weights, axis=1, keepdims=True) + jnp.sum(
                new_weights, axis=1, keepdims=True
            )
            weighted = jnp.dot(weights.astype(bf16), values, preferred_element_type=f32) + jnp.dot(
                new_weights.astype(bf16), new_v[:, lanes], preferred_element_type=f32
            )
            block = stat_lanes(split_bf16(top, 3) + split_bf16(total, 2), 2 * QROWS)
            rows = pl.ds(pl.multiple_of(r * QROWS, QROWS), QROWS)
            for k in range(2):
                mine = slice(k * QROWS, (k + 1) * QROWS)
                att_held[2 * pair + k, rows, :HEAD_DIM] = weighted[
                    mine, k * HEAD_DIM : (k + 1) * HEAD_DIM
                ].astype(bf16)
                att_held[2 * pair + k, rows, HEAD_DIM:] = block[mine].astype(bf16)
        return carry

    lax.fori_loop(0, REQ_GRP, attend, 0)
    pick_row = lax.broadcasted_iota(jnp.int32, (GROUP_Q * GROWS, n_q), 0)
    pick_col = lax.broadcasted_iota(jnp.int32, (GROUP_Q * GROWS, n_q), 1)
    pick = (
        (pick_col // QROWS == pick_row % GROWS // STEPS)
        & (pick_col % QROWS // STEPS == pick_row // GROWS)
        & (pick_col % STEPS == pick_row % STEPS)
    ).astype(f32).astype(bf16)
    n_out = GROUP_Q * GROWS
    for k in range(KV_HEADS):
        picked = jnp.dot(pick, att_held[k], preferred_element_type=f32)
        below = picked[:GROWS, HEAD_DIM:]
        for j in range(1, GROUP_Q):
            below = below + pltpu.roll(picked[j * GROWS : (j + 1) * GROWS, HEAD_DIM:], 8 * j, 1)
        att_send[k, :n_out] = picked[:, :HEAD_DIM].astype(bf16)
        att_send[k, n_out:] = below.astype(bf16)
    copies = exchange(3, "seq", lambda peer: att_send.at[peer], att_recv.at[s])
    started.extend(copies)
    att_recv[s] = att_send[s]
    arrive(copies)

    stat_lane = lax.broadcasted_iota(jnp.int32, (GROWS, HEAD_DIM), 1) % 8 == 0
    tops, sums = [], []
    for i in range(N_SEQ):
        block = att_recv[i, n_out:, :].astype(f32)
        shifted = [block] + [pltpu.roll(block, HEAD_DIM - n, 1) for n in range(1, 5)]
        tops.append(jnp.where(stat_lane, shifted[0] + shifted[1] + shifted[2], 0.0))
        sums.append(jnp.where(stat_lane, shifted[3] + shifted[4], 1.0))
    best = functools.reduce(jnp.maximum, tops)
    factors = [jnp.exp(top - best) for top in tops]
    total = sum(factor * part_sum for factor, part_sum in zip(factors, sums))
    for j in range(GROUP_Q):
        rows = slice(j * GROWS, (j + 1) * GROWS)
        weighted = sum(
            factors[i][:, 8 * j : 8 * j + 1] * att_recv[i, rows, :].astype(f32)
            for i in range(N_SEQ)
        )
        attended = weighted / total[:, 8 * j : 8 * j + 1]
        att_all[g, :, j * HEAD_DIM : (j + 1) * HEAD_DIM] = attended.astype(bf16)
    copies = exchange(4, "grp", lambda peer: att_all.at[g], att_all.at[g])
    started.extend(copies)
    loads[3].wait()
    arrive(copies)

    feature = lax.broadcasted_iota(jnp.int32, (ROWS, FEAT_PAD), 1) < FEAT

    def scatter_features(stage, rows, weight, send, recv):
        def copy_of(i, source):
            return pltpu.make_async_remote_copy(
                src_ref=send.at[i],
                dst_ref=recv.at[source],
                send_sem=send_sem.at[stage, i],
                recv_sem=recv_sem.at[stage, source],
                device_id={"seq": i},
                device_id_type=MESH,
            )

        depth = weight.shape[0] // len(rows)

        def tile(c, carry):
            lanes = pl.ds(pl.multiple_of(c * 256, 256), 256)
            wide[:, lanes] = sum(
                jnp.dot(
                    rows[n][...],
                    weight[n * depth : (n + 1) * depth, lanes],
                    preferred_element_type=f32,
                )
                for n in range(len(rows))
            )
            return carry

        lax.fori_loop(0, DEPTH // 256, tile, 0)
        for i in (0, 7, 1, 6, 2, 5, 3, 4):
            first = i * FEAT // 128 * 128
            window = wide[:, first : first + 384]
            if i * FEAT - first:
                window = pltpu.roll(window, 384 - (i * FEAT - first), 1)
            send[i] = pack(jnp.where(feature, window[:, :FEAT_PAD], 0.0), 4)

            @pl.when(s != i)
            def _(i=i):
                copy_of(i, s).start()

        recv[s] = send[s]
        for i in range(N_SEQ):

            @pl.when(s != i)
            def _(i=i):
                copy_of(i, i).wait_recv()
                copy_of(i, i).wait_send()

        return unpack(sum(recv[i].astype(f32) for i in range(N_SEQ)), 4)

    columns_in = jnp.concatenate([att_all[i] for i in range(N_GRP)], axis=0)
    attn_sum = scatter_features(5, [columns_in], w_o, o_send, o_recv)
    residual = sorted_rows + attn_sum
    mid_all[s] = feature_block(residual, gains[1:2, :])
    squares_mid = gather_features(6, mid_all)

    stats = stat_lanes(split_bf16(squares_mid, 2), ROWS)
    stats = jnp.concatenate([stats, stats], axis=0).T[:16].astype(bf16)
    wide_x = x_wide[:, :DEPTH]
    gate_x = jnp.concatenate([wide_x, jnp.zeros_like(wide_x)], axis=0).T
    up_x = pltpu.roll(gate_x, ROWS, 1).astype(bf16)
    gate_x = gate_x.astype(bf16)
    units = w_gate.shape[0] // N_GRP
    loads[4].wait()
    loads[5].wait()

    def ff_copy(d):
        return pltpu.make_async_remote_copy(
            src_ref=ff_send.at[lax.rem(g + d, N_GRP)],
            dst_ref=ff_recv.at[g],
            send_sem=send_sem.at[7, d],
            recv_sem=recv_sem.at[7, d],
            device_id={"grp": lax.rem(g + d, N_GRP)},
            device_id_type=MESH,
        )

    def ff_units(d, carry):
        peer = lax.rem(g + d, N_GRP)
        rows = pl.ds(pl.multiple_of(peer * units, 16), units)
        part = jnp.dot(w_gate[rows, :], gate_x, preferred_element_type=f32) + jnp.dot(
            w_up[rows, :], up_x, preferred_element_type=f32
        )
        ff_send[peer, :units] = part.astype(bf16)
        ff_send[peer, units:] = stats

        @pl.when(d < N_GRP)
        def _():
            ff_copy(d).start()

        return carry

    lax.fori_loop(1, N_GRP + 1, ff_units, 0)
    copies = [ff_copy(d) for d in range(1, N_GRP)]
    started.extend(copies)
    ff_recv[g] = ff_send[g]
    arrive(copies)
    summed = sum(ff_recv[i].astype(f32) for i in range(N_GRP))
    scale = lax.rsqrt((summed[units : units + 1] + summed[units + 1 : units + 2]) / D + EPSILON)
    summed = summed[:units] * scale
    hidden = summed / (1.0 + jnp.exp(-summed)) * pltpu.roll(summed, ROWS, 1)
    hidden = jnp.concatenate([hidden, jnp.zeros((512 - units, 128), f32)], axis=0)
    hid_all[g] = hidden.T[:ROWS].astype(bf16)
    copies = exchange(8, "grp", lambda peer: hid_all.at[g], hid_all.at[g])
    started.extend(copies)
    loads[6].wait()
    arrive(copies)
    hidden = [hid_all[i, :, :units] for i in range(N_GRP)]
    down_sum = scatter_features(9, hidden, w_down, down_send, down_recv)
    final = (residual + down_sum).astype(bf16)
    row_i = lax.broadcasted_iota(jnp.int32, (ROWS, ROWS), 0)
    col_i = lax.broadcasted_iota(jnp.int32, (ROWS, ROWS), 1)
    origin = jnp.zeros((ROWS, ROWS), jnp.int32)
    for i in range(ROWS // STEPS):
        origin = jnp.where(col_i // STEPS == i, group_perm[i], origin)
    back = (
        ((row_i // STEPS) == origin) & ((col_i % STEPS) == (row_i % STEPS))
    ).astype(f32).astype(bf16)
    ordered = jnp.dot(back, final, preferred_element_type=f32)
    for i in range(ROWS // STEPS):
        out[i] = ordered[i * STEPS : (i + 1) * STEPS, :FEAT].astype(bf16)
    for copy in started:
        copy.wait_send()


def fused_body(
    tokens,
    lengths,
    group_perm,
    page_table,
    k_pool,
    v_pool,
    gain_in,
    qkv_weight,
    qkv_bias,
    o_weight,
    gain_mid,
    gate_weight,
    up_weight,
    down_weight,
):
    gains = [gain.reshape(1, FEAT) for gain in (gain_in, gain_mid)]
    gate_rows, up_rows = gate_weight.T, up_weight.T
    smem = pl.BlockSpec(memory_space=pltpu.SMEM)
    vmem = pl.BlockSpec(memory_space=pltpu.VMEM)
    hbm = pl.BlockSpec(memory_space=pl.ANY)
    bf16, f32 = jnp.bfloat16, jnp.float32
    return pl.pallas_call(
        fused_kernel,
        out_shape=jax.ShapeDtypeStruct(tokens.shape, bf16),
        in_specs=[smem] * 3 + [vmem] * 4 + [hbm] * 7,
        out_specs=vmem,
        scratch_shapes=[
            pltpu.VMEM(k_pool.shape, bf16),
            pltpu.VMEM(v_pool.shape, bf16),
            pltpu.VMEM(qkv_weight.shape, bf16),
            pltpu.VMEM(o_weight.shape, bf16),
            pltpu.VMEM(gate_rows.shape, bf16),
            pltpu.VMEM(up_rows.shape, bf16),
            pltpu.VMEM(down_weight.shape, bf16),
            pltpu.VMEM((N_SEQ, 96, 128), bf16),
            pltpu.VMEM((ROWS, DEPTH + 128), f32),
            pltpu.VMEM((ROWS, DEPTH), bf16),
            pltpu.VMEM((N_GRP, GROWS, 1024), bf16),
            pltpu.VMEM((N_GRP, GROWS, 1024), bf16),
            pltpu.VMEM((N_SEQ, GROWS, 896), bf16),
            pltpu.VMEM((REQ_GRP, KV_HEADS // 2, 2 * QROWS, 256), bf16),
            pltpu.VMEM((GROWS, KV_HEADS * HEAD_DIM), bf16),
            pltpu.VMEM((GROWS, KV_HEADS * HEAD_DIM), bf16),
            pltpu.VMEM((N_SEQ, REQ_GRP * QROWS, 2 * HEAD_DIM), bf16),
            pltpu.VMEM((N_SEQ, 96, 128), bf16),
            pltpu.VMEM((N_SEQ, 96, 128), bf16),
            pltpu.VMEM((N_GRP, GROWS, GROUP_Q * HEAD_DIM), bf16),
            pltpu.VMEM((ROWS, DEPTH + 128), f32),
            pltpu.VMEM((N_SEQ, 80, 128), bf16),
            pltpu.VMEM((N_SEQ, 80, 128), bf16),
            pltpu.VMEM((N_SEQ, 96, 128), bf16),
            pltpu.VMEM((N_GRP, gate_rows.shape[0] // N_GRP + 16, 128), bf16),
            pltpu.VMEM((N_GRP, gate_rows.shape[0] // N_GRP + 16, 128), bf16),
            pltpu.VMEM((N_GRP, ROWS, 512), bf16),
            pltpu.VMEM((N_SEQ, 80, 128), bf16),
            pltpu.VMEM((N_SEQ, 80, 128), bf16),
            pltpu.VMEM((ROWS, FEAT_PAD), f32),
            pltpu.VMEM((8, FEAT_PAD), f32),
            pltpu.SemaphoreType.DMA((7,)),
            pltpu.SemaphoreType.DMA((11, N_SEQ)),
            pltpu.SemaphoreType.DMA((11, N_SEQ)),
        ],
        compiler_params=pltpu.CompilerParams(
            collective_id=0, has_side_effects=True, vmem_limit_bytes=56 * 2**20
        ),
    )(
        lengths,
        group_perm,
        page_table,
        tokens,
        gains[0],
        qkv_bias,
        gains[1],
        k_pool,
        v_pool,
        qkv_weight,
        o_weight,
        gate_rows,
        up_rows,
        down_weight,
    )


def solution(mesh):
    fused = mesh.shape["seq"] == KV_HEADS and mesh.shape["grp"] == N_GRP
    return jax.shard_map(
        fused_body if fused else body,
        mesh=mesh,
        in_specs=(
            P(None, None, ("grp", "seq")),
            P(),
            P(),
            P(),
            P(("grp", "seq"), None, None),
            P(("grp", "seq"), None, None),
            P(("grp", "seq")),
            P("grp", "seq"),
            P("seq"),
            P("seq", "grp"),
            P(("grp", "seq")),
            P("grp", "seq"),
            P("grp", "seq"),
            P("seq", "grp"),
        ),
        out_specs=P(None, None, ("grp", "seq")),
        check_vma=False,
    )
```

```python
import functools

import jax
import jax.numpy as jnp
from jax import lax
from jax.experimental import pallas as pl
from jax.experimental.pallas import tpu as pltpu
from jax.sharding import PartitionSpec as P

D = 5120
HEADS = 40
KV_HEADS = 8
HEAD_DIM = 128
STEPS = 4
REQ_GRP = 4
SHARD_PAGES = 8
PAGE = 128
BLOCK_PAGES = 4


EPSILON = 1e-06
LOW_SCORE = -1e30
ROPE_BASE = 1000000.0


def rotary(values, position):
    half_dim = values.shape[-1] // 2
    exponent = jnp.arange(half_dim, dtype=jnp.float32) * (2.0 / values.shape[-1])
    inverse = jnp.exp(-exponent * jnp.log(jnp.float32(ROPE_BASE)))
    angle = position[..., None, None] * inverse
    cosine = jnp.cos(angle)
    sine_part = jnp.sin(angle)
    first_half = values[..., :half_dim]
    second_half = values[..., half_dim:]
    return jnp.concatenate(
        [
            first_half * cosine - second_half * sine_part,
            second_half * cosine + first_half * sine_part,
        ],
        axis=-1,
    )


def absorb(carried, query_mat, key_block, value_block, live_mask, score_scale):
    best_score, weight_sums, weighted = carried
    scores = (
        jnp.einsum("hqd,khd->hqk", query_mat, key_block, preferred_element_type=jnp.float32)
        * score_scale
    )
    scores = jnp.where(live_mask, scores, LOW_SCORE)
    fresh_top = jnp.maximum(best_score, jnp.max(scores, axis=-1))
    rescale = jnp.exp(best_score - fresh_top)
    weights = jnp.where(live_mask, jnp.exp(scores - fresh_top[..., None]), 0.0)
    weight_sums = weight_sums * rescale + jnp.sum(weights, axis=-1)
    weighted = weighted * rescale[..., None] + jnp.einsum(
        "hqk,khd->hqd",
        weights.astype(jnp.bfloat16),
        value_block,
        preferred_element_type=jnp.float32,
    )
    return (fresh_top, weight_sums, weighted)


def body(
    tokens,
    lengths,
    group_perm,
    page_table,
    k_pool,
    v_pool,
    gain_in,
    qkv_weight,
    qkv_bias,
    o_weight,
    gain_mid,
    gate_weight,
    up_weight,
    down_weight,
):
    n_seq = lax.axis_size("seq")
    grp_idx = lax.axis_index("grp")
    seq_idx = lax.axis_index("seq")
    group_q = HEADS // KV_HEADS
    query_rows = STEPS * group_q
    q_width = HEADS * HEAD_DIM
    kv_width = KV_HEADS * HEAD_DIM
    score_scale = HEAD_DIM ** (-0.5)
    sorted_rows = jnp.take(tokens, group_perm, axis=0).astype(jnp.float32)
    squares_in = lax.psum(jnp.sum(sorted_rows * sorted_rows, axis=-1), ("grp", "seq"))
    normed_in = (sorted_rows * lax.rsqrt(squares_in / D + EPSILON)[..., None] * gain_in).astype(
        jnp.bfloat16
    )
    proj_part = jnp.einsum(
        "rtc,ck->rtk",
        lax.all_gather(normed_in, "seq", axis=2, tiled=True),
        qkv_weight,
        preferred_element_type=jnp.float32,
    )
    proj_share = (
        lax.psum_scatter(
            proj_part.astype(jnp.bfloat16), "grp", scatter_dimension=0, tiled=True
        ).astype(jnp.float32)
        + qkv_bias
    )
    proj_full = lax.all_gather(proj_share, "seq", axis=2, tiled=True)
    members = lax.dynamic_slice_in_dim(group_perm, grp_idx * REQ_GRP, REQ_GRP)
    my_lengths = jnp.take(lengths, members)
    steps_range = jnp.arange(STEPS, dtype=jnp.int32)
    position = (my_lengths[:, None] + steps_range[None, :]).astype(jnp.float32)
    queries = rotary(
        proj_full[..., :q_width].reshape(REQ_GRP, STEPS, HEADS, HEAD_DIM), position
    ).astype(jnp.bfloat16)
    new_keys = rotary(
        proj_full[..., q_width : q_width + kv_width].reshape(REQ_GRP, STEPS, KV_HEADS, HEAD_DIM),
        position,
    ).astype(jnp.bfloat16)
    new_values = (
        proj_full[..., q_width + kv_width :]
        .reshape(REQ_GRP, STEPS, KV_HEADS, HEAD_DIM)
        .astype(jnp.bfloat16)
    )
    shard_rows = SHARD_PAGES * PAGE
    block_rows = BLOCK_PAGES * PAGE
    shard_base = seq_idx * shard_rows
    slot_table = lax.dynamic_slice_in_dim(
        jnp.take(page_table, members, axis=0), seq_idx * SHARD_PAGES, SHARD_PAGES, 1
    )
    is_last = seq_idx == n_seq - 1
    causal = (
        steps_range[None, :] <= (jnp.arange(query_rows, dtype=jnp.int32) // group_q)[:, None]
    ) & is_last
    causal = causal[None]
    query_all = (
        queries.reshape(REQ_GRP, STEPS, KV_HEADS, group_q, HEAD_DIM)
        .transpose(0, 2, 1, 3, 4)
        .reshape(REQ_GRP, KV_HEADS, query_rows, HEAD_DIM)
    )
    live_all = jnp.clip(my_lengths - shard_base, 0, shard_rows)
    block_offsets = jnp.arange(block_rows, dtype=jnp.int32)
    initial = (
        jnp.full((REQ_GRP, KV_HEADS, query_rows), LOW_SCORE, jnp.float32),
        jnp.zeros((REQ_GRP, KV_HEADS, query_rows), jnp.float32),
        jnp.zeros((REQ_GRP, KV_HEADS, query_rows, HEAD_DIM), jnp.float32),
    )
    absorb_all = jax.vmap(absorb, in_axes=(0, 0, 0, 0, None, None))
    carried = absorb_all(initial, query_all, new_keys, new_values, causal, score_scale)
    absorb_masked = jax.vmap(absorb, in_axes=(0, 0, 0, 0, 0, None))
    block_count = (jnp.max(live_all) + block_rows - 1) // block_rows

    def advance_all(block_index, running):
        slot_ids = lax.dynamic_slice_in_dim(slot_table, block_index * BLOCK_PAGES, BLOCK_PAGES, 1)
        key_block = jnp.take(k_pool, slot_ids.reshape(-1), axis=0).reshape(
            REQ_GRP, block_rows, KV_HEADS, HEAD_DIM
        )
        value_block = jnp.take(v_pool, slot_ids.reshape(-1), axis=0).reshape(
            REQ_GRP, block_rows, KV_HEADS, HEAD_DIM
        )
        positions = shard_base + block_index * block_rows + block_offsets
        live_mask = (positions[None, :] < my_lengths[:, None])[:, None, None, :]
        return absorb_masked(running, query_all, key_block, value_block, live_mask, score_scale)

    best_score, weight_sums, weighted = lax.fori_loop(0, block_count, advance_all, carried)
    top_score = lax.pmax(best_score, "seq")
    factor = jnp.exp(best_score - top_score)
    weight_sums, weighted = (
        lax.psum((weight_sums * factor).astype(jnp.bfloat16), "seq").astype(jnp.float32),
        lax.psum((weighted * factor[..., None]).astype(jnp.bfloat16), "seq").astype(jnp.float32),
    )
    attended = (weighted / weight_sums[..., None]).reshape(
        REQ_GRP, KV_HEADS, STEPS, group_q, HEAD_DIM
    )
    attended = (
        attended.transpose(0, 2, 1, 3, 4).reshape(REQ_GRP, STEPS, q_width).astype(jnp.bfloat16)
    )
    out_width = o_weight.shape[0]
    attended_cols = lax.dynamic_slice_in_dim(attended, seq_idx * out_width, out_width, 2)
    out_terms = jnp.einsum(
        "rtc,cd->rtd",
        lax.all_gather(attended_cols, "grp", axis=0, tiled=True),
        o_weight,
        preferred_element_type=jnp.float32,
    )
    attn_sum = lax.psum_scatter(
        out_terms.astype(jnp.bfloat16), "seq", scatter_dimension=2, tiled=True
    ).astype(jnp.float32)
    residual = sorted_rows + attn_sum
    squares_mid = lax.psum(jnp.sum(residual * residual, axis=-1), ("grp", "seq"))
    normed_mid = (residual * lax.rsqrt(squares_mid / D + EPSILON)[..., None] * gain_mid).astype(
        jnp.bfloat16
    )
    segment = lax.all_gather(normed_mid, "seq", axis=2, tiled=True)
    gate_part = jnp.einsum("rtc,cf->rtf", segment, gate_weight, preferred_element_type=jnp.float32)
    up_part = jnp.einsum("rtc,cf->rtf", segment, up_weight, preferred_element_type=jnp.float32)
    gate_sum, up_sum = (
        lax.psum(gate_part.astype(jnp.bfloat16), "grp").astype(jnp.float32),
        lax.psum(up_part.astype(jnp.bfloat16), "grp").astype(jnp.float32),
    )
    hidden = (jax.nn.silu(gate_sum) * up_sum).astype(jnp.bfloat16)
    down_terms = jnp.einsum("rtf,fd->rtd", hidden, down_weight, preferred_element_type=jnp.float32)
    down_sum = lax.psum_scatter(
        down_terms.astype(jnp.bfloat16), "seq", scatter_dimension=2, tiled=True
    ).astype(jnp.float32)
    restore = jnp.argsort(group_perm)
    return jnp.take(residual + down_sum, restore, axis=0).astype(jnp.bfloat16)


N_GRP = 4
N_SEQ = 8
ROWS = 64
GROWS = REQ_GRP * STEPS
FEAT = D // (N_GRP * N_SEQ)
FEAT_PAD = 256
DEPTH = D // N_GRP
GROUP_Q = HEADS // KV_HEADS
QROWS = 32
SHARD_ROWS = SHARD_PAGES * PAGE
MESH = pl.DeviceIdType.MESH


def stat_lanes(pieces, rows, at=0, width=128, base=None):
    lane = lax.broadcasted_iota(jnp.int32, (rows, width), 1)
    block = jnp.zeros((rows, width), jnp.float32) if base is None else base
    for offset, piece in enumerate(pieces):
        block = jnp.where(lane == at + offset, piece, block)
    return block


def split_bf16(value, count):
    pieces = []
    for _ in range(count):
        piece = value.astype(jnp.bfloat16).astype(jnp.float32)
        pieces.append(piece)
        value = value - piece
    return pieces


def pack(values, parts):
    rows, width = ROWS // parts, 128 // parts
    rest = values[:, 128:]
    below = rest[:rows]
    for a in range(1, parts):
        below = below + pltpu.roll(rest[a * rows : (a + 1) * rows], a * width, 1)
    return jnp.concatenate([values[:, :128], below], axis=0).astype(jnp.bfloat16)


def unpack(block, parts):
    rows, width = ROWS // parts, 128 // parts
    below = block[ROWS:]
    lane = lax.broadcasted_iota(jnp.int32, (rows, 128), 1)
    rest = [
        jnp.where(lane < width, pltpu.roll(below, 128 - a * width, 1) if a else below, 0.0)
        for a in range(parts)
    ]
    return jnp.concatenate([block[:ROWS], jnp.concatenate(rest, axis=0)], axis=1)


def fused_kernel(
    lengths,
    group_perm,
    page_table,
    tokens,
    gain_in,
    qkv_bias,
    gain_mid,
    k_hbm,
    v_hbm,
    qkv_hbm,
    o_hbm,
    gate_hbm,
    up_hbm,
    down_hbm,
    out,
    k_pool,
    v_pool,
    w_qkv,
    w_o,
    w_gate,
    w_up,
    w_down,
    x_all,
    x_wide,
    x_bf,
    qkv_send,
    qkv_recv,
    heads_all,
    q_pairs,
    new_k,
    new_v,
    att_held,
    att_send,
    att_recv,
    att_all,
    wide,
    o_send,
    o_recv,
    mid_all,
    ff_send,
    ff_recv,
    hid_all,
    down_send,
    down_recv,
    padded,
    gains,
    load_sem,
    send_sem,
    recv_sem,
):
    g = lax.axis_index("grp")
    s = lax.axis_index("seq")
    f32, bf16 = jnp.float32, jnp.bfloat16

    loads = [
        pltpu.make_async_copy(src, dst, load_sem.at[i])
        for i, (src, dst) in enumerate(
            [
                (qkv_hbm, w_qkv),
                (k_hbm, k_pool),
                (v_hbm, v_pool),
                (o_hbm, w_o),
                (gate_hbm, w_gate),
                (up_hbm, w_up),
                (down_hbm, w_down),
            ]
        )
    ]
    loads[0].start()
    barrier = pltpu.get_barrier_semaphore()
    for d in range(1, N_SEQ):
        pl.semaphore_signal(
            barrier, inc=1, device_id={"seq": lax.rem(s + d, N_SEQ)}, device_id_type=MESH
        )
    for d in range(1, N_GRP):
        pl.semaphore_signal(
            barrier, inc=1, device_id={"grp": lax.rem(g + d, N_GRP)}, device_id_type=MESH
        )

    def exchange(stage, axis, source, target):
        me, count = (s, N_SEQ) if axis == "seq" else (g, N_GRP)
        copies = []
        for d in range(1, count):
            peer = lax.rem(me + d, count)
            copy = pltpu.make_async_remote_copy(
                src_ref=source(peer),
                dst_ref=target,
                send_sem=send_sem.at[stage, d],
                recv_sem=recv_sem.at[stage, d],
                device_id={axis: peer},
                device_id_type=MESH,
            )
            copy.start()
            copies.append(copy)
        return copies

    def arrive(copies):
        for copy in copies:
            copy.wait_recv()

    started = []

    padded[...] = jnp.zeros_like(padded)
    wide[...] = jnp.zeros_like(wide)
    for i in range(ROWS // STEPS):
        padded[i * STEPS : (i + 1) * STEPS, :FEAT] = tokens[group_perm[i]].astype(f32)
    gains[...] = jnp.zeros_like(gains)
    gains[0:1, :FEAT] = gain_in[...]
    gains[1:2, :FEAT] = gain_mid[...]
    sorted_rows = padded[...]

    def feature_block(values, gain):
        squares = jnp.sum(values * values, axis=1, keepdims=True)
        return pack(
            stat_lanes(split_bf16(squares, 2), ROWS, FEAT, FEAT_PAD, values * gain), 2
        )

    x_all[s] = feature_block(sorted_rows, gains[0:1, :])
    pl.semaphore_wait(barrier, N_SEQ + N_GRP - 2)

    def gather_features(stage, blocks):
        copies = exchange(stage, "seq", lambda peer: blocks.at[s], blocks.at[s])
        started.extend(copies)
        if stage == 0:
            loads[1].start()
        arrive(copies)
        lane = lax.broadcasted_iota(jnp.int32, (ROWS, FEAT_PAD), 1)
        x_wide[...] = jnp.zeros_like(x_wide)
        squares = jnp.zeros((ROWS, 1), f32)
        for i in range(N_SEQ):
            block = unpack(blocks[i].astype(f32), 2)
            kept = jnp.where(lane < FEAT, block, 0.0)
            squares = squares + jnp.sum(block - kept, axis=1, keepdims=True)
            first = i * FEAT // 128 * 128
            kept = jnp.concatenate([kept, jnp.zeros((ROWS, 128), f32)], axis=1)
            if i * FEAT - first:
                kept = pltpu.roll(kept, i * FEAT - first, 1)
            x_wide[:, first : first + 384] += kept
        x_bf[...] = x_wide[:, :DEPTH].astype(bf16)
        return squares

    squares_in = gather_features(0, x_all)

    loads[0].wait()
    part = jnp.dot(x_bf[...], w_qkv[...], preferred_element_type=f32).astype(bf16)
    stats = stat_lanes(split_bf16(squares_in, 2), ROWS).astype(bf16)
    for i in range(N_GRP):
        rows = slice(i * GROWS, (i + 1) * GROWS)
        qkv_send[i, :, :896] = part[rows]
        qkv_send[i, :, 896:] = stats[rows]
    copies = exchange(1, "grp", lambda peer: qkv_send.at[peer], qkv_recv.at[g])
    started.extend(copies)
    for load in loads[2:]:
        load.start()
    qkv_recv[g] = qkv_send[g]

    row16 = lax.broadcasted_iota(jnp.int32, (GROWS, HEAD_DIM), 0)
    lane16 = lax.broadcasted_iota(jnp.int32, (GROWS, HEAD_DIM), 1)
    position = row16 % STEPS
    for r in range(REQ_GRP):
        length = lengths[group_perm[g * REQ_GRP + r]]
        position = position + jnp.where(row16 // STEPS == r, length, 0)
    half = HEAD_DIM // 2
    exponent = (lane16 % half).astype(f32) * (2.0 / HEAD_DIM)
    angle = position.astype(f32) * jnp.exp(-exponent * jnp.log(jnp.full((), ROPE_BASE, f32)))
    cosine = jnp.cos(angle)
    sine = jnp.where(lane16 < half, -jnp.sin(angle), jnp.sin(angle))

    arrive(copies)
    summed = sum(qkv_recv[i].astype(f32) for i in range(N_GRP))
    scale = lax.rsqrt(jnp.sum(summed[:, 896:], axis=1, keepdims=True) / D + EPSILON)
    share = summed[:, :896] * scale + qkv_bias[...].reshape(1, 896)
    per_dev = 896 // HEAD_DIM
    for j in range(per_dev):
        unit = share[:, j * HEAD_DIM : (j + 1) * HEAD_DIM]
        turned = unit * cosine + pltpu.roll(unit, half, 1) * sine
        unit = jnp.where(s * per_dev + j < HEADS + KV_HEADS, turned, unit)
        heads_all[s, :, j * HEAD_DIM : (j + 1) * HEAD_DIM] = unit.astype(bf16)
    copies = exchange(2, "seq", lambda peer: heads_all.at[s], heads_all.at[s])
    started.extend(copies)
    q_pairs[...] = jnp.zeros_like(q_pairs)
    n_q = REQ_GRP * QROWS
    spread_row = lax.broadcasted_iota(jnp.int32, (n_q, GROUP_Q * GROWS), 0)
    spread_col = lax.broadcasted_iota(jnp.int32, (n_q, GROUP_Q * GROWS), 1)
    spread = (
        (spread_row // QROWS == spread_col % GROWS // STEPS)
        & (spread_row % QROWS // STEPS == spread_col // GROWS)
        & (spread_row % STEPS == spread_col % STEPS)
    ).astype(f32).astype(bf16)
    pick_row = lax.broadcasted_iota(jnp.int32, (GROUP_Q * GROWS, n_q), 0)
    pick_col = lax.broadcasted_iota(jnp.int32, (GROUP_Q * GROWS, n_q), 1)
    pick = (
        (pick_col // QROWS == pick_row % GROWS // STEPS)
        & (pick_col % QROWS // STEPS == pick_row // GROWS)
        & (pick_col % STEPS == pick_row % STEPS)
    ).astype(f32).astype(bf16)
    row_i = lax.broadcasted_iota(jnp.int32, (ROWS, ROWS), 0)
    col_i = lax.broadcasted_iota(jnp.int32, (ROWS, ROWS), 1)
    origin = jnp.zeros((ROWS, ROWS), jnp.int32)
    for i in range(ROWS // STEPS):
        origin = jnp.where(col_i // STEPS == i, group_perm[i], origin)
    back = (
        ((row_i // STEPS) == origin) & ((col_i % STEPS) == (row_i % STEPS))
    ).astype(f32).astype(bf16)
    arrive(copies)

    def head(h):
        lane = (h % per_dev) * HEAD_DIM
        return heads_all[h // per_dev, :, lane : lane + HEAD_DIM]

    for k in range(KV_HEADS):
        stacked = jnp.concatenate([head(k * GROUP_Q + j) for j in range(GROUP_Q)], axis=0)
        placed = jnp.dot(spread, stacked, preferred_element_type=f32).astype(bf16)
        for r in range(REQ_GRP):
            q_pairs[
                r,
                k // 2,
                (k % 2) * QROWS : (k % 2 + 1) * QROWS,
                (k % 2) * HEAD_DIM : (k % 2 + 1) * HEAD_DIM,
            ] = placed[r * QROWS : (r + 1) * QROWS]
        new_k[:, k * HEAD_DIM : (k + 1) * HEAD_DIM] = head(HEADS + k)
        new_v[:, k * HEAD_DIM : (k + 1) * HEAD_DIM] = head(HEADS + KV_HEADS + k)

    loads[1].wait()
    loads[2].wait()
    score_scale = HEAD_DIM ** (-0.5)
    new_row = lax.broadcasted_iota(jnp.int32, (2 * QROWS, GROWS), 0)
    new_col = lax.broadcasted_iota(jnp.int32, (2 * QROWS, GROWS), 1)
    causal = (new_col % STEPS <= new_row % STEPS) & (s == N_SEQ - 1)
    columns = lax.broadcasted_iota(jnp.int32, (2 * QROWS, SHARD_ROWS), 1)
    contract_last = (((1,), (1,)), ((), ()))

    def attend(r, carry):
        request = group_perm[g * REQ_GRP + r]
        live = columns < lengths[request] - s * SHARD_ROWS
        own = causal & (new_col // STEPS == r)
        slots = [page_table[request, s * SHARD_PAGES + p] for p in range(SHARD_PAGES)]
        for pair in range(KV_HEADS // 2):
            lanes = slice(pair * 256, (pair + 1) * 256)
            query = q_pairs[r, pair]
            keys = jnp.concatenate([k_pool[slot, :, lanes] for slot in slots], axis=0)
            values = jnp.concatenate([v_pool[slot, :, lanes] for slot in slots], axis=0)
            scores = (
                lax.dot_general(query, keys, contract_last, preferred_element_type=f32)
                * score_scale
            )
            scores = jnp.where(live, scores, LOW_SCORE)
            fresh = (
                lax.dot_general(query, new_k[:, lanes], contract_last, preferred_element_type=f32)
                * score_scale
            )
            fresh = jnp.where(own, fresh, LOW_SCORE)
            top = jnp.maximum(
                jnp.max(scores, axis=1, keepdims=True), jnp.max(fresh, axis=1, keepdims=True)
            )
            weights = jnp.where(live, jnp.exp(scores - top), 0.0)
            new_weights = jnp.where(own, jnp.exp(fresh - top), 0.0)
            total = jnp.sum(weights, axis=1, keepdims=True) + jnp.sum(
                new_weights, axis=1, keepdims=True
            )
            weighted = jnp.dot(weights.astype(bf16), values, preferred_element_type=f32) + jnp.dot(
                new_weights.astype(bf16), new_v[:, lanes], preferred_element_type=f32
            )
            block = stat_lanes(split_bf16(top, 3) + split_bf16(total, 2), 2 * QROWS)
            rows = pl.ds(pl.multiple_of(r * QROWS, QROWS), QROWS)
            for k in range(2):
                mine = slice(k * QROWS, (k + 1) * QROWS)
                att_held[2 * pair + k, rows, :HEAD_DIM] = weighted[
                    mine, k * HEAD_DIM : (k + 1) * HEAD_DIM
                ].astype(bf16)
                att_held[2 * pair + k, rows, HEAD_DIM:] = block[mine].astype(bf16)
        return carry

    lax.fori_loop(0, REQ_GRP, attend, 0)
    n_out = GROUP_Q * GROWS
    for k in range(KV_HEADS):
        picked = jnp.dot(pick, att_held[k], preferred_element_type=f32)
        below = picked[:GROWS, HEAD_DIM:]
        for j in range(1, GROUP_Q):
            below = below + pltpu.roll(picked[j * GROWS : (j + 1) * GROWS, HEAD_DIM:], 8 * j, 1)
        att_send[k, :n_out] = picked[:, :HEAD_DIM].astype(bf16)
        att_send[k, n_out:] = below.astype(bf16)
    copies = exchange(3, "seq", lambda peer: att_send.at[peer], att_recv.at[s])
    started.extend(copies)
    att_recv[s] = att_send[s]
    arrive(copies)

    stat_lane = lax.broadcasted_iota(jnp.int32, (GROWS, HEAD_DIM), 1) % 8 == 0
    tops, sums = [], []
    for i in range(N_SEQ):
        block = att_recv[i, n_out:, :].astype(f32)
        shifted = [block] + [pltpu.roll(block, HEAD_DIM - n, 1) for n in range(1, 5)]
        tops.append(jnp.where(stat_lane, shifted[0] + shifted[1] + shifted[2], 0.0))
        sums.append(jnp.where(stat_lane, shifted[3] + shifted[4], 1.0))
    best = functools.reduce(jnp.maximum, tops)
    factors = [jnp.exp(top - best) for top in tops]
    total = sum(factor * part_sum for factor, part_sum in zip(factors, sums))
    for j in range(GROUP_Q):
        rows = slice(j * GROWS, (j + 1) * GROWS)
        weighted = sum(
            factors[i][:, 8 * j : 8 * j + 1] * att_recv[i, rows, :].astype(f32)
            for i in range(N_SEQ)
        )
        attended = weighted / total[:, 8 * j : 8 * j + 1]
        att_all[g, :, j * HEAD_DIM : (j + 1) * HEAD_DIM] = attended.astype(bf16)
    copies = exchange(4, "grp", lambda peer: att_all.at[g], att_all.at[g])
    started.extend(copies)
    loads[3].wait()
    arrive(copies)

    feature = lax.broadcasted_iota(jnp.int32, (ROWS, FEAT_PAD), 1) < FEAT

    def scatter_features(stage, rows, weight, send, recv):
        def copy_of(i, source):
            return pltpu.make_async_remote_copy(
                src_ref=send.at[i],
                dst_ref=recv.at[source],
                send_sem=send_sem.at[stage, i],
                recv_sem=recv_sem.at[stage, source],
                device_id={"seq": i},
                device_id_type=MESH,
            )

        depth = weight.shape[0] // len(rows)

        def tile(c, carry):
            lanes = pl.ds(pl.multiple_of(c * 256, 256), 256)
            wide[:, lanes] = sum(
                jnp.dot(
                    rows[n][...],
                    weight[n * depth : (n + 1) * depth, lanes],
                    preferred_element_type=f32,
                )
                for n in range(len(rows))
            )
            return carry

        lax.fori_loop(0, DEPTH // 256, tile, 0)
        for i in (0, 7, 1, 6, 2, 5, 3, 4):
            first = i * FEAT // 128 * 128
            window = wide[:, first : first + 384]
            if i * FEAT - first:
                window = pltpu.roll(window, 384 - (i * FEAT - first), 1)
            send[i] = pack(jnp.where(feature, window[:, :FEAT_PAD], 0.0), 4)

            @pl.when(s != i)
            def _(i=i):
                copy_of(i, s).start()

        recv[s] = send[s]
        for i in range(N_SEQ):

            @pl.when(s != i)
            def _(i=i):
                copy_of(i, i).wait_recv()
                copy_of(i, i).wait_send()

        return unpack(sum(recv[i].astype(f32) for i in range(N_SEQ)), 4)

    columns_in = jnp.concatenate([att_all[i] for i in range(N_GRP)], axis=0)
    attn_sum = scatter_features(5, [columns_in], w_o, o_send, o_recv)
    residual = sorted_rows + attn_sum
    mid_all[s] = feature_block(residual, gains[1:2, :])
    squares_mid = gather_features(6, mid_all)

    stats = stat_lanes(split_bf16(squares_mid, 2), ROWS)
    stats = jnp.concatenate([stats, stats], axis=0).T[:16].astype(bf16)
    wide_x = x_wide[:, :DEPTH]
    gate_x = jnp.concatenate([wide_x, jnp.zeros_like(wide_x)], axis=0).T
    up_x = pltpu.roll(gate_x, ROWS, 1).astype(bf16)
    gate_x = gate_x.astype(bf16)
    units = w_gate.shape[0] // N_GRP
    loads[4].wait()
    loads[5].wait()

    def ff_copy(d):
        return pltpu.make_async_remote_copy(
            src_ref=ff_send.at[lax.rem(g + d, N_GRP)],
            dst_ref=ff_recv.at[g],
            send_sem=send_sem.at[7, d],
            recv_sem=recv_sem.at[7, d],
            device_id={"grp": lax.rem(g + d, N_GRP)},
            device_id_type=MESH,
        )

    def ff_units(d, carry):
        peer = lax.rem(g + d, N_GRP)
        rows = pl.ds(pl.multiple_of(peer * units, 16), units)
        part = jnp.dot(w_gate[rows, :], gate_x, preferred_element_type=f32) + jnp.dot(
            w_up[rows, :], up_x, preferred_element_type=f32
        )
        ff_send[peer, :units] = part.astype(bf16)
        ff_send[peer, units:] = stats

        @pl.when(d < N_GRP)
        def _():
            ff_copy(d).start()

        return carry

    lax.fori_loop(1, N_GRP + 1, ff_units, 0)
    copies = [ff_copy(d) for d in range(1, N_GRP)]
    started.extend(copies)
    ff_recv[g] = ff_send[g]
    arrive(copies)
    summed = sum(ff_recv[i].astype(f32) for i in range(N_GRP))
    scale = lax.rsqrt((summed[units : units + 1] + summed[units + 1 : units + 2]) / D + EPSILON)
    summed = summed[:units] * scale
    hidden = summed / (1.0 + jnp.exp(-summed)) * pltpu.roll(summed, ROWS, 1)
    hidden = jnp.concatenate([hidden, jnp.zeros((512 - units, 128), f32)], axis=0)
    hid_all[g] = hidden.T[:ROWS].astype(bf16)
    copies = exchange(8, "grp", lambda peer: hid_all.at[g], hid_all.at[g])
    started.extend(copies)
    loads[6].wait()
    arrive(copies)
    hidden = [hid_all[i, :, :units] for i in range(N_GRP)]
    down_sum = scatter_features(9, hidden, w_down, down_send, down_recv)
    final = (residual + down_sum).astype(bf16)
    ordered = jnp.dot(back, final, preferred_element_type=f32)
    for i in range(ROWS // STEPS):
        out[i] = ordered[i * STEPS : (i + 1) * STEPS, :FEAT].astype(bf16)
    for copy in started:
        copy.wait_send()


def fused_body(
    tokens,
    lengths,
    group_perm,
    page_table,
    k_pool,
    v_pool,
    gain_in,
    qkv_weight,
    qkv_bias,
    o_weight,
    gain_mid,
    gate_weight,
    up_weight,
    down_weight,
):
    gains = [gain.reshape(1, FEAT) for gain in (gain_in, gain_mid)]
    gate_rows, up_rows = gate_weight.T, up_weight.T
    smem = pl.BlockSpec(memory_space=pltpu.SMEM)
    vmem = pl.BlockSpec(memory_space=pltpu.VMEM)
    hbm = pl.BlockSpec(memory_space=pl.ANY)
    bf16, f32 = jnp.bfloat16, jnp.float32
    return pl.pallas_call(
        fused_kernel,
        out_shape=jax.ShapeDtypeStruct(tokens.shape, bf16),
        in_specs=[smem] * 3 + [vmem] * 4 + [hbm] * 7,
        out_specs=vmem,
        scratch_shapes=[
            pltpu.VMEM(k_pool.shape, bf16),
            pltpu.VMEM(v_pool.shape, bf16),
            pltpu.VMEM(qkv_weight.shape, bf16),
            pltpu.VMEM(o_weight.shape, bf16),
            pltpu.VMEM(gate_rows.shape, bf16),
            pltpu.VMEM(up_rows.shape, bf16),
            pltpu.VMEM(down_weight.shape, bf16),
            pltpu.VMEM((N_SEQ, 96, 128), bf16),
            pltpu.VMEM((ROWS, DEPTH + 128), f32),
            pltpu.VMEM((ROWS, DEPTH), bf16),
            pltpu.VMEM((N_GRP, GROWS, 1024), bf16),
            pltpu.VMEM((N_GRP, GROWS, 1024), bf16),
            pltpu.VMEM((N_SEQ, GROWS, 896), bf16),
            pltpu.VMEM((REQ_GRP, KV_HEADS // 2, 2 * QROWS, 256), bf16),
            pltpu.VMEM((GROWS, KV_HEADS * HEAD_DIM), bf16),
            pltpu.VMEM((GROWS, KV_HEADS * HEAD_DIM), bf16),
            pltpu.VMEM((N_SEQ, REQ_GRP * QROWS, 2 * HEAD_DIM), bf16),
            pltpu.VMEM((N_SEQ, 96, 128), bf16),
            pltpu.VMEM((N_SEQ, 96, 128), bf16),
            pltpu.VMEM((N_GRP, GROWS, GROUP_Q * HEAD_DIM), bf16),
            pltpu.VMEM((ROWS, DEPTH + 128), f32),
            pltpu.VMEM((N_SEQ, 80, 128), bf16),
            pltpu.VMEM((N_SEQ, 80, 128), bf16),
            pltpu.VMEM((N_SEQ, 96, 128), bf16),
            pltpu.VMEM((N_GRP, gate_rows.shape[0] // N_GRP + 16, 128), bf16),
            pltpu.VMEM((N_GRP, gate_rows.shape[0] // N_GRP + 16, 128), bf16),
            pltpu.VMEM((N_GRP, ROWS, 512), bf16),
            pltpu.VMEM((N_SEQ, 80, 128), bf16),
            pltpu.VMEM((N_SEQ, 80, 128), bf16),
            pltpu.VMEM((ROWS, FEAT_PAD), f32),
            pltpu.VMEM((8, FEAT_PAD), f32),
            pltpu.SemaphoreType.DMA((7,)),
            pltpu.SemaphoreType.DMA((11, N_SEQ)),
            pltpu.SemaphoreType.DMA((11, N_SEQ)),
        ],
        compiler_params=pltpu.CompilerParams(
            collective_id=0, has_side_effects=True, vmem_limit_bytes=56 * 2**20
        ),
    )(
        lengths,
        group_perm,
        page_table,
        tokens,
        gains[0],
        qkv_bias,
        gains[1],
        k_pool,
        v_pool,
        qkv_weight,
        o_weight,
        gate_rows,
        up_rows,
        down_weight,
    )


def solution(mesh):
    fused = mesh.shape["seq"] == KV_HEADS and mesh.shape["grp"] == N_GRP
    return jax.shard_map(
        fused_body if fused else body,
        mesh=mesh,
        in_specs=(
            P(None, None, ("grp", "seq")),
            P(),
            P(),
            P(),
            P(("grp", "seq"), None, None),
            P(("grp", "seq"), None, None),
            P(("grp", "seq")),
            P("grp", "seq"),
            P("seq"),
            P("seq", "grp"),
            P(("grp", "seq")),
            P("grp", "seq"),
            P("grp", "seq"),
            P("seq", "grp"),
        ),
        out_specs=P(None, None, ("grp", "seq")),
        check_vma=False,
    )
```
